32 devices in a mesh: stn: 16 (over z, x, core), blk: 2 (over y).
Axes of the slice: x: 2, y: 2, z: 4, core: 2. Of those that a mesh axis runs over, the one named last changes fastest.
Arguments:
- voltages: bfloat16 [1024, 2, 63, 2, 4096], P('stn', 'blk'), may hold values from -6 to 6
- station_map: int32 [512], replicated, may hold values from 0 to 511, each once
- chan_counts: int32 [16], replicated, may hold values from 1 to 3, 32 in all
Outputs:
- visibilities: bfloat16 [16, 3, 2, 1024, 1024], P('stn', None, None, 'blk')
The draws below stay inside these ranges and needn't reach their ends.
Inputs may be any that keep to these rules, and one draw needn't show every extreme that they name: A permutation: stream rows 2 q and 2 q + 1 of voltages are the two polarizations of station station_map[q]. `chan_counts`: the counts sum to 32; the largest is 3; device d of stn correlates the consecutive channels that start at the sum of the counts before it.
All inputs are finite; a program needn't handle non-finite values.
Results may differ from the reference program's by a relative error of at most 0.0056.
Values may be sent and summed in bfloat16 or wider, within the bound.
No kernel may reach another device: no remote copies, remote signals or barrier semaphores. Data moves between devices by JAX's collectives and lax.ppermute only.
A program may use at most 384 MiB of HBM per device.

```python
import math
import jax
import jax.numpy as jnp
import numpy as np
from jax import lax

STATIONS = 512
FFT_LEN = 4096
TAPS = 16
CAP = 3
NSPEC = 48
FRAMES = 63
BAND = 32
N_STN = 16
N_BLK = 2


def level_of(stream_key, dims, pieces, smallest, high):
    gain, own = 1.0, jax.random.fold_in(stream_key, 6)
    for dim, blocks in pieces:
        draws = jnp.exp(jax.random.uniform(jax.random.fold_in(own, dim), (blocks,), jnp.float32, smallest / len(pieces), high / len(pieces)))
        gain = gain * jnp.repeat(draws, dims[dim] // blocks).reshape([-1 if axis == dim else 1 for axis in range(len(dims))])
    return gain


def split_up(amount, total, reach, skew):
    weights = [(1 << 20) // math.isqrt(rank ** skew) + 1 for rank in range(2, amount + 1)]
    spare, holding = total - reach - (amount - 1), [1] * (amount - 1)
    while spare > 0:
        movable = [i for i in range(amount - 1) if holding[i] < reach]
        whole, left = sum([weights[i] for i in movable]), spare
        for i in movable:
            addition = min(reach - holding[i], max(1, left * weights[i] // whole), spare)
            holding[i] = holding[i] + addition
            spare = spare - addition
    return np.array([reach] + holding)


def uneven(stream_key, count, total, reach, lean):
    if count == 2:
        one = jax.random.randint(stream_key, (), max(1, total - reach), min(reach, total - 1) + 1)
        return jnp.stack([one, total - one])
    sizes = jnp.asarray(split_up(count, total, reach, lean), jnp.int32)
    pairs = (count - 1) // 2
    source_of, sink = sizes[1:1 + 2 * pairs:2], sizes[2:2 + 2 * pairs:2]
    room = jnp.minimum(source_of - 1, reach - sink)
    passed = jax.random.randint(jax.random.fold_in(stream_key, 1), (pairs,), 0, 1 << 20) % (room + 1)
    sizes = sizes.at[1:1 + 2 * pairs:2].set(source_of - passed).at[2:2 + 2 * pairs:2].set(sink + passed)
    return sizes[jax.random.permutation(jax.random.fold_in(stream_key, 2), count)]


def centred(own_key, extent, scale, limit, shards=(), kind=jnp.bfloat16):
    loudness = level_of(own_key, extent, shards, -0.22, 0.18) if shards else 1.0
    drawn = jax.random.normal(own_key, extent, jnp.float32) * scale * loudness
    return jnp.minimum(jnp.maximum(drawn, -limit), limit).astype(kind)


def setup_inputs(seed: int = 0) -> dict:
    splits = jax.random.split(jax.random.key(seed), 4)
    voltages = centred(splits[0], (2 * STATIONS, N_BLK, FRAMES, 2, FFT_LEN), 1.0, 6.0, ((0, 16), (1, 2)))
    station_map = jax.random.permutation(splits[1], STATIONS).astype(jnp.int32)
    chan_counts = uneven(splits[2], N_STN, BAND, CAP, 0).astype(jnp.int32)
    return dict(voltages=voltages, station_map=station_map, chan_counts=chan_counts)


def prototype(tap_count, frame_len):
    span_len = tap_count * frame_len
    points = jnp.arange(span_len, dtype=jnp.float32) + 0.5
    window = 0.5 - 0.5 * jnp.cos(2.0 * math.pi * points / span_len)
    shifted = math.pi * (points - span_len / 2.0) / frame_len
    filt_vals = jnp.sin(shifted) / shifted * window
    filt_vals = filt_vals / jnp.sqrt(jnp.sum(filt_vals * filt_vals))
    return filt_vals.reshape(tap_count, frame_len)

def reference(voltages, station_map, chan_counts):
    row_count = 2 * STATIONS
    band_len = BAND
    taper_table = prototype(TAPS, FFT_LEN)
    block_rows = math.gcd(row_count, 64)

    def channelize(volt_block):
        folded = jnp.zeros((block_rows, N_BLK, NSPEC, 2, FFT_LEN), jnp.float32)
        for tap_idx in range(TAPS):
            folded = folded + volt_block[:, :, tap_idx:tap_idx + NSPEC].astype(jnp.float32) * taper_table[tap_idx]
        signal = lax.complex(folded[:, :, :, 0], folded[:, :, :, 1])
        spectrum = jnp.fft.fft(signal, axis=-1)[..., :band_len]
        return jnp.stack([jnp.real(spectrum), jnp.imag(spectrum)], axis=3).astype(jnp.bfloat16)
    shaped = voltages.reshape(row_count // block_rows, block_rows, N_BLK, FRAMES, 2, FFT_LEN)
    spectra = lax.map(channelize, shaped)
    spectra = spectra.reshape(row_count, N_BLK * NSPEC, 2, band_len)
    inverse = jnp.zeros((STATIONS,), jnp.int32).at[station_map].set(jnp.arange(STATIONS, dtype=jnp.int32))
    true_rows = (2 * inverse[:, None] + jnp.arange(2, dtype=jnp.int32)[None, :]).reshape(-1)
    spectra = spectra[true_rows]
    offsets = jnp.cumsum(chan_counts) - chan_counts
    samples = N_BLK * NSPEC

    def correlate(slot_idx):
        device = slot_idx // CAP
        within = slot_idx % CAP
        live_count = chan_counts[device]
        channel = offsets[device] + jnp.minimum(within, live_count - 1)
        picked = lax.dynamic_index_in_dim(spectra, channel, axis=3, keepdims=False)
        real_part = picked[:, :, 0]
        imag_part = picked[:, :, 1]
        joined = jnp.concatenate([real_part, imag_part], axis=1)
        turned = jnp.concatenate([imag_part, -real_part], axis=1)
        vis_real = jnp.dot(joined, joined.T, preferred_element_type=jnp.float32)
        vis_imag = jnp.dot(turned, joined.T, preferred_element_type=jnp.float32)
        valid_mask = (within < live_count).astype(jnp.float32)
        return (jnp.stack([vis_real, vis_imag]) * (valid_mask / samples)).astype(jnp.bfloat16)
    slot_ids = jnp.arange(N_STN * CAP, dtype=jnp.int32)
    result = lax.map(correlate, slot_ids)
    return result.reshape(N_STN, CAP, 2, row_count, row_count)
```

```python
import functools
import math

import jax
import jax.numpy as jnp
import ml_dtypes
import numpy as np
from jax import lax
from jax.experimental import pallas as pl
from jax.experimental.pallas import tpu as pltpu
from jax.sharding import PartitionSpec as P

FFT_LEN = 4096
TAPS = 16
CAP = 3
NSPEC = 48
LANES = 128


def prototype():
    span = TAPS * FFT_LEN
    points = np.arange(span, dtype=np.float64) + 0.5
    window = 0.5 - 0.5 * np.cos(2.0 * math.pi * points / span)
    shifted = math.pi * (points - span / 2.0) / FFT_LEN
    filt = np.sin(shifted) / shifted * window
    return (filt / np.sqrt(np.sum(filt * filt))).reshape(TAPS, FFT_LEN)


def frame_basis(band, count):
    limit = math.pi * (band + 0.1)
    terms = count + int(limit) + 60
    k = np.arange(terms, dtype=np.float64)
    diagonal = k * (k + 1) + (2 * k * (k + 1) - 1) / ((2 * k + 3) * (2 * k - 1)) * limit**2
    m = k[:-2]
    beside = (m + 2) * (m + 1) / ((2 * m + 3) * np.sqrt((2 * m + 1) * (2 * m + 5))) * limit**2
    matrix = np.diag(diagonal) + np.diag(beside, 2) + np.diag(beside, -2)
    _, vectors = np.linalg.eigh(matrix)
    x = (2 * np.arange(FFT_LEN) + 1.0) / FFT_LEN - 1
    legendre = np.zeros((terms, FFT_LEN))
    legendre[0] = 1.0
    legendre[1] = x
    for j in range(2, terms):
        legendre[j] = ((2 * j - 1) * x * legendre[j - 1] - (j - 1) * legendre[j - 2]) / j
    legendre *= np.sqrt((k + 0.5) * 2.0 / FFT_LEN)[:, None]
    return legendre.T @ vectors[:, :count]


@functools.lru_cache(maxsize=4)
def tables(band):
    bf16 = ml_dtypes.bfloat16
    count = -(-(2 * band + 32) // LANES) * LANES
    basis = frame_basis(band, count)
    high = basis.astype(bf16)
    low = (basis - high.astype(np.float64)).astype(bf16)
    held = high.astype(np.float64) + low.astype(np.float64)
    phase = 2.0 * math.pi / FFT_LEN * (np.outer(np.arange(FFT_LEN), np.arange(band)) % FFT_LEN)
    wave = np.concatenate([np.cos(phase), -np.sin(phase)], axis=1)
    gram = held.T @ held
    mixing = [np.linalg.solve(gram, held.T @ (row[:, None] * wave)) for row in prototype()]
    per = max(1, LANES // (2 * band))
    groups = TAPS // per
    order = [b + groups * u for b in range(groups) for u in range(per)]
    mixing = np.concatenate([mixing[t] for t in order], axis=1).astype(bf16)
    return np.concatenate([high, low], axis=1), np.concatenate([mixing, mixing], axis=0)


def channelizer(band, dests, streams, step, counts, v_ref, u_ref, w_ref, out_ref, z, p, x, turned):
    i = pl.program_id(0)
    half = u_ref.shape[1] // 2
    frames = v_ref.shape[2]
    rows = 2 * frames
    per = max(1, LANES // (2 * band))
    groups = TAPS // per
    width = per * 2 * band
    need = 2 * NSPEC + 2 * groups * (per - 1)

    signal = v_ref[...].reshape(step * rows, FFT_LEN)
    coeff = jnp.dot(signal, u_ref[...], preferred_element_type=jnp.float32)
    coeff = coeff[:, :half] + coeff[:, half:]
    high = coeff.astype(jnp.bfloat16)
    low = (coeff - high.astype(jnp.float32)).astype(jnp.bfloat16)
    z[...] = jnp.dot(
        jnp.concatenate([high, low], axis=1), w_ref[...], preferred_element_type=jnp.float32
    )
    for r in range(step):
        total = None
        for b in range(groups):
            term = z[pl.ds(r * rows + 2 * b, need), b * width : (b + 1) * width]
            total = term if total is None else total + term
        if per > 1:
            whole = total[: 2 * NSPEC]
            for u in range(1, per):
                shifted = total[2 * groups * u : 2 * groups * u + 2 * NSPEC]
                whole = whole + jnp.roll(shifted, -2 * band * u, axis=1)
            total = whole
        blocks = range(width // LANES)
        for n in blocks:
            p[n] = total[:, n * LANES : (n + 1) * LANES]
        even = jnp.concatenate([p[n, pl.ds(0, NSPEC, stride=2), :] for n in blocks], axis=1)
        odd = jnp.concatenate([p[n, pl.ds(1, NSPEC, stride=2), :] for n in blocks], axis=1)
        swapped = [-odd[:, band : 2 * band], odd[:, :band]]
        if width > 2 * band:
            swapped.append(jnp.zeros((NSPEC, width - 2 * band), jnp.float32))
        spectrum = even + jnp.concatenate(swapped, axis=1)
        for n in blocks:
            x[n, pl.ds(i * step + r, NSPEC, stride=streams), :] = spectrum[
                :, n * LANES : (n + 1) * LANES
            ]

    @pl.when(i == pl.num_programs(0) - 1)
    def _():
        lane = lax.broadcasted_iota(jnp.int32, (8, width), 1)
        row = lax.broadcasted_iota(jnp.int32, (8, width), 0)
        slot = row // 2
        base = (row % 2) * band
        picks = []
        offset = jnp.int32(0)
        for d in range(dests):
            count = counts[d]
            want = offset + jnp.minimum(slot, count - 1) + base
            picks.append(jnp.where((lane == want) & (row < 2 * CAP), 1.0, 0.0))
            offset = offset + count
        pick = jnp.concatenate(picks, axis=0).astype(jnp.bfloat16)
        spectra = jnp.concatenate([x[n] for n in range(width // LANES)], axis=1)
        out = lax.dot_general(
            pick, spectra.astype(jnp.bfloat16), (((1,), (1,)), ((), ())),
            preferred_element_type=jnp.float32,
        )
        tiles = NSPEC * streams // LANES
        for d in range(dests):
            for t in range(tiles):
                turned[d, pl.ds(t, 2 * CAP, stride=tiles), :] = out[
                    8 * d : 8 * d + 2 * CAP, t * LANES : (t + 1) * LANES
                ]
        out_ref[...] = turned[...].astype(jnp.bfloat16)


def channelize(voltages, chan_counts, dests):
    band = 2 * dests
    streams, frames = voltages.shape[0], voltages.shape[2]
    step = 4 if band <= 64 else 2
    analysis, mixing = tables(band)
    width = max(LANES, 2 * band)
    payload = 2 * CAP * NSPEC * streams // LANES
    rows = step * 2 * frames
    kernel = functools.partial(channelizer, band, dests, streams, step)
    return pl.pallas_call(
        kernel,
        grid_spec=pltpu.PrefetchScalarGridSpec(
            num_scalar_prefetch=1,
            grid=(streams // step,),
            in_specs=[
                pl.BlockSpec((step, 1, frames, 2, FFT_LEN), lambda i, c: (i, 0, 0, 0, 0)),
                pl.BlockSpec(analysis.shape, lambda i, c: (0, 0), pipeline_mode=pl.Buffered(1)),
                pl.BlockSpec(mixing.shape, lambda i, c: (0, 0), pipeline_mode=pl.Buffered(1)),
            ],
            out_specs=pl.BlockSpec((dests, payload, LANES), lambda i, c: (0, 0, 0)),
            scratch_shapes=[
                pltpu.VMEM((rows, mixing.shape[1]), jnp.float32),
                pltpu.VMEM((width // LANES, 2 * NSPEC, LANES), jnp.float32),
                pltpu.VMEM((width // LANES, NSPEC * streams, LANES), jnp.float32),
                pltpu.VMEM((dests, payload, LANES), jnp.float32),
            ],
        ),
        out_shape=jax.ShapeDtypeStruct((dests, payload, LANES), jnp.bfloat16),
        compiler_params=pltpu.CompilerParams(vmem_limit_bytes=60 * 1024 * 1024),
        cost_estimate=pl.CostEstimate(
            flops=2 * streams * 2 * frames * FFT_LEN * analysis.shape[1],
            bytes_accessed=2 * voltages.size, transcendentals=0,
        ),
    )(chan_counts, voltages, jnp.asarray(analysis), jnp.asarray(mixing))


def correlator(direct, counts, where, dest_ref, *refs):
    out_ref, pre, post = refs[-3:]
    k = pl.program_id(0)
    time_len = pre.shape[1]
    total = pre.shape[2]

    @pl.when(k == 0)
    def _():
        if direct:
            own, other = refs[:2]
            sources, payload = own.shape[0], own.shape[1]
            tiles = payload // (2 * CAP)
            lane = lax.broadcasted_iota(jnp.int32, (payload, LANES), 1)
            left = lane < LANES // 2
            for h, ref in enumerate((own, other)):
                for q in range(sources // 2):
                    a = ref[2 * q].astype(jnp.float32)
                    b = ref[2 * q + 1].astype(jnp.float32)
                    first = jnp.where(left, a, jnp.roll(b, LANES // 2, axis=1))
                    second = jnp.where(left, jnp.roll(a, LANES // 2, axis=1), b)
                    for part in range(2 * CAP):
                        rows = slice(part * tiles, (part + 1) * tiles)
                        both = jnp.concatenate([first[rows], second[rows]], axis=0)
                        pre[part, h * NSPEC : (h + 1) * NSPEC, q * LANES : (q + 1) * LANES] = (
                            both.astype(jnp.bfloat16)
                        )
        else:
            pre[...] = refs[0][...]
        spot = lax.broadcasted_iota(jnp.int32, (total, total), 0)
        turn = jnp.where(spot == dest_ref[...], 1.0, 0.0).astype(jnp.bfloat16)
        ordered = lax.dot_general(
            pre[...].reshape(2 * CAP * time_len, total), turn, (((1,), (1,)), ((), ())),
            preferred_element_type=jnp.float32,
        )
        post[...] = ordered.astype(jnp.bfloat16).reshape(CAP, 2 * time_len, total)

    rows = out_ref.shape[3]
    every = post[k]
    near = post[k, :, pl.ds(pl.multiple_of(where[1] * rows, LANES), rows)]
    turned = jnp.concatenate([near[time_len:], -near[:time_len]], axis=0)
    valid = jnp.where(k < counts[where[0]], 1.0, 0.0) / jnp.float32(time_len)
    for part, left in enumerate((near, turned)):
        vis = lax.dot_general(
            left, every, (((0,), (0,)), ((), ())), preferred_element_type=jnp.float32
        )
        out_ref[0, 0, part] = (vis * valid).astype(jnp.bfloat16)


def correlate(own, other, dest, chan_counts, where, streams):
    sources = own.shape[0]
    total = sources * streams
    spread = LANES // streams
    direct = spread == 2
    if direct:
        operands = (own, other)
        specs = [pl.BlockSpec(own.shape, lambda k, c, w: (0, 0, 0))] * 2
    else:
        tiles = NSPEC // spread
        both = jnp.stack([own, other], axis=0).reshape(2, sources, 2 * CAP, tiles, spread, streams)
        both = both.transpose(2, 0, 3, 4, 1, 5).reshape(2 * CAP, 2 * NSPEC, total)
        operands = (both,)
        specs = [pl.BlockSpec(both.shape, lambda k, c, w: (0, 0, 0))]
    rows = total // 2
    return pl.pallas_call(
        functools.partial(correlator, direct),
        grid_spec=pltpu.PrefetchScalarGridSpec(
            num_scalar_prefetch=2,
            grid=(CAP,),
            in_specs=[pl.BlockSpec((1, total), lambda k, c, w: (0, 0))] + specs,
            out_specs=pl.BlockSpec((1, 1, 2, rows, total), lambda k, c, w: (0, k, 0, 0, 0)),
            scratch_shapes=[
                pltpu.VMEM((2 * CAP, 2 * NSPEC, total), jnp.bfloat16),
                pltpu.VMEM((CAP, 4 * NSPEC, total), jnp.bfloat16),
            ],
        ),
        out_shape=jax.ShapeDtypeStruct((1, CAP, 2, rows, total), jnp.bfloat16),
        compiler_params=pltpu.CompilerParams(vmem_limit_bytes=60 * 1024 * 1024),
    )(chan_counts, where, dest, *operands)


def body(voltages, station_map, chan_counts):
    dests = lax.axis_size("stn")
    streams = voltages.shape[0]
    outgoing = channelize(voltages, chan_counts, dests)
    own = lax.all_to_all(outgoing, "stn", split_axis=0, concat_axis=0, tiled=True)
    other = lax.ppermute(own, "blk", [(0, 1), (1, 0)])
    dest = (2 * station_map[:, None] + jnp.arange(2, dtype=jnp.int32)[None, :]).reshape(1, -1)
    where = jnp.stack([lax.axis_index("stn"), lax.axis_index("blk")]).astype(jnp.int32)
    return correlate(own, other, dest, chan_counts, where, streams)


def solution(mesh):
    return jax.shard_map(
        body,
        mesh=mesh,
        in_specs=(P("stn", "blk", None, None, None), P(), P()),
        out_specs=P("stn", None, None, "blk", None),
        check_vma=False,
    )
```

```python
import functools
import math

import jax
import jax.numpy as jnp
import ml_dtypes
import numpy as np
from jax import lax
from jax.experimental import pallas as pl
from jax.experimental.pallas import tpu as pltpu
from jax.sharding import PartitionSpec as P

FFT_LEN = 4096
TAPS = 16
CAP = 3
NSPEC = 48
LANES = 128


def prototype():
    span = TAPS * FFT_LEN
    points = np.arange(span, dtype=np.float64) + 0.5
    window = 0.5 - 0.5 * np.cos(2.0 * math.pi * points / span)
    shifted = math.pi * (points - span / 2.0) / FFT_LEN
    filt = np.sin(shifted) / shifted * window
    return (filt / np.sqrt(np.sum(filt * filt))).reshape(TAPS, FFT_LEN)


def frame_basis(band, count):
    limit = math.pi * (band + 0.1)
    terms = count + int(limit) + 60
    k = np.arange(terms, dtype=np.float64)
    diagonal = k * (k + 1) + (2 * k * (k + 1) - 1) / ((2 * k + 3) * (2 * k - 1)) * limit**2
    m = k[:-2]
    beside = (m + 2) * (m + 1) / ((2 * m + 3) * np.sqrt((2 * m + 1) * (2 * m + 5))) * limit**2
    matrix = np.diag(diagonal) + np.diag(beside, 2) + np.diag(beside, -2)
    _, vectors = np.linalg.eigh(matrix)
    x = (2 * np.arange(FFT_LEN) + 1.0) / FFT_LEN - 1
    legendre = np.zeros((terms, FFT_LEN))
    legendre[0] = 1.0
    legendre[1] = x
    for j in range(2, terms):
        legendre[j] = ((2 * j - 1) * x * legendre[j - 1] - (j - 1) * legendre[j - 2]) / j
    legendre *= np.sqrt((k + 0.5) * 2.0 / FFT_LEN)[:, None]
    return legendre.T @ vectors[:, :count]


SHIFTS = 4


def turn_lanes(value, shift):
    shift = shift % LANES
    return pltpu.roll(value, shift, axis=1) if shift else value


def packing(band):
    if 3 * (2 * band + 21) <= 2 * LANES:
        return 2 * band + 21, 2 * LANES, True
    count = -(-(2 * band + 32) // (LANES // 2)) * (LANES // 2)
    return count, -(-2 * count // LANES) * LANES, False


@functools.lru_cache(maxsize=4)
def tables(band):
    bf16 = ml_dtypes.bfloat16
    count, packed, triple = packing(band)
    basis = frame_basis(band, count)
    high = basis.astype(bf16)
    low = (basis - high.astype(np.float64)).astype(bf16)
    held = high.astype(np.float64) + low.astype(np.float64)
    lanes = -(-count // LANES) * LANES
    analysis = np.zeros((FFT_LEN, 2 * lanes), bf16)
    analysis[:, :count] = high
    analysis[:, lanes : lanes + count] = low

    phase = 2.0 * math.pi / FFT_LEN * (np.outer(np.arange(FFT_LEN), np.arange(band)) % FFT_LEN)
    wave = np.concatenate([np.cos(phase), -np.sin(phase)], axis=1)
    gram = held.T @ held
    taper = prototype()
    mixing = np.zeros((TAPS // SHIFTS, 2, packed, SHIFTS, 2 * band), bf16)
    for t in range(TAPS):
        real = np.linalg.solve(gram, held.T @ (taper[t][:, None] * wave))
        imag = np.concatenate([-real[:, band:], real[:, :band]], axis=1)
        for c, full in enumerate((real, imag)):
            part = mixing[t // SHIFTS, c, :, t % SHIFTS]
            top = full.astype(bf16)
            part[:count] = top
            part[count : 2 * count] = top
            if triple:
                part[2 * count : 3 * count] = (full - top.astype(np.float64)).astype(bf16)
    return analysis, mixing.reshape(-1, SHIFTS * 2 * band)


def channelizer(band, dests, streams, step, counts, v_ref, u_ref, w_ref, out_ref, y, p, x, turned):
    i = pl.program_id(0)
    last = pl.num_programs(0) - 1
    count, packed, triple = packing(band)
    lanes = u_ref.shape[1] // 2
    rows = 2 * v_ref.shape[2]
    reach = NSPEC + 8
    wide = max(1, 2 * band // LANES)

    def analyse():
        signal = v_ref[...].reshape(step * rows, FFT_LEN)
        coeff = jnp.dot(signal, u_ref[...], preferred_element_type=jnp.float32)
        coeff = coeff[:, :lanes] + coeff[:, lanes:]
        high = coeff.astype(jnp.bfloat16).astype(jnp.float32)
        low = coeff - high
        if triple:
            lane = lax.broadcasted_iota(jnp.int32, coeff.shape, 1)
            low = turn_lanes(low, count)
            spare = 2 * count - LANES
            y[0, : step * rows] = jnp.where(lane < count, high, low)
            y[1, : step * rows] = jnp.where(lane < spare, low, turn_lanes(high, spare))
        else:
            both = jnp.concatenate([high[:, :count], low[:, :count]], axis=1)
            for n in range(packed // LANES):
                y[n, : step * rows] = both[:, n * LANES : (n + 1) * LANES]

    def mix(block):
        taps = []
        for r in range(step):
            taps.append(jnp.concatenate([
                y[n, pl.ds(r * rows + 2 * SHIFTS * m + c, reach, stride=2), :]
                for m in range(TAPS // SHIFTS) for c in range(2) for n in range(packed // LANES)
            ], axis=1))
        taps = jnp.concatenate(taps, axis=0).astype(jnp.bfloat16)
        mixed = jnp.dot(taps, w_ref[...], preferred_element_type=jnp.float32)
        for n in range(mixed.shape[1] // LANES):
            p[n] = mixed[:, n * LANES : (n + 1) * LANES]
        for r in range(step):
            place = pl.ds(block * step + r, NSPEC, stride=streams)
            if 2 * band >= LANES:
                for n in range(wide):
                    x[n, place, :] = sum(
                        p[wide * h + n, pl.ds(r * reach + h, NSPEC), :] for h in range(SHIFTS)
                    )
            else:
                per = LANES // (2 * band)
                lane = lax.broadcasted_iota(jnp.int32, (NSPEC, LANES), 1)
                total = None
                for u in reversed(range(per)):
                    part = sum(
                        p[b, pl.ds(r * reach + b * per + u, NSPEC), :] for b in range(SHIFTS // per)
                    )
                    total = part if total is None else jnp.where(
                        lane < 2 * band * (u + 1), part, total
                    )
                whole = total
                for u in range(1, per):
                    whole = whole + turn_lanes(total, -2 * band * u)
                x[0, place, :] = whole

    @pl.when(i < last)
    def _():
        mix(jnp.maximum(i - 1, 0))
        analyse()

    @pl.when(i == last)
    def _():
        mix(i - 1)
        lane = lax.broadcasted_iota(jnp.int32, (8, wide * LANES), 1)
        row = lax.broadcasted_iota(jnp.int32, (8, wide * LANES), 0)
        slot = row // 2
        base = (row % 2) * band
        picks = []
        offset = jnp.int32(0)
        for d in range(dests):
            held = counts[d]
            want = offset + jnp.minimum(slot, held - 1) + base
            picks.append(jnp.where((lane == want) & (row < 2 * CAP), 1.0, 0.0))
            offset = offset + held
        pick = jnp.concatenate(picks, axis=0).astype(jnp.bfloat16)
        spectra = jnp.concatenate([x[n] for n in range(wide)], axis=1)
        out = lax.dot_general(
            pick, spectra.astype(jnp.bfloat16), (((1,), (1,)), ((), ())),
            preferred_element_type=jnp.float32,
        )
        tiles = NSPEC * streams // LANES
        for d in range(dests):
            for t in range(tiles):
                turned[d, pl.ds(t, 2 * CAP, stride=tiles), :] = out[
                    8 * d : 8 * d + 2 * CAP, t * LANES : (t + 1) * LANES
                ]
        out_ref[...] = turned[...].astype(jnp.bfloat16)


def channelize(voltages, chan_counts, dests, start, streams):
    band = 2 * dests
    frames = voltages.shape[2]
    step = 4 if band <= 64 else 2
    analysis, mixing = tables(band)
    packed = packing(band)[1]
    payload = 2 * CAP * NSPEC * streams // LANES
    steps = streams // step
    first = start // step
    kernel = functools.partial(channelizer, band, dests, streams, step)
    return pl.pallas_call(
        kernel,
        grid_spec=pltpu.PrefetchScalarGridSpec(
            num_scalar_prefetch=1,
            grid=(steps + 1,),
            in_specs=[
                pl.BlockSpec(
                    (step, 1, frames, 2, FFT_LEN),
                    lambda i, c: (first + jnp.minimum(i, steps - 1), 0, 0, 0, 0),
                ),
                pl.BlockSpec(analysis.shape, lambda i, c: (0, 0), pipeline_mode=pl.Buffered(1)),
                pl.BlockSpec(mixing.shape, lambda i, c: (0, 0), pipeline_mode=pl.Buffered(1)),
            ],
            out_specs=pl.BlockSpec((dests, payload, LANES), lambda i, c: (0, 0, 0)),
            scratch_shapes=[
                pltpu.VMEM((packed // LANES, step * 2 * frames + 16, LANES), jnp.float32),
                pltpu.VMEM((SHIFTS * 2 * band // LANES, step * (NSPEC + 8), LANES), jnp.float32),
                pltpu.VMEM((max(1, 2 * band // LANES), NSPEC * streams, LANES), jnp.float32),
                pltpu.VMEM((dests, payload, LANES), jnp.float32),
            ],
        ),
        out_shape=jax.ShapeDtypeStruct((dests, payload, LANES), jnp.bfloat16),
        compiler_params=pltpu.CompilerParams(vmem_limit_bytes=60 * 1024 * 1024),
        cost_estimate=pl.CostEstimate(
            flops=2 * streams * 2 * frames * FFT_LEN * analysis.shape[1],
            bytes_accessed=2 * 2 * frames * FFT_LEN * streams, transcendentals=0,
        ),
    )(chan_counts, voltages, jnp.asarray(analysis), jnp.asarray(mixing))


def correlator(direct, counts, where, dest_ref, *refs):
    out_ref, pre, post = refs[-3:]
    k = pl.program_id(0)
    time_len = pre.shape[1]
    total = pre.shape[2]

    @pl.when(k == 0)
    def _():
        if direct:
            base = 0
            for c in range(len(refs[:-3]) // 2):
                for h, ref in enumerate(refs[2 * c : 2 * c + 2]):
                    sources, payload = ref.shape[0], ref.shape[1]
                    tiles = payload // (2 * CAP)
                    spread = NSPEC // tiles
                    width = LANES // spread
                    lane = lax.broadcasted_iota(jnp.int32, (payload, LANES), 1)
                    for q in range(sources // spread):
                        parts = [ref[spread * q + a].astype(jnp.float32) for a in range(spread)]
                        groups = []
                        for g in range(spread):
                            group = None
                            for a in range(spread):
                                moved = turn_lanes(parts[a], (a - g) * width)
                                group = moved if a == 0 else jnp.where(
                                    lane < a * width, group, moved
                                )
                            groups.append(group)
                        for part in range(2 * CAP):
                            rows = slice(part * tiles, (part + 1) * tiles)
                            both = jnp.concatenate([group[rows] for group in groups], axis=0)
                            pre[
                                part, h * NSPEC : (h + 1) * NSPEC,
                                base + q * LANES : base + (q + 1) * LANES,
                            ] = both.astype(jnp.bfloat16)
                base = base + sources * width
        else:
            pre[...] = refs[0][...]
        spot = lax.broadcasted_iota(jnp.int32, (total, total), 0)
        turn = jnp.where(spot == dest_ref[...], 1.0, 0.0).astype(jnp.bfloat16)
        ordered = lax.dot_general(
            pre[...].reshape(2 * CAP * time_len, total), turn, (((1,), (1,)), ((), ())),
            preferred_element_type=jnp.float32,
        )
        post[...] = ordered.astype(jnp.bfloat16).reshape(CAP, 2 * time_len, total)

    rows = out_ref.shape[3]
    every = post[k]
    near = post[k, :, pl.ds(pl.multiple_of(where[1] * rows, LANES), rows)]
    turned = jnp.concatenate([near[time_len:], -near[:time_len]], axis=0)
    valid = jnp.where(k < counts[where[0]], 1.0, 0.0) / jnp.float32(time_len)
    for part, left in enumerate((near, turned)):
        vis = lax.dot_general(
            left, every, (((0,), (0,)), ((), ())), preferred_element_type=jnp.float32
        )
        out_ref[0, 0, part] = (vis * valid).astype(jnp.bfloat16)


def correlate(pairs, dest, chan_counts, where, total):
    sources, payload = pairs[0][0].shape[:2]
    spread = 2 * CAP * NSPEC // payload
    direct = spread <= 4
    if direct:
        operands = [half for pair in pairs for half in pair]
    else:
        operands = []
        for pair in pairs:
            both = jnp.stack(pair).reshape(2, sources, 2 * CAP, NSPEC // spread, spread, -1)
            both = both.transpose(2, 0, 3, 4, 1, 5).reshape(2 * CAP, 2 * NSPEC, -1)
            operands.append(both)
        operands = [jnp.concatenate(operands, axis=2)]
    specs = [pl.BlockSpec(a.shape, lambda k, c, w: (0, 0, 0)) for a in operands]
    rows = total // 2
    return pl.pallas_call(
        functools.partial(correlator, direct),
        grid_spec=pltpu.PrefetchScalarGridSpec(
            num_scalar_prefetch=2,
            grid=(CAP,),
            in_specs=[pl.BlockSpec((1, total), lambda k, c, w: (0, 0))] + specs,
            out_specs=pl.BlockSpec((1, 1, 2, rows, total), lambda k, c, w: (0, k, 0, 0, 0)),
            scratch_shapes=[
                pltpu.VMEM((2 * CAP, 2 * NSPEC, total), jnp.bfloat16),
                pltpu.VMEM((CAP, 4 * NSPEC, total), jnp.bfloat16),
            ],
        ),
        out_shape=jax.ShapeDtypeStruct((1, CAP, 2, rows, total), jnp.bfloat16),
        compiler_params=pltpu.CompilerParams(vmem_limit_bytes=60 * 1024 * 1024),
    )(chan_counts, where, dest, *operands)


def body(voltages, station_map, chan_counts):
    dests = lax.axis_size("stn")
    streams = voltages.shape[0]
    sizes = (32, 32) if streams == 64 else (streams,)
    pairs = []
    places = []
    start = 0
    dest = (2 * station_map[:, None] + jnp.arange(2, dtype=jnp.int32)[None, :]).reshape(dests, -1)
    for size in sizes:
        outgoing = channelize(voltages, chan_counts, dests, start, size)
        own = lax.all_to_all(outgoing, "stn", split_axis=0, concat_axis=0, tiled=True)
        other = lax.ppermute(own, "blk", [(0, 1), (1, 0)])
        pairs.append((own, other))
        places.append(dest[:, start : start + size].reshape(1, -1))
        start = start + size
    dest = jnp.concatenate(places, axis=1)
    where = jnp.stack([lax.axis_index("stn"), lax.axis_index("blk")]).astype(jnp.int32)
    return correlate(pairs, dest, chan_counts, where, dests * streams)


def solution(mesh):
    return jax.shard_map(
        body,
        mesh=mesh,
        in_specs=(P("stn", "blk", None, None, None), P(), P()),
        out_specs=P("stn", None, None, "blk", None),
        check_vma=False,
    )
```

```python
import functools
import math

import jax
import jax.numpy as jnp
import ml_dtypes
import numpy as np
from jax import lax
from jax.experimental import pallas as pl
from jax.experimental.pallas import tpu as pltpu
from jax.sharding import PartitionSpec as P

FFT_LEN = 4096
TAPS = 16
CAP = 3
NSPEC = 48
LANES = 128


def prototype():
    span = TAPS * FFT_LEN
    points = np.arange(span, dtype=np.float64) + 0.5
    window = 0.5 - 0.5 * np.cos(2.0 * math.pi * points / span)
    shifted = math.pi * (points - span / 2.0) / FFT_LEN
    filt = np.sin(shifted) / shifted * window
    return (filt / np.sqrt(np.sum(filt * filt))).reshape(TAPS, FFT_LEN)


def frame_basis(band, count):
    limit = math.pi * (band + 0.1)
    terms = count + int(limit) + 60
    k = np.arange(terms, dtype=np.float64)
    diagonal = k * (k + 1) + (2 * k * (k + 1) - 1) / ((2 * k + 3) * (2 * k - 1)) * limit**2
    m = k[:-2]
    beside = (m + 2) * (m + 1) / ((2 * m + 3) * np.sqrt((2 * m + 1) * (2 * m + 5))) * limit**2
    matrix = np.diag(diagonal) + np.diag(beside, 2) + np.diag(beside, -2)
    _, vectors = np.linalg.eigh(matrix)
    x = (2 * np.arange(FFT_LEN) + 1.0) / FFT_LEN - 1
    legendre = np.zeros((terms, FFT_LEN))
    legendre[0] = 1.0
    legendre[1] = x
    for j in range(2, terms):
        legendre[j] = ((2 * j - 1) * x * legendre[j - 1] - (j - 1) * legendre[j - 2]) / j
    legendre *= np.sqrt((k + 0.5) * 2.0 / FFT_LEN)[:, None]
    return legendre.T @ vectors[:, :count]


SHIFTS = 4


def turn_lanes(value, shift):
    shift = shift % LANES
    return pltpu.roll(value, shift, axis=1) if shift else value


def packing(band):
    if 3 * (2 * band + 21) <= 2 * LANES:
        return 2 * band + 21, 2 * LANES, True
    count = -(-(2 * band + 32) // (LANES // 2)) * (LANES // 2)
    return count, -(-2 * count // LANES) * LANES, False


@functools.lru_cache(maxsize=4)
def tables(band):
    bf16 = ml_dtypes.bfloat16
    count, packed, triple = packing(band)
    basis = frame_basis(band, count)
    high = basis.astype(bf16)
    low = (basis - high.astype(np.float64)).astype(bf16)
    held = high.astype(np.float64) + low.astype(np.float64)
    lanes = -(-count // LANES) * LANES
    analysis = np.zeros((FFT_LEN, 2 * lanes), bf16)
    analysis[:, :count] = high
    analysis[:, lanes : lanes + count] = low

    phase = 2.0 * math.pi / FFT_LEN * (np.outer(np.arange(FFT_LEN), np.arange(band)) % FFT_LEN)
    wave = np.concatenate([np.cos(phase), -np.sin(phase)], axis=1)
    gram = held.T @ held
    taper = prototype()
    mixing = np.zeros((TAPS // SHIFTS, 2, packed, SHIFTS, 2 * band), bf16)
    for t in range(TAPS):
        real = np.linalg.solve(gram, held.T @ (taper[t][:, None] * wave))
        imag = np.concatenate([-real[:, band:], real[:, :band]], axis=1)
        for c, full in enumerate((real, imag)):
            part = mixing[t // SHIFTS, c, :, t % SHIFTS]
            top = full.astype(bf16)
            part[:count] = top
            part[count : 2 * count] = top
            if triple:
                part[2 * count : 3 * count] = (full - top.astype(np.float64)).astype(bf16)
    return analysis, mixing.reshape(-1, SHIFTS * 2 * band)


def channelizer(
    band, dests, first, streams, step, counts, v_ref, u_hbm, w_hbm, out_ref,
    held, u_ref, w_ref, y, p, x, turned, arrived,
):
    i = pl.program_id(0)
    last = pl.num_programs(0) - 1
    count, packed, triple = packing(band)
    lanes = u_ref.shape[1] // 2
    rows = 2 * v_ref.shape[2]
    tables_in = [
        pltpu.make_async_copy(u_hbm, u_ref, arrived.at[2]),
        pltpu.make_async_copy(w_hbm, w_ref, arrived.at[3]),
    ]

    def fetch(block):
        slot = block % 2
        return pltpu.make_async_copy(
            v_ref.at[pl.ds(first + block * step, step), 0],
            held.at[slot, :, :, :, pl.ds(0, FFT_LEN)],
            arrived.at[slot],
        )

    reach = NSPEC + 8
    wide = max(1, 2 * band // LANES)

    def analyse():
        signal = held[i % 2].reshape(step * rows, FFT_LEN + LANES)[:, :FFT_LEN]
        coeff = jnp.dot(signal, u_ref[...], preferred_element_type=jnp.float32)
        coeff = coeff[:, :lanes] + coeff[:, lanes:]
        high = coeff.astype(jnp.bfloat16).astype(jnp.float32)
        low = coeff - high
        if triple:
            lane = lax.broadcasted_iota(jnp.int32, coeff.shape, 1)
            low = turn_lanes(low, count)
            spare = 2 * count - LANES
            y[0, : step * rows] = jnp.where(lane < count, high, low)
            y[1, : step * rows] = jnp.where(lane < spare, low, turn_lanes(high, spare))
        else:
            both = jnp.concatenate([high[:, :count], low[:, :count]], axis=1)
            for n in range(packed // LANES):
                y[n, : step * rows] = both[:, n * LANES : (n + 1) * LANES]

    def mix(block):
        taps = []
        for r in range(step):
            taps.append(jnp.concatenate([
                y[n, pl.ds(r * rows + 2 * SHIFTS * m + c, reach, stride=2), :]
                for m in range(TAPS // SHIFTS) for c in range(2) for n in range(packed // LANES)
            ], axis=1))
        taps = jnp.concatenate(taps, axis=0).astype(jnp.bfloat16)
        mixed = jnp.dot(taps, w_ref[...], preferred_element_type=jnp.float32)
        for n in range(mixed.shape[1] // LANES):
            p[n] = mixed[:, n * LANES : (n + 1) * LANES]
        for r in range(step):
            place = pl.ds(block * step + r, NSPEC, stride=streams)
            if 2 * band >= LANES:
                for n in range(wide):
                    x[n, place, :] = sum(
                        p[wide * h + n, pl.ds(r * reach + h, NSPEC), :] for h in range(SHIFTS)
                    )
            else:
                per = LANES // (2 * band)
                lane = lax.broadcasted_iota(jnp.int32, (NSPEC, LANES), 1)
                total = None
                for u in reversed(range(per)):
                    part = sum(
                        p[b, pl.ds(r * reach + b * per + u, NSPEC), :] for b in range(SHIFTS // per)
                    )
                    total = part if total is None else jnp.where(
                        lane < 2 * band * (u + 1), part, total
                    )
                whole = total
                for u in range(1, per):
                    whole = whole + turn_lanes(total, -2 * band * u)
                x[0, place, :] = whole

    @pl.when(i == 0)
    def _():
        fetch(0).start()
        for copy in tables_in:
            copy.start()

    @pl.when(i + 1 < last)
    def _():
        fetch(i + 1).start()

    @pl.when(i == 0)
    def _():
        for copy in tables_in:
            copy.wait()

    @pl.when(i < last)
    def _():
        fetch(i).wait()
        mix(jnp.maximum(i - 1, 0))
        analyse()

    @pl.when(i == last)
    def _():
        mix(i - 1)
        lane = lax.broadcasted_iota(jnp.int32, (8, wide * LANES), 1)
        row = lax.broadcasted_iota(jnp.int32, (8, wide * LANES), 0)
        slot = row // 2
        base = (row % 2) * band
        picks = []
        offset = jnp.int32(0)
        for d in range(dests):
            held = counts[d]
            want = offset + jnp.minimum(slot, held - 1) + base
            picks.append(jnp.where((lane == want) & (row < 2 * CAP), 1.0, 0.0))
            offset = offset + held
        pick = jnp.concatenate(picks, axis=0).astype(jnp.bfloat16)
        spectra = jnp.concatenate([x[n] for n in range(wide)], axis=1)
        out = lax.dot_general(
            pick, spectra.astype(jnp.bfloat16), (((1,), (1,)), ((), ())),
            preferred_element_type=jnp.float32,
        )
        tiles = NSPEC * streams // LANES
        for d in range(dests):
            for t in range(tiles):
                turned[d, pl.ds(t, 2 * CAP, stride=tiles), :] = out[
                    8 * d : 8 * d + 2 * CAP, t * LANES : (t + 1) * LANES
                ]
        out_ref[...] = turned[...].astype(jnp.bfloat16)


def channelize(voltages, chan_counts, dests, start, streams):
    band = 2 * dests
    frames = voltages.shape[2]
    step = 4 if band <= 64 else 2
    analysis, mixing = tables(band)
    packed = packing(band)[1]
    payload = 2 * CAP * NSPEC * streams // LANES
    steps = streams // step
    kernel = functools.partial(channelizer, band, dests, start, streams, step)
    return pl.pallas_call(
        kernel,
        grid_spec=pltpu.PrefetchScalarGridSpec(
            num_scalar_prefetch=1,
            grid=(steps + 1,),
            in_specs=[pl.BlockSpec(memory_space=pl.ANY)] * 3,
            out_specs=pl.BlockSpec((dests, payload, LANES), lambda i, c: (0, 0, 0)),
            scratch_shapes=[
                pltpu.VMEM((2, step, frames, 2, FFT_LEN + LANES), jnp.bfloat16),
                pltpu.VMEM(analysis.shape, jnp.bfloat16),
                pltpu.VMEM(mixing.shape, jnp.bfloat16),
                pltpu.VMEM((packed // LANES, step * 2 * frames + 16, LANES), jnp.float32),
                pltpu.VMEM((SHIFTS * 2 * band // LANES, step * (NSPEC + 8), LANES), jnp.float32),
                pltpu.VMEM((max(1, 2 * band // LANES), NSPEC * streams, LANES), jnp.float32),
                pltpu.VMEM((dests, payload, LANES), jnp.float32),
                pltpu.SemaphoreType.DMA((4,)),
            ],
        ),
        out_shape=jax.ShapeDtypeStruct((dests, payload, LANES), jnp.bfloat16),
        compiler_params=pltpu.CompilerParams(vmem_limit_bytes=60 * 1024 * 1024),
        cost_estimate=pl.CostEstimate(
            flops=2 * streams * 2 * frames * FFT_LEN * analysis.shape[1],
            bytes_accessed=2 * 2 * frames * FFT_LEN * streams, transcendentals=0,
        ),
    )(chan_counts, voltages, jnp.asarray(analysis), jnp.asarray(mixing))


def correlator(direct, counts, where, dest_ref, *refs):
    out_ref, pre, post = refs[-3:]
    k = pl.program_id(0)
    time_len = pre.shape[1]
    total = pre.shape[2]

    @pl.when(k == 0)
    def _():
        if direct:
            base = 0
            for c in range(len(refs[:-3]) // 2):
                for h, ref in enumerate(refs[2 * c : 2 * c + 2]):
                    sources, payload = ref.shape[0], ref.shape[1]
                    tiles = payload // (2 * CAP)
                    spread = NSPEC // tiles
                    width = LANES // spread
                    lane = lax.broadcasted_iota(jnp.int32, (payload, LANES), 1)
                    for q in range(sources // spread):
                        parts = [ref[spread * q + a].astype(jnp.float32) for a in range(spread)]
                        groups = []
                        for g in range(spread):
                            group = None
                            for a in range(spread):
                                moved = turn_lanes(parts[a], (a - g) * width)
                                group = moved if a == 0 else jnp.where(
                                    lane < a * width, group, moved
                                )
                            groups.append(group)
                        for part in range(2 * CAP):
                            rows = slice(part * tiles, (part + 1) * tiles)
                            both = jnp.concatenate([group[rows] for group in groups], axis=0)
                            pre[
                                part, h * NSPEC : (h + 1) * NSPEC,
                                base + q * LANES : base + (q + 1) * LANES,
                            ] = both.astype(jnp.bfloat16)
                base = base + sources * width
        else:
            pre[...] = refs[0][...]
        spot = lax.broadcasted_iota(jnp.int32, (total, total), 0)
        turn = jnp.where(spot == dest_ref[...], 1.0, 0.0).astype(jnp.bfloat16)
        ordered = lax.dot_general(
            pre[...].reshape(2 * CAP * time_len, total), turn, (((1,), (1,)), ((), ())),
            preferred_element_type=jnp.float32,
        )
        post[...] = ordered.astype(jnp.bfloat16).reshape(CAP, 2 * time_len, total)

    rows = out_ref.shape[3]
    every = post[k]
    near = post[k, :, pl.ds(pl.multiple_of(where[1] * rows, LANES), rows)]
    turned = jnp.concatenate([near[time_len:], -near[:time_len]], axis=0)
    valid = jnp.where(k < counts[where[0]], 1.0, 0.0) / jnp.float32(time_len)
    for part, left in enumerate((near, turned)):
        vis = lax.dot_general(
            left, every, (((0,), (0,)), ((), ())), preferred_element_type=jnp.float32
        )
        out_ref[0, 0, part] = (vis * valid).astype(jnp.bfloat16)


def correlate(pairs, dest, chan_counts, where, total):
    sources, payload = pairs[0][0].shape[:2]
    spread = 2 * CAP * NSPEC // payload
    direct = spread <= 4
    if direct:
        operands = [half for pair in pairs for half in pair]
    else:
        operands = []
        for pair in pairs:
            both = jnp.stack(pair).reshape(2, sources, 2 * CAP, NSPEC // spread, spread, -1)
            both = both.transpose(2, 0, 3, 4, 1, 5).reshape(2 * CAP, 2 * NSPEC, -1)
            operands.append(both)
        operands = [jnp.concatenate(operands, axis=2)]
    specs = [pl.BlockSpec(a.shape, lambda k, c, w: (0, 0, 0)) for a in operands]
    rows = total // 2
    return pl.pallas_call(
        functools.partial(correlator, direct),
        grid_spec=pltpu.PrefetchScalarGridSpec(
            num_scalar_prefetch=2,
            grid=(CAP,),
            in_specs=[pl.BlockSpec((1, total), lambda k, c, w: (0, 0))] + specs,
            out_specs=pl.BlockSpec((1, 1, 2, rows, total), lambda k, c, w: (0, k, 0, 0, 0)),
            scratch_shapes=[
                pltpu.VMEM((2 * CAP, 2 * NSPEC, total), jnp.bfloat16),
                pltpu.VMEM((CAP, 4 * NSPEC, total), jnp.bfloat16),
            ],
        ),
        out_shape=jax.ShapeDtypeStruct((1, CAP, 2, rows, total), jnp.bfloat16),
        compiler_params=pltpu.CompilerParams(vmem_limit_bytes=60 * 1024 * 1024),
    )(chan_counts, where, dest, *operands)


def body(voltages, station_map, chan_counts):
    dests = lax.axis_size("stn")
    streams = voltages.shape[0]
    sizes = (32, 32) if streams == 64 else (streams,)
    pairs = []
    places = []
    start = 0
    dest = (2 * station_map[:, None] + jnp.arange(2, dtype=jnp.int32)[None, :]).reshape(dests, -1)
    for size in sizes:
        outgoing = channelize(voltages, chan_counts, dests, start, size)
        own = lax.all_to_all(outgoing, "stn", split_axis=0, concat_axis=0, tiled=True)
        other = lax.ppermute(own, "blk", [(0, 1), (1, 0)])
        pairs.append((own, other))
        places.append(dest[:, start : start + size].reshape(1, -1))
        start = start + size
    dest = jnp.concatenate(places, axis=1)
    where = jnp.stack([lax.axis_index("stn"), lax.axis_index("blk")]).astype(jnp.int32)
    return correlate(pairs, dest, chan_counts, where, dests * streams)


def solution(mesh):
    return jax.shard_map(
        body,
        mesh=mesh,
        in_specs=(P("stn", "blk", None, None, None), P(), P()),
        out_specs=P("stn", None, None, "blk", None),
        check_vma=False,
    )
```

```python
import functools
import math

import jax
import jax.numpy as jnp
import ml_dtypes
import numpy as np
from jax import lax
from jax.experimental import pallas as pl
from jax.experimental.pallas import tpu as pltpu
from jax.sharding import PartitionSpec as P

FFT_LEN = 4096
TAPS = 16
CAP = 3
NSPEC = 48
LANES = 128


def prototype():
    span = TAPS * FFT_LEN
    points = np.arange(span, dtype=np.float64) + 0.5
    window = 0.5 - 0.5 * np.cos(2.0 * math.pi * points / span)
    shifted = math.pi * (points - span / 2.0) / FFT_LEN
    filt = np.sin(shifted) / shifted * window
    return (filt / np.sqrt(np.sum(filt * filt))).reshape(TAPS, FFT_LEN)


def frame_basis(band, count):
    limit = math.pi * (band + 0.1)
    terms = count + int(limit) + 60
    k = np.arange(terms, dtype=np.float64)
    diagonal = k * (k + 1) + (2 * k * (k + 1) - 1) / ((2 * k + 3) * (2 * k - 1)) * limit**2
    m = k[:-2]
    beside = (m + 2) * (m + 1) / ((2 * m + 3) * np.sqrt((2 * m + 1) * (2 * m + 5))) * limit**2
    matrix = np.diag(diagonal) + np.diag(beside, 2) + np.diag(beside, -2)
    _, vectors = np.linalg.eigh(matrix)
    x = (2 * np.arange(FFT_LEN) + 1.0) / FFT_LEN - 1
    legendre = np.zeros((terms, FFT_LEN))
    legendre[0] = 1.0
    legendre[1] = x
    for j in range(2, terms):
        legendre[j] = ((2 * j - 1) * x * legendre[j - 1] - (j - 1) * legendre[j - 2]) / j
    legendre *= np.sqrt((k + 0.5) * 2.0 / FFT_LEN)[:, None]
    return legendre.T @ vectors[:, :count]


SHIFTS = 4


def turn_lanes(value, shift):
    shift = shift % LANES
    return pltpu.roll(value, shift, axis=1) if shift else value


def packing(band):
    if 3 * (2 * band + 21) <= 2 * LANES:
        return 2 * band + 21, 2 * LANES, True
    count = -(-(2 * band + 32) // (LANES // 2)) * (LANES // 2)
    return count, -(-2 * count // LANES) * LANES, False


@functools.lru_cache(maxsize=4)
def tables(band):
    bf16 = ml_dtypes.bfloat16
    count, packed, triple = packing(band)
    basis = frame_basis(band, count)
    high = basis.astype(bf16)
    low = (basis - high.astype(np.float64)).astype(bf16)
    held = high.astype(np.float64) + low.astype(np.float64)
    lanes = -(-count // LANES) * LANES
    analysis = np.zeros((FFT_LEN, 2 * lanes), bf16)
    analysis[:, :count] = high
    analysis[:, lanes : lanes + count] = low

    phase = 2.0 * math.pi / FFT_LEN * (np.outer(np.arange(FFT_LEN), np.arange(band)) % FFT_LEN)
    wave = np.concatenate([np.cos(phase), -np.sin(phase)], axis=1)
    gram = held.T @ held
    taper = prototype()
    mixing = np.zeros((TAPS // SHIFTS, 2, packed, SHIFTS, 2 * band), bf16)
    for t in range(TAPS):
        real = np.linalg.solve(gram, held.T @ (taper[t][:, None] * wave))
        imag = np.concatenate([-real[:, band:], real[:, :band]], axis=1)
        for c, full in enumerate((real, imag)):
            part = mixing[t // SHIFTS, c, :, t % SHIFTS]
            top = full.astype(bf16)
            part[:count] = top
            part[count : 2 * count] = top
            if triple:
                part[2 * count : 3 * count] = (full - top.astype(np.float64)).astype(bf16)
    return analysis, mixing.reshape(-1, SHIFTS * 2 * band)


def channelizer(
    band, dests, first, streams, step, by_tile, counts, v_ref, u_hbm, w_hbm, out_ref,
    held, u_ref, w_ref, y, p, x, turned, arrived,
):
    i = pl.program_id(0)
    last = pl.num_programs(0) - 1
    count, packed, triple = packing(band)
    lanes = u_ref.shape[1] // 2
    rows = 2 * v_ref.shape[2]
    tables_in = [
        pltpu.make_async_copy(u_hbm, u_ref, arrived.at[2]),
        pltpu.make_async_copy(w_hbm, w_ref, arrived.at[3]),
    ]

    tiles_in = FFT_LEN // LANES

    def fetch(block):
        slot = block % 2
        frames_in = v_ref.at[pl.ds(first + block * step, step), 0]
        if by_tile:
            return [
                pltpu.make_async_copy(
                    frames_in.at[:, :, :, pl.ds(j * LANES, LANES)], held.at[slot, j], arrived.at[slot]
                )
                for j in range(tiles_in)
            ]
        return [pltpu.make_async_copy(frames_in, held.at[slot], arrived.at[slot])]

    reach = NSPEC + 8
    wide = max(1, 2 * band // LANES)

    def analyse():
        if by_tile:
            signal = jnp.concatenate(
                [held[i % 2, j].reshape(step * rows, LANES) for j in range(tiles_in)], axis=1
            )
        else:
            signal = held[i % 2].reshape(step * rows, FFT_LEN)
        coeff = jnp.dot(signal, u_ref[...], preferred_element_type=jnp.float32)
        coeff = coeff[:, :lanes] + coeff[:, lanes:]
        high = coeff.astype(jnp.bfloat16).astype(jnp.float32)
        low = coeff - high
        if triple:
            lane = lax.broadcasted_iota(jnp.int32, coeff.shape, 1)
            low = turn_lanes(low, count)
            spare = 2 * count - LANES
            y[0, : step * rows] = jnp.where(lane < count, high, low)
            y[1, : step * rows] = jnp.where(lane < spare, low, turn_lanes(high, spare))
        else:
            both = jnp.concatenate([high[:, :count], low[:, :count]], axis=1)
            for n in range(packed // LANES):
                y[n, : step * rows] = both[:, n * LANES : (n + 1) * LANES]

    def mix(block):
        taps = []
        for r in range(step):
            taps.append(jnp.concatenate([
                y[n, pl.ds(r * rows + 2 * SHIFTS * m + c, reach, stride=2), :]
                for m in range(TAPS // SHIFTS) for c in range(2) for n in range(packed // LANES)
            ], axis=1))
        taps = jnp.concatenate(taps, axis=0).astype(jnp.bfloat16)
        mixed = jnp.dot(taps, w_ref[...], preferred_element_type=jnp.float32)
        for n in range(mixed.shape[1] // LANES):
            p[n] = mixed[:, n * LANES : (n + 1) * LANES]
        for r in range(step):
            place = pl.ds(block * step + r, NSPEC, stride=streams)
            if 2 * band >= LANES:
                for n in range(wide):
                    x[n, place, :] = sum(
                        p[wide * h + n, pl.ds(r * reach + h, NSPEC), :] for h in range(SHIFTS)
                    )
            else:
                per = LANES // (2 * band)
                lane = lax.broadcasted_iota(jnp.int32, (NSPEC, LANES), 1)
                total = None
                for u in reversed(range(per)):
                    part = sum(
                        p[b, pl.ds(r * reach + b * per + u, NSPEC), :] for b in range(SHIFTS // per)
                    )
                    total = part if total is None else jnp.where(
                        lane < 2 * band * (u + 1), part, total
                    )
                whole = total
                for u in range(1, per):
                    whole = whole + turn_lanes(total, -2 * band * u)
                x[0, place, :] = whole

    @pl.when(i == 0)
    def _():
        for copy in fetch(0) + tables_in:
            copy.start()

    @pl.when(i + 1 < last)
    def _():
        for copy in fetch(i + 1):
            copy.start()

    @pl.when(i == 0)
    def _():
        for copy in tables_in:
            copy.wait()

    @pl.when(i < last)
    def _():
        whole = held.at[i % 2]
        pltpu.make_async_copy(whole, whole, arrived.at[i % 2]).wait()
        mix(jnp.maximum(i - 1, 0))
        analyse()

    @pl.when(i == last)
    def _():
        mix(i - 1)
        lane = lax.broadcasted_iota(jnp.int32, (8, wide * LANES), 1)
        row = lax.broadcasted_iota(jnp.int32, (8, wide * LANES), 0)
        slot = row // 2
        base = (row % 2) * band
        picks = []
        offset = jnp.int32(0)
        for d in range(dests):
            held = counts[d]
            want = offset + jnp.minimum(slot, held - 1) + base
            picks.append(jnp.where((lane == want) & (row < 2 * CAP), 1.0, 0.0))
            offset = offset + held
        pick = jnp.concatenate(picks, axis=0).astype(jnp.bfloat16)
        spectra = jnp.concatenate([x[n] for n in range(wide)], axis=1)
        out = lax.dot_general(
            pick, spectra.astype(jnp.bfloat16), (((1,), (1,)), ((), ())),
            preferred_element_type=jnp.float32,
        )
        tiles = NSPEC * streams // LANES
        for d in range(dests):
            for t in range(tiles):
                turned[d, pl.ds(t, 2 * CAP, stride=tiles), :] = out[
                    8 * d : 8 * d + 2 * CAP, t * LANES : (t + 1) * LANES
                ]
        out_ref[...] = turned[...].astype(jnp.bfloat16)


def channelize(voltages, chan_counts, dests, start, streams, step, by_tile):
    band = 2 * dests
    frames = voltages.shape[2]
    analysis, mixing = tables(band)
    packed = packing(band)[1]
    payload = 2 * CAP * NSPEC * streams // LANES
    steps = streams // step
    kernel = functools.partial(channelizer, band, dests, start, streams, step, by_tile)
    held = (FFT_LEN // LANES, step, frames, 2, LANES) if by_tile else (step, frames, 2, FFT_LEN)
    return pl.pallas_call(
        kernel,
        grid_spec=pltpu.PrefetchScalarGridSpec(
            num_scalar_prefetch=1,
            grid=(steps + 1,),
            in_specs=[pl.BlockSpec(memory_space=pl.ANY)] * 3,
            out_specs=pl.BlockSpec((dests, payload, LANES), lambda i, c: (0, 0, 0)),
            scratch_shapes=[
                pltpu.VMEM((2,) + held, jnp.bfloat16),
                pltpu.VMEM(analysis.shape, jnp.bfloat16),
                pltpu.VMEM(mixing.shape, jnp.bfloat16),
                pltpu.VMEM((packed // LANES, step * 2 * frames + 16, LANES), jnp.float32),
                pltpu.VMEM((SHIFTS * 2 * band // LANES, step * (NSPEC + 8), LANES), jnp.float32),
                pltpu.VMEM((max(1, 2 * band // LANES), NSPEC * streams, LANES), jnp.float32),
                pltpu.VMEM((dests, payload, LANES), jnp.float32),
                pltpu.SemaphoreType.DMA((4,)),
            ],
        ),
        out_shape=jax.ShapeDtypeStruct((dests, payload, LANES), jnp.bfloat16),
        compiler_params=pltpu.CompilerParams(vmem_limit_bytes=60 * 1024 * 1024),
        cost_estimate=pl.CostEstimate(
            flops=2 * streams * 2 * frames * FFT_LEN * analysis.shape[1],
            bytes_accessed=2 * 2 * frames * FFT_LEN * streams, transcendentals=0,
        ),
    )(chan_counts, voltages, jnp.asarray(analysis), jnp.asarray(mixing))


def in_order(refs, dest_ref, pre, total):
    if len(refs) == 2:
        for h, ref in enumerate(refs):
            sources, payload = ref.shape[0], ref.shape[1]
            tiles = payload // (2 * CAP)
            spread = NSPEC // tiles
            width = LANES // spread
            lane = lax.broadcasted_iota(jnp.int32, (payload, LANES), 1)
            for q in range(sources // spread):
                parts = [ref[spread * q + a].astype(jnp.float32) for a in range(spread)]
                groups = []
                for g in range(spread):
                    group = None
                    for a in range(spread):
                        moved = turn_lanes(parts[a], (a - g) * width)
                        group = moved if a == 0 else jnp.where(lane < a * width, group, moved)
                    groups.append(group)
                for part in range(2 * CAP):
                    rows = slice(part * tiles, (part + 1) * tiles)
                    both = jnp.concatenate([group[rows] for group in groups], axis=0)
                    pre[part, h * NSPEC : (h + 1) * NSPEC, q * LANES : (q + 1) * LANES] = (
                        both.astype(jnp.bfloat16)
                    )
    else:
        pre[...] = refs[0][...]
    parts, time_len, held = pre.shape
    spot = lax.broadcasted_iota(jnp.int32, (total, held), 0)
    turn = jnp.where(spot == dest_ref[...], 1.0, 0.0).astype(jnp.bfloat16)
    return lax.dot_general(
        pre[...].reshape(parts * time_len, held), turn, (((1,), (1,)), ((), ())),
        preferred_element_type=jnp.float32,
    )


def correlator(given, counts, where, dest_ref, *refs):
    out_ref, pre, post = refs[-3:]
    refs = refs[:-3]
    k = pl.program_id(0)
    time_len = pre.shape[1]

    @pl.when(k == 0)
    def _():
        ordered = in_order(refs[:given], dest_ref, pre, post.shape[2])
        for ref in refs[given:]:
            ordered = ordered + ref[...].astype(jnp.float32)
        post[...] = ordered.astype(jnp.bfloat16).reshape(post.shape)

    rows = out_ref.shape[3]
    every = post[k]
    near = post[k, :, pl.ds(pl.multiple_of(where[1] * rows, LANES), rows)]
    turned = jnp.concatenate([near[time_len:], -near[:time_len]], axis=0)
    valid = jnp.where(k < counts[where[0]], 1.0, 0.0) / jnp.float32(time_len)
    for part, left in enumerate((near, turned)):
        vis = lax.dot_general(
            left, every, (((0,), (0,)), ((), ())), preferred_element_type=jnp.float32
        )
        out_ref[0, 0, part] = (vis * valid).astype(jnp.bfloat16)


def orderer(dest_ref, *refs):
    out_ref, pre = refs[-2:]
    out_ref[...] = in_order(refs[:-2], dest_ref, pre, out_ref.shape[1]).astype(jnp.bfloat16)


def halves(own, other):
    sources, payload = own.shape[:2]
    spread = 2 * CAP * NSPEC // payload
    held = (2 * CAP, 2 * NSPEC, sources * LANES // spread)
    if spread <= 4:
        return [own, other], held
    both = jnp.stack([own, other]).reshape(2, sources, 2 * CAP, NSPEC // spread, spread, -1)
    return [both.transpose(2, 0, 3, 4, 1, 5).reshape(held)], held


def order(own, other, dest, total):
    operands, held = halves(own, other)
    return pl.pallas_call(
        orderer,
        out_shape=jax.ShapeDtypeStruct((held[0] * held[1], total), jnp.bfloat16),
        scratch_shapes=[pltpu.VMEM(held, jnp.bfloat16)],
        compiler_params=pltpu.CompilerParams(vmem_limit_bytes=60 * 1024 * 1024),
        cost_estimate=pl.CostEstimate(
            flops=2 * held[0] * held[1] * held[2] * total, bytes_accessed=4 * own.size,
            transcendentals=0,
        ),
    )(dest, *operands)


def correlate(own, other, dest, before, chan_counts, where, total):
    operands, held = halves(own, other)
    given = len(operands)
    operands = operands + before
    specs = [
        pl.BlockSpec(a.shape, functools.partial(lambda n, k, c, w: (0,) * n, a.ndim))
        for a in [dest] + operands
    ]
    rows = total // 2
    return pl.pallas_call(
        functools.partial(correlator, given),
        grid_spec=pltpu.PrefetchScalarGridSpec(
            num_scalar_prefetch=2,
            grid=(CAP,),
            in_specs=specs,
            out_specs=pl.BlockSpec((1, 1, 2, rows, total), lambda k, c, w: (0, k, 0, 0, 0)),
            scratch_shapes=[
                pltpu.VMEM(held, jnp.bfloat16),
                pltpu.VMEM((CAP, 4 * NSPEC, total), jnp.bfloat16),
            ],
        ),
        out_shape=jax.ShapeDtypeStruct((1, CAP, 2, rows, total), jnp.bfloat16),
        compiler_params=pltpu.CompilerParams(vmem_limit_bytes=60 * 1024 * 1024),
    )(chan_counts, where, dest, *operands)


def body(voltages, station_map, chan_counts):
    dests = lax.axis_size("stn")
    streams = voltages.shape[0]
    total = dests * streams
    plan = ((32, 4, True), (32, 8, False)) if streams == 64 else ((streams, 2, False),)
    dest = (2 * station_map[:, None] + jnp.arange(2, dtype=jnp.int32)[None, :]).reshape(dests, -1)
    where = jnp.stack([lax.axis_index("stn"), lax.axis_index("blk")]).astype(jnp.int32)
    start = 0
    before = []
    for size, step, by_tile in plan:
        outgoing = channelize(voltages, chan_counts, dests, start, size, step, by_tile)
        own = lax.all_to_all(outgoing, "stn", split_axis=0, concat_axis=0, tiled=True)
        other = lax.ppermute(own, "blk", [(0, 1), (1, 0)])
        place = dest[:, start : start + size].reshape(1, -1)
        start = start + size
        if start < streams:
            before.append(order(own, other, place, total))
    return correlate(own, other, place, before, chan_counts, where, total)


def solution(mesh):
    return jax.shard_map(
        body,
        mesh=mesh,
        in_specs=(P("stn", "blk", None, None, None), P(), P()),
        out_specs=P("stn", None, None, "blk", None),
        check_vma=False,
    )
```

```python
import functools
import math

import jax
import jax.numpy as jnp
import ml_dtypes
import numpy as np
from jax import lax
from jax.experimental import pallas as pl
from jax.experimental.pallas import tpu as pltpu
from jax.sharding import PartitionSpec as P

FFT_LEN = 4096
TAPS = 16
CAP = 3
NSPEC = 48
LANES = 128


def prototype():
    span = TAPS * FFT_LEN
    points = np.arange(span, dtype=np.float64) + 0.5
    window = 0.5 - 0.5 * np.cos(2.0 * math.pi * points / span)
    shifted = math.pi * (points - span / 2.0) / FFT_LEN
    filt = np.sin(shifted) / shifted * window
    return (filt / np.sqrt(np.sum(filt * filt))).reshape(TAPS, FFT_LEN)


def frame_basis(band, count):
    limit = math.pi * (band + 0.1)
    terms = count + int(limit) + 60
    k = np.arange(terms, dtype=np.float64)
    diagonal = k * (k + 1) + (2 * k * (k + 1) - 1) / ((2 * k + 3) * (2 * k - 1)) * limit**2
    m = k[:-2]
    beside = (m + 2) * (m + 1) / ((2 * m + 3) * np.sqrt((2 * m + 1) * (2 * m + 5))) * limit**2
    matrix = np.diag(diagonal) + np.diag(beside, 2) + np.diag(beside, -2)
    _, vectors = np.linalg.eigh(matrix)
    x = (2 * np.arange(FFT_LEN) + 1.0) / FFT_LEN - 1
    legendre = np.zeros((terms, FFT_LEN))
    legendre[0] = 1.0
    legendre[1] = x
    for j in range(2, terms):
        legendre[j] = ((2 * j - 1) * x * legendre[j - 1] - (j - 1) * legendre[j - 2]) / j
    legendre *= np.sqrt((k + 0.5) * 2.0 / FFT_LEN)[:, None]
    return legendre.T @ vectors[:, :count]


SHIFTS = 4


def turn_lanes(value, shift):
    shift = shift % LANES
    return pltpu.roll(value, shift, axis=1) if shift else value


def packing(band):
    if 3 * (2 * band + 21) <= 2 * LANES:
        return 2 * band + 21, 2 * LANES, True
    count = -(-(2 * band + 32) // (LANES // 2)) * (LANES // 2)
    return count, -(-2 * count // LANES) * LANES, False


@functools.lru_cache(maxsize=4)
def tables(band):
    bf16 = ml_dtypes.bfloat16
    count, packed, triple = packing(band)
    basis = frame_basis(band, count)
    high = basis.astype(bf16)
    low = (basis - high.astype(np.float64)).astype(bf16)
    held = high.astype(np.float64) + low.astype(np.float64)
    lanes = -(-count // LANES) * LANES
    analysis = np.zeros((FFT_LEN, 2 * lanes), bf16)
    analysis[:, :count] = high
    analysis[:, lanes : lanes + count] = low

    phase = 2.0 * math.pi / FFT_LEN * (np.outer(np.arange(FFT_LEN), np.arange(band)) % FFT_LEN)
    wave = np.concatenate([np.cos(phase), -np.sin(phase)], axis=1)
    gram = held.T @ held
    taper = prototype()
    mixing = np.zeros((TAPS // SHIFTS, 2, packed, SHIFTS, 2 * band), bf16)
    for t in range(TAPS):
        real = np.linalg.solve(gram, held.T @ (taper[t][:, None] * wave))
        imag = np.concatenate([-real[:, band:], real[:, :band]], axis=1)
        for c, full in enumerate((real, imag)):
            part = mixing[t // SHIFTS, c, :, t % SHIFTS]
            top = full.astype(bf16)
            part[:count] = top
            part[count : 2 * count] = top
            if triple:
                part[2 * count : 3 * count] = (full - top.astype(np.float64)).astype(bf16)
    return analysis, mixing.reshape(-1, SHIFTS * 2 * band)


def channelizer(
    band, dests, first, streams, step, turned_dot, counts, v_ref, u_hbm, w_hbm, out_ref,
    held, u_ref, w_ref, y, p, x, turned, arrived,
):
    i = pl.program_id(0)
    last = pl.num_programs(0) - 1
    count, packed, triple = packing(band)
    lanes = u_ref.shape[0 if turned_dot else 1] // 2
    rows = 2 * v_ref.shape[2]
    tables_in = [
        pltpu.make_async_copy(u_hbm, u_ref, arrived.at[2]),
        pltpu.make_async_copy(w_hbm, w_ref, arrived.at[3]),
    ]

    def fetch(block):
        slot = block % 2
        frames_in = v_ref.at[pl.ds(first + block * step, step), 0]
        return [pltpu.make_async_copy(frames_in, held.at[slot], arrived.at[slot])]

    reach = NSPEC + 8
    wide = max(1, 2 * band // LANES)

    def analyse():
        if turned_dot:
            signal = held[i % 2].reshape(step * rows, FFT_LEN)
            coeff = lax.dot_general(
                u_ref[...], signal, (((1,), (1,)), ((), ())), preferred_element_type=jnp.float32
            )
            coeff = (coeff[:lanes] + coeff[lanes:]).T
        else:
            coeff = []
            for part in range(2):
                signal = held[i % 2, part * step // 2 : (part + 1) * step // 2]
                signal = signal.reshape(step * rows // 2, FFT_LEN)
                coeff.append(jnp.dot(signal, u_ref[...], preferred_element_type=jnp.float32))
            coeff = jnp.concatenate(coeff, axis=0)
            coeff = coeff[:, :lanes] + coeff[:, lanes:]
        high = coeff.astype(jnp.bfloat16).astype(jnp.float32)
        low = coeff - high
        if triple:
            lane = lax.broadcasted_iota(jnp.int32, coeff.shape, 1)
            low = turn_lanes(low, count)
            spare = 2 * count - LANES
            y[0, : step * rows] = jnp.where(lane < count, high, low)
            y[1, : step * rows] = jnp.where(lane < spare, low, turn_lanes(high, spare))
        else:
            both = jnp.concatenate([high[:, :count], low[:, :count]], axis=1)
            for n in range(packed // LANES):
                y[n, : step * rows] = both[:, n * LANES : (n + 1) * LANES]

    def mix(block):
        taps = []
        for r in range(step):
            taps.append(jnp.concatenate([
                y[n, pl.ds(r * rows + 2 * SHIFTS * m + c, reach, stride=2), :]
                for m in range(TAPS // SHIFTS) for c in range(2) for n in range(packed // LANES)
            ], axis=1))
        taps = jnp.concatenate(taps, axis=0).astype(jnp.bfloat16)
        mixed = jnp.dot(taps, w_ref[...], preferred_element_type=jnp.float32)
        for n in range(mixed.shape[1] // LANES):
            p[n] = mixed[:, n * LANES : (n + 1) * LANES]
        for r in range(step):
            place = pl.ds(block * step + r, NSPEC, stride=streams)
            if 2 * band >= LANES:
                for n in range(wide):
                    x[n, place, :] = sum(
                        p[wide * h + n, pl.ds(r * reach + h, NSPEC), :] for h in range(SHIFTS)
                    )
            else:
                per = LANES // (2 * band)
                lane = lax.broadcasted_iota(jnp.int32, (NSPEC, LANES), 1)
                total = None
                for u in reversed(range(per)):
                    part = sum(
                        p[b, pl.ds(r * reach + b * per + u, NSPEC), :] for b in range(SHIFTS // per)
                    )
                    total = part if total is None else jnp.where(
                        lane < 2 * band * (u + 1), part, total
                    )
                whole = total
                for u in range(1, per):
                    whole = whole + turn_lanes(total, -2 * band * u)
                x[0, place, :] = whole

    @pl.when(i == 0)
    def _():
        for copy in fetch(0) + tables_in:
            copy.start()

    @pl.when(i + 1 < last)
    def _():
        for copy in fetch(i + 1):
            copy.start()

    @pl.when(i == 0)
    def _():
        for copy in tables_in:
            copy.wait()

    @pl.when(i < last)
    def _():
        whole = held.at[i % 2]
        pltpu.make_async_copy(whole, whole, arrived.at[i % 2]).wait()
        mix(jnp.maximum(i - 1, 0))
        analyse()

    @pl.when(i == last)
    def _():
        mix(i - 1)
        lane = lax.broadcasted_iota(jnp.int32, (8, wide * LANES), 1)
        row = lax.broadcasted_iota(jnp.int32, (8, wide * LANES), 0)
        slot = row // 2
        base = (row % 2) * band
        picks = []
        offset = jnp.int32(0)
        for d in range(dests):
            held = counts[d]
            want = offset + jnp.minimum(slot, held - 1) + base
            picks.append(jnp.where((lane == want) & (row < 2 * CAP), 1.0, 0.0))
            offset = offset + held
        pick = jnp.concatenate(picks, axis=0).astype(jnp.bfloat16)
        spectra = jnp.concatenate([x[n] for n in range(wide)], axis=1)
        out = lax.dot_general(
            pick, spectra.astype(jnp.bfloat16), (((1,), (1,)), ((), ())),
            preferred_element_type=jnp.float32,
        )
        tiles = NSPEC * streams // LANES
        for d in range(dests):
            for t in range(tiles):
                turned[d, pl.ds(t, 2 * CAP, stride=tiles), :] = out[
                    8 * d : 8 * d + 2 * CAP, t * LANES : (t + 1) * LANES
                ]
        out_ref[...] = turned[...].astype(jnp.bfloat16)


def channelize(voltages, chan_counts, dests, start, streams, step, turned_dot):
    band = 2 * dests
    frames = voltages.shape[2]
    analysis, mixing = tables(band)
    if turned_dot:
        analysis = np.ascontiguousarray(analysis.T)
    packed = packing(band)[1]
    payload = 2 * CAP * NSPEC * streams // LANES
    steps = streams // step
    kernel = functools.partial(channelizer, band, dests, start, streams, step, turned_dot)
    return pl.pallas_call(
        kernel,
        grid_spec=pltpu.PrefetchScalarGridSpec(
            num_scalar_prefetch=1,
            grid=(steps + 1,),
            in_specs=[pl.BlockSpec(memory_space=pl.ANY)] * 3,
            out_specs=pl.BlockSpec((dests, payload, LANES), lambda i, c: (0, 0, 0)),
            scratch_shapes=[
                pltpu.VMEM((2, step, frames, 2, FFT_LEN), jnp.bfloat16),
                pltpu.VMEM(analysis.shape, jnp.bfloat16),
                pltpu.VMEM(mixing.shape, jnp.bfloat16),
                pltpu.VMEM((packed // LANES, step * 2 * frames + 16, LANES), jnp.float32),
                pltpu.VMEM((SHIFTS * 2 * band // LANES, step * (NSPEC + 8), LANES), jnp.float32),
                pltpu.VMEM((max(1, 2 * band // LANES), NSPEC * streams, LANES), jnp.float32),
                pltpu.VMEM((dests, payload, LANES), jnp.float32),
                pltpu.SemaphoreType.DMA((4,)),
            ],
        ),
        out_shape=jax.ShapeDtypeStruct((dests, payload, LANES), jnp.bfloat16),
        compiler_params=pltpu.CompilerParams(vmem_limit_bytes=60 * 1024 * 1024),
        cost_estimate=pl.CostEstimate(
            flops=2 * streams * 2 * frames * analysis.size,
            bytes_accessed=2 * 2 * frames * FFT_LEN * streams, transcendentals=0,
        ),
    )(chan_counts, voltages, jnp.asarray(analysis), jnp.asarray(mixing))


def in_order(refs, dest_ref, pre, total):
    if len(refs) == 2:
        for h, ref in enumerate(refs):
            sources, payload = ref.shape[0], ref.shape[1]
            tiles = payload // (2 * CAP)
            spread = NSPEC // tiles
            width = LANES // spread
            lane = lax.broadcasted_iota(jnp.int32, (payload, LANES), 1)
            for q in range(sources // spread):
                parts = [ref[spread * q + a].astype(jnp.float32) for a in range(spread)]
                groups = []
                for g in range(spread):
                    group = None
                    for a in range(spread):
                        moved = turn_lanes(parts[a], (a - g) * width)
                        group = moved if a == 0 else jnp.where(lane < a * width, group, moved)
                    groups.append(group)
                for part in range(2 * CAP):
                    rows = slice(part * tiles, (part + 1) * tiles)
                    both = jnp.concatenate([group[rows] for group in groups], axis=0)
                    pre[part, h * NSPEC : (h + 1) * NSPEC, q * LANES : (q + 1) * LANES] = (
                        both.astype(jnp.bfloat16)
                    )
    else:
        pre[...] = refs[0][...]
    parts, time_len, held = pre.shape
    spot = lax.broadcasted_iota(jnp.int32, (total, held), 0)
    turn = jnp.where(spot == dest_ref[...], 1.0, 0.0).astype(jnp.bfloat16)
    return lax.dot_general(
        pre[...].reshape(parts * time_len, held), turn, (((1,), (1,)), ((), ())),
        preferred_element_type=jnp.float32,
    )


def correlator(given, counts, where, dest_ref, *refs):
    out_ref, pre, post = refs[-3:]
    refs = refs[:-3]
    k = pl.program_id(0)
    time_len = pre.shape[1]

    @pl.when(k == 0)
    def _():
        ordered = in_order(refs[:given], dest_ref, pre, post.shape[2])
        for ref in refs[given:]:
            ordered = ordered + ref[...].astype(jnp.float32)
        post[...] = ordered.astype(jnp.bfloat16).reshape(post.shape)

    rows = out_ref.shape[3]
    every = post[k]
    near = post[k, :, pl.ds(pl.multiple_of(where[1] * rows, LANES), rows)]
    turned = jnp.concatenate([near[time_len:], -near[:time_len]], axis=0)
    valid = jnp.where(k < counts[where[0]], 1.0, 0.0) / jnp.float32(time_len)
    for part, left in enumerate((near, turned)):
        vis = lax.dot_general(
            left, every, (((0,), (0,)), ((), ())), preferred_element_type=jnp.float32
        )
        out_ref[0, 0, part] = (vis * valid).astype(jnp.bfloat16)


def orderer(dest_ref, *refs):
    out_ref, pre = refs[-2:]
    out_ref[...] = in_order(refs[:-2], dest_ref, pre, out_ref.shape[1]).astype(jnp.bfloat16)


def halves(own, other):
    sources, payload = own.shape[:2]
    spread = 2 * CAP * NSPEC // payload
    held = (2 * CAP, 2 * NSPEC, sources * LANES // spread)
    if spread <= 4:
        return [own, other], held
    both = jnp.stack([own, other]).reshape(2, sources, 2 * CAP, NSPEC // spread, spread, -1)
    return [both.transpose(2, 0, 3, 4, 1, 5).reshape(held)], held


def order(own, other, dest, total):
    operands, held = halves(own, other)
    return pl.pallas_call(
        orderer,
        out_shape=jax.ShapeDtypeStruct((held[0] * held[1], total), jnp.bfloat16),
        scratch_shapes=[pltpu.VMEM(held, jnp.bfloat16)],
        compiler_params=pltpu.CompilerParams(vmem_limit_bytes=60 * 1024 * 1024),
        cost_estimate=pl.CostEstimate(
            flops=2 * held[0] * held[1] * held[2] * total, bytes_accessed=4 * own.size,
            transcendentals=0,
        ),
    )(dest, *operands)


def correlate(own, other, dest, before, chan_counts, where, total):
    operands, held = halves(own, other)
    given = len(operands)
    operands = operands + before
    specs = [
        pl.BlockSpec(a.shape, functools.partial(lambda n, k, c, w: (0,) * n, a.ndim))
        for a in [dest] + operands
    ]
    rows = total // 2
    return pl.pallas_call(
        functools.partial(correlator, given),
        grid_spec=pltpu.PrefetchScalarGridSpec(
            num_scalar_prefetch=2,
            grid=(CAP,),
            in_specs=specs,
            out_specs=pl.BlockSpec((1, 1, 2, rows, total), lambda k, c, w: (0, k, 0, 0, 0)),
            scratch_shapes=[
                pltpu.VMEM(held, jnp.bfloat16),
                pltpu.VMEM((CAP, 4 * NSPEC, total), jnp.bfloat16),
            ],
        ),
        out_shape=jax.ShapeDtypeStruct((1, CAP, 2, rows, total), jnp.bfloat16),
        compiler_params=pltpu.CompilerParams(vmem_limit_bytes=60 * 1024 * 1024),
    )(chan_counts, where, dest, *operands)


def body(voltages, station_map, chan_counts):
    dests = lax.axis_size("stn")
    streams = voltages.shape[0]
    total = dests * streams
    plan = ((32, 4, True), (32, 4, False)) if streams == 64 else ((streams, 2, False),)
    dest = (2 * station_map[:, None] + jnp.arange(2, dtype=jnp.int32)[None, :]).reshape(dests, -1)
    where = jnp.stack([lax.axis_index("stn"), lax.axis_index("blk")]).astype(jnp.int32)
    start = 0
    before = []
    for size, step, turned_dot in plan:
        outgoing = channelize(voltages, chan_counts, dests, start, size, step, turned_dot)
        own = lax.all_to_all(outgoing, "stn", split_axis=0, concat_axis=0, tiled=True)
        other = lax.ppermute(own, "blk", [(0, 1), (1, 0)])
        place = dest[:, start : start + size].reshape(1, -1)
        start = start + size
        if start < streams:
            before.append(order(own, other, place, total))
    return correlate(own, other, place, before, chan_counts, where, total)


def solution(mesh):
    return jax.shard_map(
        body,
        mesh=mesh,
        in_specs=(P("stn", "blk", None, None, None), P(), P()),
        out_specs=P("stn", None, None, "blk", None),
        check_vma=False,
    )
```

```python
import functools
import math

import jax
import jax.numpy as jnp
import ml_dtypes
import numpy as np
from jax import lax
from jax.experimental import pallas as pl
from jax.experimental.pallas import tpu as pltpu
from jax.sharding import PartitionSpec as P

FFT_LEN = 4096
TAPS = 16
CAP = 3
NSPEC = 48
LANES = 128


def prototype():
    span = TAPS * FFT_LEN
    points = np.arange(span, dtype=np.float64) + 0.5
    window = 0.5 - 0.5 * np.cos(2.0 * math.pi * points / span)
    shifted = math.pi * (points - span / 2.0) / FFT_LEN
    filt = np.sin(shifted) / shifted * window
    return (filt / np.sqrt(np.sum(filt * filt))).reshape(TAPS, FFT_LEN)


def frame_basis(band, count):
    limit = math.pi * (band + 0.1)
    terms = count + int(limit) + 60
    k = np.arange(terms, dtype=np.float64)
    diagonal = k * (k + 1) + (2 * k * (k + 1) - 1) / ((2 * k + 3) * (2 * k - 1)) * limit**2
    m = k[:-2]
    beside = (m + 2) * (m + 1) / ((2 * m + 3) * np.sqrt((2 * m + 1) * (2 * m + 5))) * limit**2
    matrix = np.diag(diagonal) + np.diag(beside, 2) + np.diag(beside, -2)
    _, vectors = np.linalg.eigh(matrix)
    x = (2 * np.arange(FFT_LEN) + 1.0) / FFT_LEN - 1
    legendre = np.zeros((terms, FFT_LEN))
    legendre[0] = 1.0
    legendre[1] = x
    for j in range(2, terms):
        legendre[j] = ((2 * j - 1) * x * legendre[j - 1] - (j - 1) * legendre[j - 2]) / j
    legendre *= np.sqrt((k + 0.5) * 2.0 / FFT_LEN)[:, None]
    return legendre.T @ vectors[:, :count]


SHIFTS = 4


def turn_lanes(value, shift):
    shift = shift % LANES
    return pltpu.roll(value, shift, axis=1) if shift else value


def packing(band):
    if 3 * (2 * band + 21) <= 2 * LANES:
        return 2 * band + 21, 2 * LANES, True
    count = -(-(2 * band + 32) // (LANES // 2)) * (LANES // 2)
    return count, -(-2 * count // LANES) * LANES, False


@functools.lru_cache(maxsize=4)
def tables(band):
    bf16 = ml_dtypes.bfloat16
    count, packed, triple = packing(band)
    basis = frame_basis(band, count)
    high = basis.astype(bf16)
    low = (basis - high.astype(np.float64)).astype(bf16)
    held = high.astype(np.float64) + low.astype(np.float64)
    lanes = -(-count // LANES) * LANES
    analysis = np.zeros((FFT_LEN, 2 * lanes), bf16)
    analysis[:, :count] = high
    analysis[:, lanes : lanes + count] = low

    phase = 2.0 * math.pi / FFT_LEN * (np.outer(np.arange(FFT_LEN), np.arange(band)) % FFT_LEN)
    wave = np.concatenate([np.cos(phase), -np.sin(phase)], axis=1)
    gram = held.T @ held
    taper = prototype()
    mixing = np.zeros((TAPS // SHIFTS, 2, packed, SHIFTS, 2 * band), bf16)
    for t in range(TAPS):
        real = np.linalg.solve(gram, held.T @ (taper[t][:, None] * wave))
        imag = np.concatenate([-real[:, band:], real[:, :band]], axis=1)
        for c, full in enumerate((real, imag)):
            part = mixing[t // SHIFTS, c, :, t % SHIFTS]
            top = full.astype(bf16)
            part[:count] = top
            part[count : 2 * count] = top
            if triple:
                part[2 * count : 3 * count] = (full - top.astype(np.float64)).astype(bf16)
    return analysis, mixing.reshape(-1, SHIFTS * 2 * band)


def channelizer(
    band, dests, first, streams, step, queues, counts, v_ref, u_hbm, w_hbm, out_ref,
    held, u_ref, w_ref, y, p, x, turned, arrived,
):
    i = pl.program_id(0)
    ahead = held.shape[0]
    last = pl.num_programs(0) - 1
    count, packed, triple = packing(band)
    lanes = u_ref.shape[1] // 2
    rows = 2 * v_ref.shape[2]
    reach = NSPEC + 8
    wide = max(1, 2 * band // LANES)
    tables_in = [
        pltpu.make_async_copy(u_hbm, u_ref, arrived.at[ahead, 0]),
        pltpu.make_async_copy(w_hbm, w_ref, arrived.at[ahead, 1]),
    ]

    def fetch(block):
        slot = block % ahead
        return [
            pltpu.make_async_copy(
                v_ref.at[first + block * step + r, 0], held.at[slot, r], arrived.at[slot, r]
            )
            for r in range(step)
        ]

    def begin(block):
        for r, copy in enumerate(fetch(block)):
            copy.start(priority=r % queues)

    def analyse():
        signal = held[i % ahead].reshape(step * rows, FFT_LEN)
        coeff = jnp.dot(signal, u_ref[...], preferred_element_type=jnp.float32)
        coeff = coeff[:, :lanes] + coeff[:, lanes:]
        high = coeff.astype(jnp.bfloat16).astype(jnp.float32)
        low = coeff - high
        if triple:
            lane = lax.broadcasted_iota(jnp.int32, coeff.shape, 1)
            low = turn_lanes(low, count)
            spare = 2 * count - LANES
            y[0, : step * rows] = jnp.where(lane < count, high, low)
            y[1, : step * rows] = jnp.where(lane < spare, low, turn_lanes(high, spare))
        else:
            both = jnp.concatenate([high[:, :count], low[:, :count]], axis=1)
            for n in range(packed // LANES):
                y[n, : step * rows] = both[:, n * LANES : (n + 1) * LANES]

    def mix(block):
        taps = []
        for r in range(step):
            taps.append(jnp.concatenate([
                y[n, pl.ds(r * rows + 2 * SHIFTS * m + c, reach, stride=2), :]
                for m in range(TAPS // SHIFTS) for c in range(2) for n in range(packed // LANES)
            ], axis=1))
        taps = jnp.concatenate(taps, axis=0).astype(jnp.bfloat16)
        mixed = jnp.dot(taps, w_ref[...], preferred_element_type=jnp.float32)
        for n in range(mixed.shape[1] // LANES):
            p[n] = mixed[:, n * LANES : (n + 1) * LANES]
        for r in range(step):
            place = pl.ds(block * step + r, NSPEC, stride=streams)
            if 2 * band >= LANES:
                for n in range(wide):
                    x[n, place, :] = sum(
                        p[wide * h + n, pl.ds(r * reach + h, NSPEC), :] for h in range(SHIFTS)
                    )
            else:
                per = LANES // (2 * band)
                lane = lax.broadcasted_iota(jnp.int32, (NSPEC, LANES), 1)
                total = None
                for u in reversed(range(per)):
                    part = sum(
                        p[b, pl.ds(r * reach + b * per + u, NSPEC), :] for b in range(SHIFTS // per)
                    )
                    total = part if total is None else jnp.where(
                        lane < 2 * band * (u + 1), part, total
                    )
                whole = total
                for u in range(1, per):
                    whole = whole + turn_lanes(total, -2 * band * u)
                x[0, place, :] = whole

    @pl.when(i == 0)
    def _():
        begin(0)
        for copy in tables_in:
            copy.start()
        for block in range(1, min(ahead - 1, streams // step)):
            begin(block)

    @pl.when(i + ahead - 1 < last)
    def _():
        begin(i + ahead - 1)

    @pl.when(i == 0)
    def _():
        for copy in tables_in:
            copy.wait()

    @pl.when(i < last)
    def _():
        for copy in fetch(i):
            copy.wait()
        mix(jnp.maximum(i - 1, 0))
        analyse()

    @pl.when(i == last)
    def _():
        mix(i - 1)
        lane = lax.broadcasted_iota(jnp.int32, (8, wide * LANES), 1)
        row = lax.broadcasted_iota(jnp.int32, (8, wide * LANES), 0)
        slot = row // 2
        base = (row % 2) * band
        picks = []
        offset = jnp.int32(0)
        for d in range(dests):
            held = counts[d]
            want = offset + jnp.minimum(slot, held - 1) + base
            picks.append(jnp.where((lane == want) & (row < 2 * CAP), 1.0, 0.0))
            offset = offset + held
        pick = jnp.concatenate(picks, axis=0).astype(jnp.bfloat16)
        spectra = jnp.concatenate([x[n] for n in range(wide)], axis=1)
        out = lax.dot_general(
            pick, spectra.astype(jnp.bfloat16), (((1,), (1,)), ((), ())),
            preferred_element_type=jnp.float32,
        )
        tiles = NSPEC * streams // LANES
        for d in range(dests):
            for t in range(tiles):
                turned[d, pl.ds(t, 2 * CAP, stride=tiles), :] = out[
                    8 * d : 8 * d + 2 * CAP, t * LANES : (t + 1) * LANES
                ]
        out_ref[...] = turned[...].astype(jnp.bfloat16)


def channelize(voltages, chan_counts, dests, start, streams, step, queues):
    band = 2 * dests
    frames = voltages.shape[2]
    analysis, mixing = tables(band)
    packed = packing(band)[1]
    ahead = 4 if band <= 64 else 2
    payload = 2 * CAP * NSPEC * streams // LANES
    steps = streams // step
    kernel = functools.partial(channelizer, band, dests, start, streams, step, queues)
    return pl.pallas_call(
        kernel,
        grid_spec=pltpu.PrefetchScalarGridSpec(
            num_scalar_prefetch=1,
            grid=(steps + 1,),
            in_specs=[pl.BlockSpec(memory_space=pl.ANY)] * 3,
            out_specs=pl.BlockSpec((dests, payload, LANES), lambda i, c: (0, 0, 0)),
            scratch_shapes=[
                pltpu.VMEM((ahead, step, frames, 2, FFT_LEN), jnp.bfloat16),
                pltpu.VMEM(analysis.shape, jnp.bfloat16),
                pltpu.VMEM(mixing.shape, jnp.bfloat16),
                pltpu.VMEM((packed // LANES, step * 2 * frames + 16, LANES), jnp.float32),
                pltpu.VMEM((SHIFTS * 2 * band // LANES, step * (NSPEC + 8), LANES), jnp.float32),
                pltpu.VMEM((max(1, 2 * band // LANES), NSPEC * streams, LANES), jnp.float32),
                pltpu.VMEM((dests, payload, LANES), jnp.float32),
                pltpu.SemaphoreType.DMA((ahead + 1, step)),
            ],
        ),
        out_shape=jax.ShapeDtypeStruct((dests, payload, LANES), jnp.bfloat16),
        compiler_params=pltpu.CompilerParams(vmem_limit_bytes=60 * 1024 * 1024),
        cost_estimate=pl.CostEstimate(
            flops=2 * streams * 2 * frames * analysis.size,
            bytes_accessed=2 * 2 * frames * FFT_LEN * streams, transcendentals=0,
        ),
    )(chan_counts, voltages, jnp.asarray(analysis), jnp.asarray(mixing))


def in_order(refs, dest_ref, pre, total):
    if len(refs) == 2:
        for h, ref in enumerate(refs):
            sources, payload = ref.shape[0], ref.shape[1]
            tiles = payload // (2 * CAP)
            spread = NSPEC // tiles
            width = LANES // spread
            lane = lax.broadcasted_iota(jnp.int32, (payload, LANES), 1)
            for q in range(sources // spread):
                parts = [ref[spread * q + a].astype(jnp.float32) for a in range(spread)]
                groups = []
                for g in range(spread):
                    group = None
                    for a in range(spread):
                        moved = turn_lanes(parts[a], (a - g) * width)
                        group = moved if a == 0 else jnp.where(lane < a * width, group, moved)
                    groups.append(group)
                for part in range(2 * CAP):
                    rows = slice(part * tiles, (part + 1) * tiles)
                    both = jnp.concatenate([group[rows] for group in groups], axis=0)
                    pre[part, h * NSPEC : (h + 1) * NSPEC, q * LANES : (q + 1) * LANES] = (
                        both.astype(jnp.bfloat16)
                    )
    else:
        pre[...] = refs[0][...]
    parts, time_len, held = pre.shape
    spot = lax.broadcasted_iota(jnp.int32, (total, held), 0)
    turn = jnp.where(spot == dest_ref[...], 1.0, 0.0).astype(jnp.bfloat16)
    return lax.dot_general(
        pre[...].reshape(parts * time_len, held), turn, (((1,), (1,)), ((), ())),
        preferred_element_type=jnp.float32,
    )


def correlator(given, counts, where, dest_ref, *refs):
    out_ref, pre, post = refs[-3:]
    refs = refs[:-3]
    k = pl.program_id(0)
    time_len = pre.shape[1]

    @pl.when(k == 0)
    def _():
        ordered = in_order(refs[:given], dest_ref, pre, post.shape[2])
        for ref in refs[given:]:
            ordered = ordered + ref[...].astype(jnp.float32)
        post[...] = ordered.astype(jnp.bfloat16).reshape(post.shape)

    rows = out_ref.shape[3]
    every = post[k]
    near = post[k, :, pl.ds(pl.multiple_of(where[1] * rows, LANES), rows)]
    turned = jnp.concatenate([near[time_len:], -near[:time_len]], axis=0)
    valid = jnp.where(k < counts[where[0]], 1.0, 0.0) / jnp.float32(time_len)
    for part, left in enumerate((near, turned)):
        vis = lax.dot_general(
            left, every, (((0,), (0,)), ((), ())), preferred_element_type=jnp.float32
        )
        out_ref[0, 0, part] = (vis * valid).astype(jnp.bfloat16)


def orderer(dest_ref, *refs):
    out_ref, pre = refs[-2:]
    out_ref[...] = in_order(refs[:-2], dest_ref, pre, out_ref.shape[1]).astype(jnp.bfloat16)


def halves(own, other):
    sources, payload = own.shape[:2]
    spread = 2 * CAP * NSPEC // payload
    held = (2 * CAP, 2 * NSPEC, sources * LANES // spread)
    if spread <= 4:
        return [own, other], held
    both = jnp.stack([own, other]).reshape(2, sources, 2 * CAP, NSPEC // spread, spread, -1)
    return [both.transpose(2, 0, 3, 4, 1, 5).reshape(held)], held


def order(own, other, dest, total):
    operands, held = halves(own, other)
    return pl.pallas_call(
        orderer,
        out_shape=jax.ShapeDtypeStruct((held[0] * held[1], total), jnp.bfloat16),
        scratch_shapes=[pltpu.VMEM(held, jnp.bfloat16)],
        compiler_params=pltpu.CompilerParams(vmem_limit_bytes=60 * 1024 * 1024),
        cost_estimate=pl.CostEstimate(
            flops=2 * held[0] * held[1] * held[2] * total, bytes_accessed=4 * own.size,
            transcendentals=0,
        ),
    )(dest, *operands)


def correlate(own, other, dest, before, chan_counts, where, total):
    operands, held = halves(own, other)
    given = len(operands)
    operands = operands + before
    specs = [
        pl.BlockSpec(a.shape, functools.partial(lambda n, k, c, w: (0,) * n, a.ndim))
        for a in [dest] + operands
    ]
    rows = total // 2
    return pl.pallas_call(
        functools.partial(correlator, given),
        grid_spec=pltpu.PrefetchScalarGridSpec(
            num_scalar_prefetch=2,
            grid=(CAP,),
            in_specs=specs,
            out_specs=pl.BlockSpec((1, 1, 2, rows, total), lambda k, c, w: (0, k, 0, 0, 0)),
            scratch_shapes=[
                pltpu.VMEM(held, jnp.bfloat16),
                pltpu.VMEM((CAP, 4 * NSPEC, total), jnp.bfloat16),
            ],
        ),
        out_shape=jax.ShapeDtypeStruct((1, CAP, 2, rows, total), jnp.bfloat16),
        compiler_params=pltpu.CompilerParams(vmem_limit_bytes=60 * 1024 * 1024),
    )(chan_counts, where, dest, *operands)


def body(voltages, station_map, chan_counts):
    dests = lax.axis_size("stn")
    streams = voltages.shape[0]
    total = dests * streams
    plan = ((32, 4, 1), (32, 4, 2)) if streams == 64 else ((streams, 2, 1),)
    dest = (2 * station_map[:, None] + jnp.arange(2, dtype=jnp.int32)[None, :]).reshape(dests, -1)
    where = jnp.stack([lax.axis_index("stn"), lax.axis_index("blk")]).astype(jnp.int32)
    start = 0
    before = []
    for size, step, queues in plan:
        outgoing = channelize(voltages, chan_counts, dests, start, size, step, queues)
        own = lax.all_to_all(outgoing, "stn", split_axis=0, concat_axis=0, tiled=True)
        other = lax.ppermute(own, "blk", [(0, 1), (1, 0)])
        place = dest[:, start : start + size].reshape(1, -1)
        start = start + size
        if start < streams:
            before.append(order(own, other, place, total))
    return correlate(own, other, place, before, chan_counts, where, total)


def solution(mesh):
    return jax.shard_map(
        body,
        mesh=mesh,
        in_specs=(P("stn", "blk", None, None, None), P(), P()),
        out_specs=P("stn", None, None, "blk", None),
        check_vma=False,
    )
```

```python
import functools
import math

import jax
import jax.numpy as jnp
import ml_dtypes
import numpy as np
from jax import lax
from jax.experimental import pallas as pl
from jax.experimental.pallas import tpu as pltpu
from jax.sharding import PartitionSpec as P

FFT_LEN = 4096
TAPS = 16
CAP = 3
NSPEC = 48
LANES = 128


def prototype():
    span = TAPS * FFT_LEN
    points = np.arange(span, dtype=np.float64) + 0.5
    window = 0.5 - 0.5 * np.cos(2.0 * math.pi * points / span)
    shifted = math.pi * (points - span / 2.0) / FFT_LEN
    filt = np.sin(shifted) / shifted * window
    return (filt / np.sqrt(np.sum(filt * filt))).reshape(TAPS, FFT_LEN)


def frame_basis(band, count):
    limit = math.pi * (band + 0.1)
    terms = count + int(limit) + 60
    k = np.arange(terms, dtype=np.float64)
    diagonal = k * (k + 1) + (2 * k * (k + 1) - 1) / ((2 * k + 3) * (2 * k - 1)) * limit**2
    m = k[:-2]
    beside = (m + 2) * (m + 1) / ((2 * m + 3) * np.sqrt((2 * m + 1) * (2 * m + 5))) * limit**2
    matrix = np.diag(diagonal) + np.diag(beside, 2) + np.diag(beside, -2)
    _, vectors = np.linalg.eigh(matrix)
    x = (2 * np.arange(FFT_LEN) + 1.0) / FFT_LEN - 1
    legendre = np.zeros((terms, FFT_LEN))
    legendre[0] = 1.0
    legendre[1] = x
    for j in range(2, terms):
        legendre[j] = ((2 * j - 1) * x * legendre[j - 1] - (j - 1) * legendre[j - 2]) / j
    legendre *= np.sqrt((k + 0.5) * 2.0 / FFT_LEN)[:, None]
    return legendre.T @ vectors[:, :count]


def turn_lanes(value, shift):
    shift = shift % LANES
    return pltpu.roll(value, shift, axis=1) if shift else value


def packing(band):
    if 3 * (2 * band + 16) <= 2 * LANES:
        return 2 * band + 16, 2 * LANES, True
    count = -(-(2 * band + 32) // (LANES // 2)) * (LANES // 2)
    return count, -(-2 * count // LANES) * LANES, False


@functools.lru_cache(maxsize=4)
def tables(band, shifts):
    bf16 = ml_dtypes.bfloat16
    count, packed, triple = packing(band)
    basis = frame_basis(band, count)
    high = basis.astype(bf16)
    low = (basis - high.astype(np.float64)).astype(bf16)
    held = high.astype(np.float64) + low.astype(np.float64)
    analysis = np.ascontiguousarray(np.concatenate([high, low], axis=1).T)

    phase = 2.0 * math.pi / FFT_LEN * (np.outer(np.arange(FFT_LEN), np.arange(band)) % FFT_LEN)
    wave = np.concatenate([np.cos(phase), -np.sin(phase)], axis=1)
    gram = held.T @ held
    taper = prototype()
    mixing = np.zeros((TAPS // shifts, 2, packed, shifts, 2 * band), bf16)
    for t in range(TAPS):
        real = np.linalg.solve(gram, held.T @ (taper[t][:, None] * wave))
        imag = np.concatenate([-real[:, band:], real[:, :band]], axis=1)
        for c, full in enumerate((real, imag)):
            part = mixing[t // shifts, c, :, t % shifts]
            top = full.astype(bf16)
            part[:count] = top
            part[count : 2 * count] = top
            if triple:
                part[2 * count : 3 * count] = (full - top.astype(np.float64)).astype(bf16)
    return analysis, mixing.reshape(-1, shifts * 2 * band)


def channelizer(
    band, dests, first, streams, step, shifts, counts, v_ref, u_hbm, w_hbm, out_ref,
    held, u_ref, w_ref, y, p, x, turned, arrived,
):
    i = pl.program_id(0)
    ahead = held.shape[0]
    last = pl.num_programs(0) - 1
    count, packed, triple = packing(band)
    rows = 2 * v_ref.shape[2]
    reach = NSPEC + 8
    wide = max(1, 2 * band // LANES)
    tables_in = [
        pltpu.make_async_copy(u_hbm, u_ref, arrived.at[ahead, 0]),
        pltpu.make_async_copy(w_hbm, w_ref, arrived.at[ahead, 1]),
    ]

    def fetch(block):
        slot = block % ahead
        return [
            pltpu.make_async_copy(
                v_ref.at[first + block * step + r, 0], held.at[slot, r], arrived.at[slot, r]
            )
            for r in range(step)
        ]

    def begin(block):
        for r, copy in enumerate(fetch(block)):
            copy.start(priority=r % 2)

    def analyse():
        signal = held[i % ahead].reshape(step * rows, FFT_LEN)
        coeff = lax.dot_general(
            u_ref[...], signal, (((1,), (1,)), ((), ())), preferred_element_type=jnp.float32
        )
        coeff = coeff[:count] + coeff[count:]
        if triple:
            coeff = jnp.concatenate(
                [coeff, jnp.zeros((LANES - count, step * rows), jnp.float32)], axis=0
            )
        coeff = coeff.T
        high = coeff.astype(jnp.bfloat16).astype(jnp.float32)
        low = coeff - high
        if triple:
            lane = lax.broadcasted_iota(jnp.int32, coeff.shape, 1)
            low = turn_lanes(low, count)
            spare = 2 * count - LANES
            y[0, : step * rows] = jnp.where(lane < count, high, low)
            y[1, : step * rows] = jnp.where(lane < spare, low, turn_lanes(high, spare))
        else:
            both = jnp.concatenate([high, low], axis=1)
            for n in range(packed // LANES):
                y[n, : step * rows] = both[:, n * LANES : (n + 1) * LANES]

    def mix(block):
        taps = []
        for r in range(step):
            taps.append(jnp.concatenate([
                y[n, pl.ds(r * rows + 2 * shifts * m + c, reach, stride=2), :]
                for m in range(TAPS // shifts) for c in range(2) for n in range(packed // LANES)
            ], axis=1))
        taps = jnp.concatenate(taps, axis=0).astype(jnp.bfloat16)
        mixed = jnp.dot(taps, w_ref[...], preferred_element_type=jnp.float32)
        for n in range(mixed.shape[1] // LANES):
            p[n] = mixed[:, n * LANES : (n + 1) * LANES]
        for r in range(step):
            place = pl.ds(block * step + r, NSPEC, stride=streams)
            if 2 * band >= LANES:
                for n in range(wide):
                    x[n, place, :] = sum(
                        p[wide * h + n, pl.ds(r * reach + h, NSPEC), :] for h in range(shifts)
                    )
            else:
                per = LANES // (2 * band)
                lane = lax.broadcasted_iota(jnp.int32, (NSPEC, LANES), 1)
                total = None
                for u in reversed(range(per)):
                    part = sum(
                        p[b, pl.ds(r * reach + b * per + u, NSPEC), :] for b in range(shifts // per)
                    )
                    total = part if total is None else jnp.where(
                        lane < 2 * band * (u + 1), part, total
                    )
                whole = total
                for u in range(1, per):
                    whole = whole + turn_lanes(total, -2 * band * u)
                x[0, place, :] = whole

    @pl.when(i == 0)
    def _():
        begin(0)
        for copy in tables_in:
            copy.start()
        for copy in tables_in:
            copy.wait()

    @pl.when(i < last)
    def _():
        for copy in fetch(i):
            copy.wait()

    @pl.when(i == 0)
    def _():
        for block in range(1, min(ahead - 1, streams // step)):
            begin(block)

    @pl.when(i + ahead - 1 < last)
    def _():
        begin(i + ahead - 1)

    @pl.when(i < last)
    def _():
        mix(jnp.maximum(i - 1, 0))
        analyse()

    @pl.when(i == last)
    def _():
        mix(i - 1)
        lane = lax.broadcasted_iota(jnp.int32, (8, wide * LANES), 1)
        row = lax.broadcasted_iota(jnp.int32, (8, wide * LANES), 0)
        slot = row // 2
        base = (row % 2) * band
        picks = []
        offset = jnp.int32(0)
        for d in range(dests):
            held = counts[d]
            want = offset + jnp.minimum(slot, held - 1) + base
            picks.append(jnp.where((lane == want) & (row < 2 * CAP), 1.0, 0.0))
            offset = offset + held
        pick = jnp.concatenate(picks, axis=0).astype(jnp.bfloat16)
        spectra = jnp.concatenate([x[n] for n in range(wide)], axis=1)
        out = lax.dot_general(
            pick, spectra.astype(jnp.bfloat16), (((1,), (1,)), ((), ())),
            preferred_element_type=jnp.float32,
        )
        tiles = NSPEC * streams // LANES
        for d in range(dests):
            for t in range(tiles):
                turned[d, pl.ds(t, 2 * CAP, stride=tiles), :] = out[
                    8 * d : 8 * d + 2 * CAP, t * LANES : (t + 1) * LANES
                ]
        out_ref[...] = turned[...].astype(jnp.bfloat16)


def channelize(voltages, chan_counts, dests, start, streams, step, shifts):
    band = 2 * dests
    frames = voltages.shape[2]
    analysis, mixing = tables(band, shifts)
    packed = packing(band)[1]
    ahead = 4 if band <= 64 else 2
    payload = 2 * CAP * NSPEC * streams // LANES
    steps = streams // step
    kernel = functools.partial(channelizer, band, dests, start, streams, step, shifts)
    return pl.pallas_call(
        kernel,
        grid_spec=pltpu.PrefetchScalarGridSpec(
            num_scalar_prefetch=1,
            grid=(steps + 1,),
            in_specs=[pl.BlockSpec(memory_space=pl.ANY)] * 3,
            out_specs=pl.BlockSpec((dests, payload, LANES), lambda i, c: (0, 0, 0)),
            scratch_shapes=[
                pltpu.VMEM((ahead, step, frames, 2, FFT_LEN), jnp.bfloat16),
                pltpu.VMEM(analysis.shape, jnp.bfloat16),
                pltpu.VMEM(mixing.shape, jnp.bfloat16),
                pltpu.VMEM((packed // LANES, step * 2 * frames + 16, LANES), jnp.float32),
                pltpu.VMEM((shifts * 2 * band // LANES, step * (NSPEC + 8), LANES), jnp.float32),
                pltpu.VMEM((max(1, 2 * band // LANES), NSPEC * streams, LANES), jnp.float32),
                pltpu.VMEM((dests, payload, LANES), jnp.float32),
                pltpu.SemaphoreType.DMA((ahead + 1, step)),
            ],
        ),
        out_shape=jax.ShapeDtypeStruct((dests, payload, LANES), jnp.bfloat16),
        compiler_params=pltpu.CompilerParams(vmem_limit_bytes=60 * 1024 * 1024),
        cost_estimate=pl.CostEstimate(
            flops=2 * streams * 2 * frames * analysis.size,
            bytes_accessed=2 * 2 * frames * FFT_LEN * streams, transcendentals=0,
        ),
    )(chan_counts, voltages, jnp.asarray(analysis), jnp.asarray(mixing))


def in_order(refs, dest_ref, pre, total):
    if len(refs) == 2:
        for h, ref in enumerate(refs):
            sources, payload = ref.shape[0], ref.shape[1]
            tiles = payload // (2 * CAP)
            spread = NSPEC // tiles
            width = LANES // spread
            lane = lax.broadcasted_iota(jnp.int32, (payload, LANES), 1)
            for q in range(sources // spread):
                parts = [ref[spread * q + a].astype(jnp.float32) for a in range(spread)]
                groups = []
                for g in range(spread):
                    group = None
                    for a in range(spread):
                        moved = turn_lanes(parts[a], (a - g) * width)
                        group = moved if a == 0 else jnp.where(lane < a * width, group, moved)
                    groups.append(group)
                for part in range(2 * CAP):
                    rows = slice(part * tiles, (part + 1) * tiles)
                    both = jnp.concatenate([group[rows] for group in groups], axis=0)
                    pre[part, h * NSPEC : (h + 1) * NSPEC, q * LANES : (q + 1) * LANES] = (
                        both.astype(jnp.bfloat16)
                    )
    else:
        pre[...] = refs[0][...]
    parts, time_len, held = pre.shape
    spot = lax.broadcasted_iota(jnp.int32, (total, held), 0)
    turn = jnp.where(spot == dest_ref[...], 1.0, 0.0).astype(jnp.bfloat16)
    return lax.dot_general(
        pre[...].reshape(parts * time_len, held), turn, (((1,), (1,)), ((), ())),
        preferred_element_type=jnp.float32,
    )


def correlator(given, counts, where, dest_ref, *refs):
    out_ref, pre, post = refs[-3:]
    refs = refs[:-3]
    k = pl.program_id(0)
    time_len = pre.shape[1]

    @pl.when(k == 0)
    def _():
        ordered = in_order(refs[:given], dest_ref, pre, post.shape[2])
        for ref in refs[given:]:
            ordered = ordered + ref[...].astype(jnp.float32)
        post[...] = ordered.astype(jnp.bfloat16).reshape(post.shape)

    rows = out_ref.shape[3]
    every = post[k]
    near = post[k, :, pl.ds(pl.multiple_of(where[1] * rows, LANES), rows)]
    turned = jnp.concatenate([near[time_len:], -near[:time_len]], axis=0)
    valid = jnp.where(k < counts[where[0]], 1.0, 0.0) / jnp.float32(time_len)
    for part, left in enumerate((near, turned)):
        vis = lax.dot_general(
            left, every, (((0,), (0,)), ((), ())), preferred_element_type=jnp.float32
        )
        out_ref[0, 0, part] = (vis * valid).astype(jnp.bfloat16)


def orderer(dest_ref, *refs):
    out_ref, pre = refs[-2:]
    out_ref[...] = in_order(refs[:-2], dest_ref, pre, out_ref.shape[1]).astype(jnp.bfloat16)


def halves(own, other):
    sources, payload = own.shape[:2]
    spread = 2 * CAP * NSPEC // payload
    held = (2 * CAP, 2 * NSPEC, sources * LANES // spread)
    if spread <= 4:
        return [own, other], held
    both = jnp.stack([own, other]).reshape(2, sources, 2 * CAP, NSPEC // spread, spread, -1)
    return [both.transpose(2, 0, 3, 4, 1, 5).reshape(held)], held


def order(own, other, dest, total):
    operands, held = halves(own, other)
    return pl.pallas_call(
        orderer,
        out_shape=jax.ShapeDtypeStruct((held[0] * held[1], total), jnp.bfloat16),
        scratch_shapes=[pltpu.VMEM(held, jnp.bfloat16)],
        compiler_params=pltpu.CompilerParams(vmem_limit_bytes=60 * 1024 * 1024),
        cost_estimate=pl.CostEstimate(
            flops=2 * held[0] * held[1] * held[2] * total, bytes_accessed=4 * own.size,
            transcendentals=0,
        ),
    )(dest, *operands)


def correlate(own, other, dest, before, chan_counts, where, total):
    operands, held = halves(own, other)
    given = len(operands)
    operands = operands + before
    specs = [
        pl.BlockSpec(a.shape, functools.partial(lambda n, k, c, w: (0,) * n, a.ndim))
        for a in [dest] + operands
    ]
    rows = total // 2
    return pl.pallas_call(
        functools.partial(correlator, given),
        grid_spec=pltpu.PrefetchScalarGridSpec(
            num_scalar_prefetch=2,
            grid=(CAP,),
            in_specs=specs,
            out_specs=pl.BlockSpec((1, 1, 2, rows, total), lambda k, c, w: (0, k, 0, 0, 0)),
            scratch_shapes=[
                pltpu.VMEM(held, jnp.bfloat16),
                pltpu.VMEM((CAP, 4 * NSPEC, total), jnp.bfloat16),
            ],
        ),
        out_shape=jax.ShapeDtypeStruct((1, CAP, 2, rows, total), jnp.bfloat16),
        compiler_params=pltpu.CompilerParams(vmem_limit_bytes=60 * 1024 * 1024),
    )(chan_counts, where, dest, *operands)


def body(voltages, station_map, chan_counts):
    dests = lax.axis_size("stn")
    streams = voltages.shape[0]
    total = dests * streams
    plan = ((32, 4, 4), (32, 4, 8)) if streams == 64 else ((streams, 2, 4),)
    dest = (2 * station_map[:, None] + jnp.arange(2, dtype=jnp.int32)[None, :]).reshape(dests, -1)
    where = jnp.stack([lax.axis_index("stn"), lax.axis_index("blk")]).astype(jnp.int32)
    start = 0
    before = []
    for size, step, shifts in plan:
        outgoing = channelize(voltages, chan_counts, dests, start, size, step, shifts)
        own = lax.all_to_all(outgoing, "stn", split_axis=0, concat_axis=0, tiled=True)
        other = lax.ppermute(own, "blk", [(0, 1), (1, 0)])
        place = dest[:, start : start + size].reshape(1, -1)
        start = start + size
        if start < streams:
            before.append(order(own, other, place, total))
    return correlate(own, other, place, before, chan_counts, where, total)


def solution(mesh):
    return jax.shard_map(
        body,
        mesh=mesh,
        in_specs=(P("stn", "blk", None, None, None), P(), P()),
        out_specs=P("stn", None, None, "blk", None),
        check_vma=False,
    )
```

```python
import functools
import math

import jax
import jax.numpy as jnp
import ml_dtypes
import numpy as np
from jax import lax
from jax.experimental import pallas as pl
from jax.experimental.pallas import tpu as pltpu
from jax.sharding import PartitionSpec as P

FFT_LEN = 4096
TAPS = 16
CAP = 3
NSPEC = 48
LANES = 128


def prototype():
    span = TAPS * FFT_LEN
    points = np.arange(span, dtype=np.float64) + 0.5
    window = 0.5 - 0.5 * np.cos(2.0 * math.pi * points / span)
    shifted = math.pi * (points - span / 2.0) / FFT_LEN
    filt = np.sin(shifted) / shifted * window
    return (filt / np.sqrt(np.sum(filt * filt))).reshape(TAPS, FFT_LEN)


def frame_basis(band, count):
    limit = math.pi * (band + 0.1)
    terms = count + int(limit) + 60
    k = np.arange(terms, dtype=np.float64)
    diagonal = k * (k + 1) + (2 * k * (k + 1) - 1) / ((2 * k + 3) * (2 * k - 1)) * limit**2
    m = k[:-2]
    beside = (m + 2) * (m + 1) / ((2 * m + 3) * np.sqrt((2 * m + 1) * (2 * m + 5))) * limit**2
    matrix = np.diag(diagonal) + np.diag(beside, 2) + np.diag(beside, -2)
    _, vectors = np.linalg.eigh(matrix)
    x = (2 * np.arange(FFT_LEN) + 1.0) / FFT_LEN - 1
    legendre = np.zeros((terms, FFT_LEN))
    legendre[0] = 1.0
    legendre[1] = x
    for j in range(2, terms):
        legendre[j] = ((2 * j - 1) * x * legendre[j - 1] - (j - 1) * legendre[j - 2]) / j
    legendre *= np.sqrt((k + 0.5) * 2.0 / FFT_LEN)[:, None]
    return legendre.T @ vectors[:, :count]


def shifts_of(band):
    return 8 if band <= 64 else 4


def turn_lanes(value, shift):
    shift = shift % LANES
    return pltpu.roll(value, shift, axis=1) if shift else value


def packing(band):
    if 3 * (2 * band + 16) <= 2 * LANES:
        return 2 * band + 16, 2 * LANES, True
    count = -(-(2 * band + 32) // (LANES // 2)) * (LANES // 2)
    return count, -(-2 * count // LANES) * LANES, False


@functools.lru_cache(maxsize=4)
def tables(band):
    bf16 = ml_dtypes.bfloat16
    count, packed, triple = packing(band)
    shifts = shifts_of(band)
    basis = frame_basis(band, count)
    high = basis.astype(bf16)
    low = (basis - high.astype(np.float64)).astype(bf16)
    held = high.astype(np.float64) + low.astype(np.float64)
    lanes = -(-count // LANES) * LANES
    analysis = np.zeros((FFT_LEN, 2 * lanes), bf16)
    analysis[:, :count] = high
    analysis[:, lanes : lanes + count] = low

    phase = 2.0 * math.pi / FFT_LEN * (np.outer(np.arange(FFT_LEN), np.arange(band)) % FFT_LEN)
    wave = np.concatenate([np.cos(phase), -np.sin(phase)], axis=1)
    gram = held.T @ held
    taper = prototype()
    mixing = np.zeros((TAPS // shifts, 2, packed, shifts, 2 * band), bf16)
    for t in range(TAPS):
        real = np.linalg.solve(gram, held.T @ (taper[t][:, None] * wave))
        imag = np.concatenate([-real[:, band:], real[:, :band]], axis=1)
        for c, full in enumerate((real, imag)):
            part = mixing[t // shifts, c, :, t % shifts]
            top = full.astype(bf16)
            part[:count] = top
            part[count : 2 * count] = top
            if triple:
                part[2 * count : 3 * count] = (full - top.astype(np.float64)).astype(bf16)
    return analysis, mixing.reshape(-1, shifts * 2 * band)


def channelizer(
    band, dests, first, streams, step, unit, counts, v_ref, u_hbm, w_hbm, out_ref,
    held, u_ref, w_ref, y, p, x, turned, arrived,
):
    i = pl.program_id(0)
    ahead = held.shape[0]
    shifts = shifts_of(band)
    last = pl.num_programs(0) - 1
    count, packed, triple = packing(band)
    lanes = u_ref.shape[1] // 2
    rows = 2 * v_ref.shape[2]
    reach = NSPEC + 8
    wide = max(1, 2 * band // LANES)
    tables_in = [
        pltpu.make_async_copy(u_hbm, u_ref, arrived.at[ahead, 0]),
        pltpu.make_async_copy(w_hbm, w_ref, arrived.at[ahead, 1]),
    ]

    def fetch(block):
        slot = block % ahead
        return [
            pltpu.make_async_copy(
                v_ref.at[first + block * step + r, 0], held.at[slot, r], arrived.at[slot, r]
            )
            for r in range(step)
        ]

    def begin(block):
        for r, copy in enumerate(fetch(block)):
            copy.start(priority=r % 2)

    def analyse():
        signal = held[i % ahead].reshape(step * rows, FFT_LEN)
        coeff = jnp.dot(signal, u_ref[...], preferred_element_type=jnp.float32)
        coeff = coeff[:, :lanes] + coeff[:, lanes:]
        high = coeff.astype(jnp.bfloat16).astype(jnp.float32)
        low = coeff - high
        if triple:
            lane = lax.broadcasted_iota(jnp.int32, coeff.shape, 1)
            low = turn_lanes(low, count)
            spare = 2 * count - LANES
            y[0, : step * rows] = jnp.where(lane < count, high, low)
            y[1, : step * rows] = jnp.where(lane < spare, low, turn_lanes(high, spare))
        else:
            both = jnp.concatenate([high[:, :count], low[:, :count]], axis=1)
            for n in range(packed // LANES):
                y[n, : step * rows] = both[:, n * LANES : (n + 1) * LANES]

    def mix(block):
        taps = []
        for r in range(step):
            taps.append(jnp.concatenate([
                y[n, pl.ds(r * rows + 2 * shifts * m + c, reach, stride=2), :]
                for m in range(TAPS // shifts) for c in range(2) for n in range(packed // LANES)
            ], axis=1))
        taps = jnp.concatenate(taps, axis=0).astype(jnp.bfloat16)
        mixed = jnp.dot(taps, w_ref[...], preferred_element_type=jnp.float32)
        for n in range(mixed.shape[1] // LANES):
            p[n] = mixed[:, n * LANES : (n + 1) * LANES]
        for r in range(step):
            stream = block * step + r
            place = pl.ds(stream // unit * (NSPEC * unit) + stream % unit, NSPEC, stride=unit)
            if 2 * band >= LANES:
                for n in range(wide):
                    x[n, place, :] = sum(
                        p[wide * h + n, pl.ds(r * reach + h, NSPEC), :] for h in range(shifts)
                    )
            else:
                per = LANES // (2 * band)
                lane = lax.broadcasted_iota(jnp.int32, (NSPEC, LANES), 1)
                total = None
                for u in reversed(range(per)):
                    part = sum(
                        p[b, pl.ds(r * reach + b * per + u, NSPEC), :] for b in range(shifts // per)
                    )
                    total = part if total is None else jnp.where(
                        lane < 2 * band * (u + 1), part, total
                    )
                whole = total
                for u in range(1, per):
                    whole = whole + turn_lanes(total, -2 * band * u)
                x[0, place, :] = whole

    @pl.when(i == 0)
    def _():
        begin(0)
        for copy in tables_in:
            copy.start()
        for block in range(1, min(ahead - 1, streams // step)):
            begin(block)

    @pl.when(i + ahead - 1 < last)
    def _():
        begin(i + ahead - 1)

    @pl.when(i == 0)
    def _():
        for copy in tables_in:
            copy.wait()

    @pl.when(i < last)
    def _():
        for copy in fetch(i):
            copy.wait()
        mix(jnp.maximum(i - 1, 0))
        analyse()

    @pl.when(i == last)
    def _():
        mix(i - 1)
        lane = lax.broadcasted_iota(jnp.int32, (8, wide * LANES), 1)
        row = lax.broadcasted_iota(jnp.int32, (8, wide * LANES), 0)
        slot = row // 2
        base = (row % 2) * band
        picks = []
        offset = jnp.int32(0)
        for d in range(dests):
            held = counts[d]
            want = offset + jnp.minimum(slot, held - 1) + base
            picks.append(jnp.where((lane == want) & (row < 2 * CAP), 1.0, 0.0))
            offset = offset + held
        pick = jnp.concatenate(picks, axis=0).astype(jnp.bfloat16)
        spectra = jnp.concatenate([x[n] for n in range(wide)], axis=1)
        out = lax.dot_general(
            pick, spectra.astype(jnp.bfloat16), (((1,), (1,)), ((), ())),
            preferred_element_type=jnp.float32,
        )
        tiles = NSPEC * unit // LANES
        for d in range(dests):
            for t in range(streams // unit * tiles):
                row = t // tiles * (2 * CAP * tiles) + t % tiles
                turned[d, pl.ds(row, 2 * CAP, stride=tiles), :] = out[
                    8 * d : 8 * d + 2 * CAP, t * LANES : (t + 1) * LANES
                ]
        out_ref[...] = turned[...].astype(jnp.bfloat16)


def channelize(voltages, chan_counts, dests, start, streams, step, unit):
    band = 2 * dests
    frames = voltages.shape[2]
    analysis, mixing = tables(band)
    packed = packing(band)[1]
    shifts = shifts_of(band)
    ahead = 4 if band <= 64 else 2
    payload = 2 * CAP * NSPEC * streams // LANES
    steps = streams // step
    kernel = functools.partial(channelizer, band, dests, start, streams, step, unit)
    return pl.pallas_call(
        kernel,
        grid_spec=pltpu.PrefetchScalarGridSpec(
            num_scalar_prefetch=1,
            grid=(steps + 1,),
            in_specs=[pl.BlockSpec(memory_space=pl.ANY)] * 3,
            out_specs=pl.BlockSpec((dests, payload, LANES), lambda i, c: (0, 0, 0)),
            scratch_shapes=[
                pltpu.VMEM((ahead, step, frames, 2, FFT_LEN), jnp.bfloat16),
                pltpu.VMEM(analysis.shape, jnp.bfloat16),
                pltpu.VMEM(mixing.shape, jnp.bfloat16),
                pltpu.VMEM((packed // LANES, step * 2 * frames + 16, LANES), jnp.float32),
                pltpu.VMEM((shifts * 2 * band // LANES, step * (NSPEC + 8), LANES), jnp.float32),
                pltpu.VMEM((max(1, 2 * band // LANES), NSPEC * streams, LANES), jnp.float32),
                pltpu.VMEM((dests, payload, LANES), jnp.float32),
                pltpu.SemaphoreType.DMA((ahead + 1, step)),
            ],
        ),
        out_shape=jax.ShapeDtypeStruct((dests, payload, LANES), jnp.bfloat16),
        compiler_params=pltpu.CompilerParams(vmem_limit_bytes=60 * 1024 * 1024),
        cost_estimate=pl.CostEstimate(
            flops=2 * streams * 2 * frames * analysis.size,
            bytes_accessed=2 * 2 * frames * FFT_LEN * streams, transcendentals=0,
        ),
    )(chan_counts, voltages, jnp.asarray(analysis), jnp.asarray(mixing))


def gather_streams(refs, apart, pre, unit):
    spread = LANES // unit
    tiles = NSPEC // spread
    base = 0
    for own, other in zip(refs[::2], refs[1::2]):
        sources, payload = own.shape[:2]
        units = payload // (2 * CAP * tiles)
        lane = lax.broadcasted_iota(jnp.int32, (payload, LANES), 1) // unit
        for q in range(sources // spread):
            for h, ref in enumerate((own, other)):
                parts = [ref[spread * q + a].astype(jnp.float32) for a in range(spread)]
                bit = 1
                while bit < spread:
                    even = lane // bit % 2 == 0
                    mixed = []
                    for a in range(spread):
                        twin = parts[a ^ bit]
                        if a & bit:
                            mixed.append(jnp.where(even, turn_lanes(twin, -unit * bit), parts[a]))
                        else:
                            mixed.append(jnp.where(even, parts[a], turn_lanes(twin, unit * bit)))
                    parts = mixed
                    bit = 2 * bit
                for g in range(spread):
                    apart[h, pl.ds(g, payload, stride=spread), :] = parts[g]
                for u in range(units):
                    place = base + (u * (sources // spread) + q) * LANES
                    for part in range(2 * CAP):
                        row = (u * 2 * CAP + part) * NSPEC
                        pre[part, h * NSPEC : (h + 1) * NSPEC, place : place + LANES] = apart[
                            h, row : row + NSPEC
                        ].astype(jnp.bfloat16)
        base = base + units * sources * unit


def correlator(unit, counts, where, dest_ref, *refs):
    out_ref, apart, pre, post = refs[-4:]
    k = pl.program_id(0)
    time_len, total = pre.shape[1:]

    @pl.when(k == 0)
    def _():
        gather_streams(refs[:-4], apart, pre, unit)
        spot = lax.broadcasted_iota(jnp.int32, (total, total), 0)
        turn = jnp.where(spot == dest_ref[...], 1.0, 0.0).astype(jnp.bfloat16)
        ordered = lax.dot_general(
            pre[...].reshape(2 * CAP * time_len, total), turn, (((1,), (1,)), ((), ())),
            preferred_element_type=jnp.float32,
        )
        post[...] = ordered.astype(jnp.bfloat16).reshape(post.shape)

    rows = out_ref.shape[3]
    every = post[k]
    near = post[k, :, pl.ds(pl.multiple_of(where[1] * rows, LANES), rows)]
    turned = jnp.concatenate([near[time_len:], -near[:time_len]], axis=0)
    valid = jnp.where(k < counts[where[0]], 1.0, 0.0) / jnp.float32(time_len)
    for part, left in enumerate((near, turned)):
        vis = lax.dot_general(
            left, every, (((0,), (0,)), ((), ())), preferred_element_type=jnp.float32
        )
        out_ref[0, 0, part] = (vis * valid).astype(jnp.bfloat16)


def correlate(operands, dest, chan_counts, where, unit):
    total = dest.shape[1]
    most = max(a.shape[1] for a in operands)
    specs = [
        pl.BlockSpec(a.shape, functools.partial(lambda n, k, c, w: (0,) * n, a.ndim))
        for a in [dest] + operands
    ]
    rows = total // 2
    return pl.pallas_call(
        functools.partial(correlator, unit),
        grid_spec=pltpu.PrefetchScalarGridSpec(
            num_scalar_prefetch=2,
            grid=(CAP,),
            in_specs=specs,
            out_specs=pl.BlockSpec((1, 1, 2, rows, total), lambda k, c, w: (0, k, 0, 0, 0)),
            scratch_shapes=[
                pltpu.VMEM((2, most * LANES // unit, LANES), jnp.float32),
                pltpu.VMEM((2 * CAP, 2 * NSPEC, total), jnp.bfloat16),
                pltpu.VMEM((CAP, 4 * NSPEC, total), jnp.bfloat16),
            ],
        ),
        out_shape=jax.ShapeDtypeStruct((1, CAP, 2, rows, total), jnp.bfloat16),
        compiler_params=pltpu.CompilerParams(vmem_limit_bytes=60 * 1024 * 1024),
    )(chan_counts, where, dest, *operands)


def body(voltages, station_map, chan_counts):
    dests = lax.axis_size("stn")
    streams = voltages.shape[0]
    unit = min(streams, 16)
    plan = ((48, 4), (16, 4)) if streams == 64 else ((streams, 2),)
    operands = []
    start = 0
    for size, step in plan:
        outgoing = channelize(voltages, chan_counts, dests, start, size, step, unit)
        own = lax.all_to_all(outgoing, "stn", split_axis=0, concat_axis=0, tiled=True)
        other = lax.ppermute(own, "blk", [(0, 1), (1, 0)])
        operands += [own, other]
        start = start + size
    dest = (2 * station_map[:, None] + jnp.arange(2, dtype=jnp.int32)[None, :]).reshape(-1)
    dest = dest.reshape(dests, streams // unit, unit).transpose(1, 0, 2).reshape(1, -1)
    where = jnp.stack([lax.axis_index("stn"), lax.axis_index("blk")]).astype(jnp.int32)
    return correlate(operands, dest, chan_counts, where, unit)


def solution(mesh):
    return jax.shard_map(
        body,
        mesh=mesh,
        in_specs=(P("stn", "blk", None, None, None), P(), P()),
        out_specs=P("stn", None, None, "blk", None),
        check_vma=False,
    )
```

```python
import functools
import math

import jax
import jax.numpy as jnp
import ml_dtypes
import numpy as np
from jax import lax
from jax.experimental import pallas as pl
from jax.experimental.pallas import tpu as pltpu
from jax.sharding import PartitionSpec as P

FFT_LEN = 4096
TAPS = 16
CAP = 3
NSPEC = 48
LANES = 128


def prototype():
    span = TAPS * FFT_LEN
    points = np.arange(span, dtype=np.float64) + 0.5
    window = 0.5 - 0.5 * np.cos(2.0 * math.pi * points / span)
    shifted = math.pi * (points - span / 2.0) / FFT_LEN
    filt = np.sin(shifted) / shifted * window
    return (filt / np.sqrt(np.sum(filt * filt))).reshape(TAPS, FFT_LEN)


def frame_basis(band, count):
    limit = math.pi * (band + 0.1)
    terms = count + int(limit) + 60
    k = np.arange(terms, dtype=np.float64)
    diagonal = k * (k + 1) + (2 * k * (k + 1) - 1) / ((2 * k + 3) * (2 * k - 1)) * limit**2
    m = k[:-2]
    beside = (m + 2) * (m + 1) / ((2 * m + 3) * np.sqrt((2 * m + 1) * (2 * m + 5))) * limit**2
    matrix = np.diag(diagonal) + np.diag(beside, 2) + np.diag(beside, -2)
    _, vectors = np.linalg.eigh(matrix)
    x = (2 * np.arange(FFT_LEN) + 1.0) / FFT_LEN - 1
    legendre = np.zeros((terms, FFT_LEN))
    legendre[0] = 1.0
    legendre[1] = x
    for j in range(2, terms):
        legendre[j] = ((2 * j - 1) * x * legendre[j - 1] - (j - 1) * legendre[j - 2]) / j
    legendre *= np.sqrt((k + 0.5) * 2.0 / FFT_LEN)[:, None]
    return legendre.T @ vectors[:, :count]


def shifts_of(band):
    return 8 if band <= 64 else 4


def turn_lanes(value, shift):
    shift = shift % LANES
    return pltpu.roll(value, shift, axis=1) if shift else value


def packing(band):
    if 3 * (2 * band + 16) <= 2 * LANES:
        return 2 * band + 16, 2 * LANES, True
    count = -(-(2 * band + 32) // (LANES // 2)) * (LANES // 2)
    return count, -(-2 * count // LANES) * LANES, False


@functools.lru_cache(maxsize=4)
def tables(band):
    bf16 = ml_dtypes.bfloat16
    count, packed, triple = packing(band)
    shifts = shifts_of(band)
    basis = frame_basis(band, count)
    high = basis.astype(bf16)
    low = (basis - high.astype(np.float64)).astype(bf16)
    held = high.astype(np.float64) + low.astype(np.float64)
    lanes = -(-count // LANES) * LANES
    analysis = np.zeros((FFT_LEN, 2 * lanes), bf16)
    analysis[:, :count] = high
    analysis[:, lanes : lanes + count] = low

    phase = 2.0 * math.pi / FFT_LEN * (np.outer(np.arange(FFT_LEN), np.arange(band)) % FFT_LEN)
    wave = np.concatenate([np.cos(phase), -np.sin(phase)], axis=1)
    gram = held.T @ held
    taper = prototype()
    mixing = np.zeros((TAPS // shifts, 2, packed, shifts, 2 * band), bf16)
    for t in range(TAPS):
        real = np.linalg.solve(gram, held.T @ (taper[t][:, None] * wave))
        imag = np.concatenate([-real[:, band:], real[:, :band]], axis=1)
        for c, full in enumerate((real, imag)):
            part = mixing[t // shifts, c, :, t % shifts]
            top = full.astype(bf16)
            part[:count] = top
            part[count : 2 * count] = top
            if triple:
                part[2 * count : 3 * count] = (full - top.astype(np.float64)).astype(bf16)
    return analysis, mixing.reshape(-1, shifts * 2 * band)


def channelizer(
    band, dests, first, streams, step, unit, counts, v_ref, u_hbm, w_hbm, out_ref,
    held, u_ref, w_ref, y, p, x, turned, arrived,
):
    i = pl.program_id(0)
    ahead = held.shape[0]
    shifts = shifts_of(band)
    last = pl.num_programs(0) - 1
    count, packed, triple = packing(band)
    lanes = u_ref.shape[1] // 2
    rows = 2 * v_ref.shape[2]
    reach = NSPEC + 8
    wide = max(1, 2 * band // LANES)
    tables_in = [
        pltpu.make_async_copy(u_hbm, u_ref, arrived.at[ahead, 0]),
        pltpu.make_async_copy(w_hbm, w_ref, arrived.at[ahead, 1]),
    ]

    def fetch(block):
        slot = block % ahead
        return [
            pltpu.make_async_copy(
                v_ref.at[first + block * step + r, 0], held.at[slot, r], arrived.at[slot, r]
            )
            for r in range(step)
        ]

    def begin(block):
        for r, copy in enumerate(fetch(block)):
            copy.start(priority=r % 2)

    def analyse():
        signal = held[i % ahead].reshape(step * rows, FFT_LEN)
        coeff = jnp.dot(signal, u_ref[...], preferred_element_type=jnp.float32)
        coeff = coeff[:, :lanes] + coeff[:, lanes:]
        high = coeff.astype(jnp.bfloat16).astype(jnp.float32)
        low = coeff - high
        if triple:
            lane = lax.broadcasted_iota(jnp.int32, coeff.shape, 1)
            low = turn_lanes(low, count)
            spare = 2 * count - LANES
            y[0, : step * rows] = jnp.where(lane < count, high, low)
            y[1, : step * rows] = jnp.where(lane < spare, low, turn_lanes(high, spare))
        else:
            both = jnp.concatenate([high[:, :count], low[:, :count]], axis=1)
            for n in range(packed // LANES):
                y[n, : step * rows] = both[:, n * LANES : (n + 1) * LANES]

    def mix(block):
        taps = []
        for r in range(step):
            taps.append(jnp.concatenate([
                y[n, pl.ds(r * rows + 2 * shifts * m + c, reach, stride=2), :]
                for m in range(TAPS // shifts) for c in range(2) for n in range(packed // LANES)
            ], axis=1))
        taps = jnp.concatenate(taps, axis=0).astype(jnp.bfloat16)
        mixed = jnp.dot(taps, w_ref[...], preferred_element_type=jnp.float32)
        for n in range(mixed.shape[1] // LANES):
            p[n] = mixed[:, n * LANES : (n + 1) * LANES]
        for r in range(step):
            stream = block * step + r
            place = pl.ds(stream // unit * (NSPEC * unit) + stream % unit, NSPEC, stride=unit)
            if 2 * band >= LANES:
                for n in range(wide):
                    x[n, place, :] = sum(
                        p[wide * h + n, pl.ds(r * reach + h, NSPEC), :] for h in range(shifts)
                    )
            else:
                per = LANES // (2 * band)
                lane = lax.broadcasted_iota(jnp.int32, (NSPEC, LANES), 1)
                total = None
                for u in reversed(range(per)):
                    part = sum(
                        p[b, pl.ds(r * reach + b * per + u, NSPEC), :] for b in range(shifts // per)
                    )
                    total = part if total is None else jnp.where(
                        lane < 2 * band * (u + 1), part, total
                    )
                whole = total
                for u in range(1, per):
                    whole = whole + turn_lanes(total, -2 * band * u)
                x[0, place, :] = whole

    @pl.when(i == 0)
    def _():
        begin(0)
        for copy in tables_in:
            copy.start()
        turned[...] = jnp.zeros(turned.shape, jnp.float32)
        for block in range(1, min(ahead - 1, streams // step)):
            begin(block)

    @pl.when(i + ahead - 1 < last)
    def _():
        begin(i + ahead - 1)

    @pl.when(i == 0)
    def _():
        for copy in tables_in:
            copy.wait()

    @pl.when(i < last)
    def _():
        for copy in fetch(i):
            copy.wait()
        mix(jnp.maximum(i - 1, 0))
        analyse()

    @pl.when(i == last)
    def _():
        mix(i - 1)
        lane = lax.broadcasted_iota(jnp.int32, (8, wide * LANES), 1)
        row = lax.broadcasted_iota(jnp.int32, (8, wide * LANES), 0)
        slot = row // 2
        base = (row % 2) * band
        picks = []
        offset = jnp.int32(0)
        for d in range(dests):
            held = counts[d]
            want = offset + jnp.minimum(slot, held - 1) + base
            picks.append(jnp.where((lane == want) & (row < 2 * CAP), 1.0, 0.0))
            offset = offset + held
        pick = jnp.concatenate(picks, axis=0).astype(jnp.bfloat16)
        spectra = jnp.concatenate([x[n] for n in range(wide)], axis=1)
        out = lax.dot_general(
            pick, spectra.astype(jnp.bfloat16), (((1,), (1,)), ((), ())),
            preferred_element_type=jnp.float32,
        )
        tiles = NSPEC * unit // LANES
        for d in range(dests):
            for t in range(streams // unit * tiles):
                row = t // tiles * (2 * CAP * tiles) + t % tiles
                turned[d, pl.ds(row, 2 * CAP, stride=tiles), :] = out[
                    8 * d : 8 * d + 2 * CAP, t * LANES : (t + 1) * LANES
                ]
        out_ref[...] = turned[...].astype(jnp.bfloat16)


def channelize(voltages, chan_counts, dests, start, streams, step, unit):
    band = 2 * dests
    frames = voltages.shape[2]
    analysis, mixing = tables(band)
    packed = packing(band)[1]
    shifts = shifts_of(band)
    ahead = 4 if band <= 64 else 2
    payload = payload_rows(streams // unit, unit)
    steps = streams // step
    kernel = functools.partial(channelizer, band, dests, start, streams, step, unit)
    return pl.pallas_call(
        kernel,
        grid_spec=pltpu.PrefetchScalarGridSpec(
            num_scalar_prefetch=1,
            grid=(steps + 1,),
            in_specs=[pl.BlockSpec(memory_space=pl.ANY)] * 3,
            out_specs=pl.BlockSpec((dests, payload, LANES), lambda i, c: (0, 0, 0)),
            scratch_shapes=[
                pltpu.VMEM((ahead, step, frames, 2, FFT_LEN), jnp.bfloat16),
                pltpu.VMEM(analysis.shape, jnp.bfloat16),
                pltpu.VMEM(mixing.shape, jnp.bfloat16),
                pltpu.VMEM((packed // LANES, step * 2 * frames + 16, LANES), jnp.float32),
                pltpu.VMEM((shifts * 2 * band // LANES, step * (NSPEC + 8), LANES), jnp.float32),
                pltpu.VMEM((max(1, 2 * band // LANES), NSPEC * streams, LANES), jnp.float32),
                pltpu.VMEM((dests, payload, LANES), jnp.float32),
                pltpu.SemaphoreType.DMA((ahead + 1, step)),
            ],
        ),
        out_shape=jax.ShapeDtypeStruct((dests, payload, LANES), jnp.bfloat16),
        compiler_params=pltpu.CompilerParams(
            vmem_limit_bytes=(32 if band <= 64 else 60) * 1024 * 1024
        ),
        cost_estimate=pl.CostEstimate(
            flops=2 * streams * 2 * frames * analysis.size,
            bytes_accessed=2 * 2 * frames * FFT_LEN * streams, transcendentals=0,
        ),
    )(chan_counts, voltages, jnp.asarray(analysis), jnp.asarray(mixing))


def payload_rows(units, unit):
    return -(-units * 2 * CAP * NSPEC * unit // (16 * LANES)) * 16


def streams_in(part, unit):
    return part.shape[0] * unit * (part.shape[1] * LANES // (2 * CAP * NSPEC * unit))


def regroup(ref, apart, pre, unit, base):
    spread = LANES // unit
    sources, payload = ref.shape[:2]
    units = streams_in(ref, unit) // (sources * unit)
    lane = lax.broadcasted_iota(jnp.int32, (payload, LANES), 1) // unit
    for q in range(sources // spread):
        parts = [ref[spread * q + a].astype(jnp.float32) for a in range(spread)]
        bit = 1
        while bit < spread:
            even = lane // bit % 2 == 0
            mixed = []
            for a in range(spread):
                twin = parts[a ^ bit]
                if a & bit:
                    mixed.append(jnp.where(even, turn_lanes(twin, -unit * bit), parts[a]))
                else:
                    mixed.append(jnp.where(even, parts[a], turn_lanes(twin, unit * bit)))
            parts = mixed
            bit = 2 * bit
        slot = q % 2
        for g in range(spread):
            apart[slot, pl.ds(g, payload, stride=spread), :] = parts[g]
        rows = 2 * CAP * NSPEC
        for u in range(units):
            place = base + (u * (sources // spread) + q) * LANES
            pre[:, place : place + LANES] = apart[slot, u * rows : (u + 1) * rows].astype(jnp.bfloat16)


def one_hot(dest, total):
    spot = lax.broadcasted_iota(jnp.int32, (total, dest.shape[1]), 0)
    return jnp.where(spot == dest, 1.0, 0.0).astype(jnp.bfloat16)


def permute(rows, turn):
    return lax.dot_general(
        rows, turn, (((1,), (1,)), ((), ())), preferred_element_type=jnp.float32
    )


def settler(unit, dest_ref, part_hbm, out_ref, part, apart, pre, arrived):
    copy = pltpu.make_async_copy(part_hbm, part, arrived)
    copy.start()
    turn = one_hot(dest_ref[...], out_ref.shape[1])
    copy.wait()
    regroup(part, apart, pre, unit, 0)
    out_ref[...] = permute(pre[...], turn).astype(jnp.bfloat16)


def settle(part, dest, total, unit):
    rows = 2 * CAP * NSPEC
    return pl.pallas_call(
        functools.partial(settler, unit),
        in_specs=[pl.BlockSpec(memory_space=pltpu.VMEM), pl.BlockSpec(memory_space=pl.ANY)],
        out_specs=pl.BlockSpec(memory_space=pltpu.VMEM),
        out_shape=jax.ShapeDtypeStruct((rows, total), jnp.bfloat16),
        scratch_shapes=[
            pltpu.VMEM(part.shape, jnp.bfloat16),
            pltpu.VMEM((2, part.shape[1] * LANES // unit, LANES), jnp.float32),
            pltpu.VMEM((rows, dest.shape[1]), jnp.bfloat16),
            pltpu.SemaphoreType.DMA,
        ],
        compiler_params=pltpu.CompilerParams(vmem_limit_bytes=32 * 1024 * 1024),
        cost_estimate=pl.CostEstimate(
            flops=2 * rows * dest.shape[1] * total, bytes_accessed=2 * part.size + 2 * rows * total,
            transcendentals=0,
        ),
    )(dest, part)


def correlator(unit, own_count, counts, where, dest_ref, *refs):
    given = (len(refs) - 6) // 2
    sources, out_ref, held = refs[:given], refs[given], refs[given + 1 : 2 * given + 1]
    apart, pre, post, near, arrived = refs[2 * given + 1 :]
    k = pl.program_id(0)
    part = pl.program_id(1)
    total = post.shape[2]
    rows = out_ref.shape[3]
    time_len = 2 * NSPEC

    @pl.when((k == 0) & (part == 0))
    def _():
        copies = [
            pltpu.make_async_copy(a, b, arrived.at[n]) for n, (a, b) in enumerate(zip(sources, held))
        ]
        for copy in copies:
            copy.start()
        turn = one_hot(dest_ref[...], total)
        for copy in copies:
            copy.wait()
        other = held[:-own_count]
        ours = held[len(held) - own_count :]
        base = 0
        for ref in other:
            regroup(ref, apart, pre, unit, base)
            base += streams_in(ref, unit)
        halves = [permute(pre[...], turn)]
        fresh = ours[0]
        width = streams_in(fresh, unit)
        regroup(fresh, apart, pre, unit, total - width)
        mine = permute(pre[:, total - width :], turn[:, total - width :])
        for ref in ours[1:]:
            mine = mine + ref[...].astype(jnp.float32)
        halves.append(mine)
        for n in range(2 * CAP):
            for h, half in enumerate(halves):
                first = n % 2 * time_len + h * NSPEC
                post[n // 2, first : first + NSPEC] = half[n * NSPEC : (n + 1) * NSPEC].astype(
                    jnp.bfloat16
                )

    @pl.when(part == 0)
    def _():
        mine = post[k, :, pl.ds(pl.multiple_of(where[1] * rows, LANES), rows)]
        near[...] = mine.T

    valid = jnp.where(k < counts[where[0]], 1.0, 0.0) / jnp.float32(time_len)

    def put(right):
        vis = jnp.dot(near[...], right, preferred_element_type=jnp.float32)
        out_ref[0, 0, 0] = (vis * valid).astype(jnp.bfloat16)

    @pl.when(part == 0)
    def _():
        put(post[k])

    @pl.when(part == 1)
    def _():
        put(jnp.concatenate([-post[k, time_len:], post[k, :time_len]], axis=0))


def correlate(others, ours, dest, chan_counts, where, unit):
    total = dest.shape[1]
    operands = others + ours
    most = max(a.shape[1] for a in operands if a.ndim == 3)
    rows = total // 2
    return pl.pallas_call(
        functools.partial(correlator, unit, len(ours)),
        grid_spec=pltpu.PrefetchScalarGridSpec(
            num_scalar_prefetch=2,
            grid=(CAP, 2),
            in_specs=[pl.BlockSpec((1, total), lambda k, p, c, w: (0, 0))]
            + [pl.BlockSpec(memory_space=pl.ANY)] * len(operands),
            out_specs=pl.BlockSpec((1, 1, 1, rows, total), lambda k, p, c, w: (0, k, p, 0, 0)),
            scratch_shapes=[pltpu.VMEM(a.shape, jnp.bfloat16) for a in operands]
            + [
                pltpu.VMEM((2, most * LANES // unit, LANES), jnp.float32),
                pltpu.VMEM((2 * CAP * NSPEC, total), jnp.bfloat16),
                pltpu.VMEM((CAP, 4 * NSPEC, total), jnp.bfloat16),
                pltpu.VMEM((rows, 4 * NSPEC), jnp.bfloat16),
                pltpu.SemaphoreType.DMA((len(operands),)),
            ],
        ),
        out_shape=jax.ShapeDtypeStruct((1, CAP, 2, rows, total), jnp.bfloat16),
        compiler_params=pltpu.CompilerParams(vmem_limit_bytes=32 * 1024 * 1024),
    )(chan_counts, where, dest, *operands)


def body(voltages, station_map, chan_counts):
    dests = lax.axis_size("stn")
    streams = voltages.shape[0]
    total = dests * streams
    unit = min(streams, 16)
    plan = (48, 16) if streams == 64 else (streams,)
    dest = (2 * station_map[:, None] + jnp.arange(2, dtype=jnp.int32)[None, :]).reshape(-1)
    dest = dest.reshape(dests, streams // unit, unit).transpose(1, 0, 2).reshape(1, -1)
    where = jnp.stack([lax.axis_index("stn"), lax.axis_index("blk")]).astype(jnp.int32)
    others, settled = [], []
    start = 0
    for size in plan:
        outgoing = channelize(voltages, chan_counts, dests, start, size, 2, unit)
        chan_counts, outgoing = lax.optimization_barrier((chan_counts, outgoing))
        own = lax.all_to_all(outgoing, "stn", split_axis=0, concat_axis=0, tiled=True)
        others.append(lax.ppermute(own, "blk", [(0, 1), (1, 0)]))
        if start + size < streams:
            spots = dest[:, start * dests : (start + size) * dests]
            settled.append(settle(own, spots, total, unit))
        start = start + size
    return correlate(others, [own] + settled, dest, chan_counts, where, unit)


def solution(mesh):
    return jax.shard_map(
        body,
        mesh=mesh,
        in_specs=(P("stn", "blk", None, None, None), P(), P()),
        out_specs=P("stn", None, None, "blk", None),
        check_vma=False,
    )
```

```python
import functools
import math

import jax
import jax.numpy as jnp
import ml_dtypes
import numpy as np
from jax import lax
from jax.experimental import pallas as pl
from jax.experimental.pallas import tpu as pltpu
from jax.sharding import PartitionSpec as P

FFT_LEN = 4096
TAPS = 16
CAP = 3
NSPEC = 48
LANES = 128


def prototype():
    span = TAPS * FFT_LEN
    points = np.arange(span, dtype=np.float64) + 0.5
    window = 0.5 - 0.5 * np.cos(2.0 * math.pi * points / span)
    shifted = math.pi * (points - span / 2.0) / FFT_LEN
    filt = np.sin(shifted) / shifted * window
    return (filt / np.sqrt(np.sum(filt * filt))).reshape(TAPS, FFT_LEN)


def frame_basis(band, count):
    limit = math.pi * (band + 0.1)
    terms = count + int(limit) + 60
    k = np.arange(terms, dtype=np.float64)
    diagonal = k * (k + 1) + (2 * k * (k + 1) - 1) / ((2 * k + 3) * (2 * k - 1)) * limit**2
    m = k[:-2]
    beside = (m + 2) * (m + 1) / ((2 * m + 3) * np.sqrt((2 * m + 1) * (2 * m + 5))) * limit**2
    matrix = np.diag(diagonal) + np.diag(beside, 2) + np.diag(beside, -2)
    _, vectors = np.linalg.eigh(matrix)
    x = (2 * np.arange(FFT_LEN) + 1.0) / FFT_LEN - 1
    legendre = np.zeros((terms, FFT_LEN))
    legendre[0] = 1.0
    legendre[1] = x
    for j in range(2, terms):
        legendre[j] = ((2 * j - 1) * x * legendre[j - 1] - (j - 1) * legendre[j - 2]) / j
    legendre *= np.sqrt((k + 0.5) * 2.0 / FFT_LEN)[:, None]
    return legendre.T @ vectors[:, :count]


def shifts_of(band):
    return 8 if band <= 64 else 4


def turn_lanes(value, shift):
    shift = shift % LANES
    return pltpu.roll(value, shift, axis=1) if shift else value


def packing(band):
    if 3 * (2 * band + 16) <= 2 * LANES:
        return 2 * band + 16, 2 * LANES, True
    count = -(-(2 * band + 32) // (LANES // 2)) * (LANES // 2)
    return count, -(-2 * count // LANES) * LANES, False


@functools.lru_cache(maxsize=4)
def tables(band):
    bf16 = ml_dtypes.bfloat16
    count, packed, triple = packing(band)
    shifts = shifts_of(band)
    basis = frame_basis(band, count)
    high = basis.astype(bf16)
    low = (basis - high.astype(np.float64)).astype(bf16)
    held = high.astype(np.float64) + low.astype(np.float64)
    lanes = -(-count // LANES) * LANES
    analysis = np.zeros((FFT_LEN, 2 * lanes), bf16)
    analysis[:, :count] = high
    analysis[:, lanes : lanes + count] = low

    phase = 2.0 * math.pi / FFT_LEN * (np.outer(np.arange(FFT_LEN), np.arange(band)) % FFT_LEN)
    wave = np.concatenate([np.cos(phase), -np.sin(phase)], axis=1)
    gram = held.T @ held
    taper = prototype()
    mixing = np.zeros((TAPS // shifts, 2, packed, shifts, 2 * band), bf16)
    for t in range(TAPS):
        real = np.linalg.solve(gram, held.T @ (taper[t][:, None] * wave))
        imag = np.concatenate([-real[:, band:], real[:, :band]], axis=1)
        for c, full in enumerate((real, imag)):
            part = mixing[t // shifts, c, :, t % shifts]
            top = full.astype(bf16)
            part[:count] = top
            part[count : 2 * count] = top
            if triple:
                part[2 * count : 3 * count] = (full - top.astype(np.float64)).astype(bf16)
    return analysis, mixing.reshape(-1, shifts * 2 * band)


def channelizer(
    band, dests, first, streams, step, unit, counts, v_ref, u_hbm, w_hbm, out_ref,
    held, u_ref, w_ref, y, p, x, turned, arrived,
):
    i = pl.program_id(0)
    ahead = held.shape[0]
    shifts = shifts_of(band)
    last = pl.num_programs(0) - 1
    count, packed, triple = packing(band)
    lanes = u_ref.shape[1] // 2
    rows = 2 * v_ref.shape[2]
    reach = NSPEC + 8
    wide = max(1, 2 * band // LANES)
    tables_in = [
        pltpu.make_async_copy(u_hbm, u_ref, arrived.at[ahead, 0]),
        pltpu.make_async_copy(w_hbm, w_ref, arrived.at[ahead, 1]),
    ]

    def fetch(block):
        slot = block % ahead
        return [
            pltpu.make_async_copy(
                v_ref.at[first + block * step + r, 0], held.at[slot, r], arrived.at[slot, r]
            )
            for r in range(step)
        ]

    def begin(block):
        for r, copy in enumerate(fetch(block)):
            copy.start(priority=r % 2)

    def analyse():
        signal = held[i % ahead].reshape(step * rows, FFT_LEN)
        coeff = jnp.dot(signal, u_ref[...], preferred_element_type=jnp.float32)
        coeff = coeff[:, :lanes] + coeff[:, lanes:]
        high = coeff.astype(jnp.bfloat16).astype(jnp.float32)
        low = coeff - high
        if triple:
            lane = lax.broadcasted_iota(jnp.int32, coeff.shape, 1)
            low = turn_lanes(low, count)
            spare = 2 * count - LANES
            y[0, : step * rows] = jnp.where(lane < count, high, low)
            y[1, : step * rows] = jnp.where(lane < spare, low, turn_lanes(high, spare))
        else:
            both = jnp.concatenate([high[:, :count], low[:, :count]], axis=1)
            for n in range(packed // LANES):
                y[n, : step * rows] = both[:, n * LANES : (n + 1) * LANES]

    def mix(block):
        taps = []
        for r in range(step):
            taps.append(jnp.concatenate([
                y[n, pl.ds(r * rows + 2 * shifts * m + c, reach, stride=2), :]
                for m in range(TAPS // shifts) for c in range(2) for n in range(packed // LANES)
            ], axis=1))
        taps = jnp.concatenate(taps, axis=0).astype(jnp.bfloat16)
        mixed = jnp.dot(taps, w_ref[...], preferred_element_type=jnp.float32)
        for n in range(mixed.shape[1] // LANES):
            p[n] = mixed[:, n * LANES : (n + 1) * LANES]
        for r in range(step):
            stream = block * step + r
            place = pl.ds(stream // unit * (NSPEC * unit) + stream % unit, NSPEC, stride=unit)
            if 2 * band >= LANES:
                for n in range(wide):
                    x[n, place, :] = sum(
                        p[wide * h + n, pl.ds(r * reach + h, NSPEC), :] for h in range(shifts)
                    )
            else:
                per = LANES // (2 * band)
                lane = lax.broadcasted_iota(jnp.int32, (NSPEC, LANES), 1)
                total = None
                for u in reversed(range(per)):
                    part = sum(
                        p[b, pl.ds(r * reach + b * per + u, NSPEC), :] for b in range(shifts // per)
                    )
                    total = part if total is None else jnp.where(
                        lane < 2 * band * (u + 1), part, total
                    )
                whole = total
                for u in range(1, per):
                    whole = whole + turn_lanes(total, -2 * band * u)
                x[0, place, :] = whole

    @pl.when(i == 0)
    def _():
        begin(0)
        for copy in tables_in:
            copy.start()
        turned[...] = jnp.zeros(turned.shape, jnp.float32)
        if streams // step > 1:
            begin(1)

    @pl.when((i > 0) & (i + ahead - 1 < last))
    def _():
        begin(i + ahead - 1)

    @pl.when(i == 0)
    def _():
        for copy in tables_in:
            copy.wait()

    @pl.when(i < last)
    def _():
        for copy in fetch(i):
            copy.wait()

    @pl.when(i == 0)
    def _():
        for block in range(2, min(ahead, streams // step)):
            begin(block)

    @pl.when(i < last)
    def _():
        mix(jnp.maximum(i - 1, 0))
        analyse()

    @pl.when(i == last)
    def _():
        mix(i - 1)
        lane = lax.broadcasted_iota(jnp.int32, (8, wide * LANES), 1)
        row = lax.broadcasted_iota(jnp.int32, (8, wide * LANES), 0)
        slot = row // 2
        base = (row % 2) * band
        picks = []
        offset = jnp.int32(0)
        for d in range(dests):
            held = counts[d]
            want = offset + jnp.minimum(slot, held - 1) + base
            picks.append(jnp.where((lane == want) & (row < 2 * CAP), 1.0, 0.0))
            offset = offset + held
        pick = jnp.concatenate(picks, axis=0).astype(jnp.bfloat16)
        spectra = jnp.concatenate([x[n] for n in range(wide)], axis=1)
        out = lax.dot_general(
            pick, spectra.astype(jnp.bfloat16), (((1,), (1,)), ((), ())),
            preferred_element_type=jnp.float32,
        )
        tiles = NSPEC * unit // LANES
        for d in range(dests):
            for t in range(streams // unit * tiles):
                row = t // tiles * (2 * CAP * tiles) + t % tiles
                turned[d, pl.ds(row, 2 * CAP, stride=tiles), :] = out[
                    8 * d : 8 * d + 2 * CAP, t * LANES : (t + 1) * LANES
                ]
        out_ref[...] = turned[...].astype(jnp.bfloat16)


def channelize(voltages, chan_counts, dests, start, streams, step, unit, room):
    band = 2 * dests
    frames = voltages.shape[2]
    analysis, mixing = tables(band)
    packed = packing(band)[1]
    shifts = shifts_of(band)
    ahead = 4 if band <= 64 else 2
    payload = payload_rows(streams // unit, unit)
    steps = streams // step
    kernel = functools.partial(channelizer, band, dests, start, streams, step, unit)
    return pl.pallas_call(
        kernel,
        grid_spec=pltpu.PrefetchScalarGridSpec(
            num_scalar_prefetch=1,
            grid=(steps + 1,),
            in_specs=[pl.BlockSpec(memory_space=pl.ANY)] * 3,
            out_specs=pl.BlockSpec((dests, payload, LANES), lambda i, c: (0, 0, 0)),
            scratch_shapes=[
                pltpu.VMEM((ahead, step, frames, 2, FFT_LEN), jnp.bfloat16),
                pltpu.VMEM(analysis.shape, jnp.bfloat16),
                pltpu.VMEM(mixing.shape, jnp.bfloat16),
                pltpu.VMEM((packed // LANES, step * 2 * frames + 16, LANES), jnp.float32),
                pltpu.VMEM((shifts * 2 * band // LANES, step * (NSPEC + 8), LANES), jnp.float32),
                pltpu.VMEM((max(1, 2 * band // LANES), NSPEC * streams, LANES), jnp.float32),
                pltpu.VMEM((dests, payload, LANES), jnp.float32),
                pltpu.SemaphoreType.DMA((ahead + 1, step)),
            ],
        ),
        out_shape=jax.ShapeDtypeStruct((dests, payload, LANES), jnp.bfloat16),
        compiler_params=pltpu.CompilerParams(
            vmem_limit_bytes=room * 1024 * 1024
        ),
        cost_estimate=pl.CostEstimate(
            flops=2 * streams * 2 * frames * analysis.size,
            bytes_accessed=2 * 2 * frames * FFT_LEN * streams, transcendentals=0,
        ),
    )(chan_counts, voltages, jnp.asarray(analysis), jnp.asarray(mixing))


def payload_rows(units, unit):
    return -(-units * 2 * CAP * NSPEC * unit // (16 * LANES)) * 16


def streams_in(part, unit):
    return part.shape[0] * unit * (part.shape[1] * LANES // (2 * CAP * NSPEC * unit))


def regroup(ref, apart, pre, unit, base):
    spread = LANES // unit
    sources, payload = ref.shape[:2]
    units = streams_in(ref, unit) // (sources * unit)
    lane = lax.broadcasted_iota(jnp.int32, (payload, LANES), 1) // unit
    for q in range(sources // spread):
        parts = [ref[spread * q + a].astype(jnp.float32) for a in range(spread)]
        bit = 1
        while bit < spread:
            even = lane // bit % 2 == 0
            mixed = []
            for a in range(spread):
                twin = parts[a ^ bit]
                if a & bit:
                    mixed.append(jnp.where(even, turn_lanes(twin, -unit * bit), parts[a]))
                else:
                    mixed.append(jnp.where(even, parts[a], turn_lanes(twin, unit * bit)))
            parts = mixed
            bit = 2 * bit
        slot = q % 2
        for g in range(spread):
            apart[slot, pl.ds(g, payload, stride=spread), :] = parts[g]
        rows = 2 * CAP * NSPEC
        for u in range(units):
            place = base + (u * (sources // spread) + q) * LANES
            pre[:, place : place + LANES] = apart[slot, u * rows : (u + 1) * rows].astype(jnp.bfloat16)


def one_hot(dest, total):
    spot = lax.broadcasted_iota(jnp.int32, (total, dest.shape[1]), 0)
    return jnp.where(spot == dest, 1.0, 0.0).astype(jnp.bfloat16)


def permute(rows, turn):
    return lax.dot_general(
        rows, turn, (((1,), (1,)), ((), ())), preferred_element_type=jnp.float32
    )


def settler(unit, dest_ref, part_hbm, out_ref, part, apart, pre, arrived):
    copy = pltpu.make_async_copy(part_hbm, part, arrived)
    copy.start()
    turn = one_hot(dest_ref[...], out_ref.shape[1])
    copy.wait()
    regroup(part, apart, pre, unit, 0)
    out_ref[...] = permute(pre[...], turn).astype(jnp.bfloat16)


def settle(part, dest, total, unit):
    rows = 2 * CAP * NSPEC
    return pl.pallas_call(
        functools.partial(settler, unit),
        in_specs=[pl.BlockSpec(memory_space=pltpu.VMEM), pl.BlockSpec(memory_space=pl.ANY)],
        out_specs=pl.BlockSpec(memory_space=pltpu.VMEM),
        out_shape=jax.ShapeDtypeStruct((rows, total), jnp.bfloat16),
        scratch_shapes=[
            pltpu.VMEM(part.shape, jnp.bfloat16),
            pltpu.VMEM((2, part.shape[1] * LANES // unit, LANES), jnp.float32),
            pltpu.VMEM((rows, dest.shape[1]), jnp.bfloat16),
            pltpu.SemaphoreType.DMA,
        ],
        compiler_params=pltpu.CompilerParams(vmem_limit_bytes=32 * 1024 * 1024),
        cost_estimate=pl.CostEstimate(
            flops=2 * rows * dest.shape[1] * total, bytes_accessed=2 * part.size + 2 * rows * total,
            transcendentals=0,
        ),
    )(dest, part)


def correlator(unit, own_count, counts, where, dest_ref, *refs):
    given = (len(refs) - 6) // 2
    sources, out_ref, held = refs[:given], refs[given], refs[given + 1 : 2 * given + 1]
    apart, pre, post, near, arrived = refs[2 * given + 1 :]
    k = pl.program_id(0)
    part = pl.program_id(1)
    total = post.shape[2]
    rows = out_ref.shape[3]
    time_len = 2 * NSPEC

    @pl.when((k == 0) & (part == 0))
    def _():
        copies = [
            pltpu.make_async_copy(a, b, arrived.at[n]) for n, (a, b) in enumerate(zip(sources, held))
        ]
        for copy in copies:
            copy.start()
        turn = one_hot(dest_ref[...], total)
        for copy in copies:
            copy.wait()
        other = held[:-own_count]
        ours = held[len(held) - own_count :]
        base = 0
        for ref in other:
            regroup(ref, apart, pre, unit, base)
            base += streams_in(ref, unit)
        halves = [permute(pre[...], turn)]
        fresh = ours[0]
        width = streams_in(fresh, unit)
        regroup(fresh, apart, pre, unit, total - width)
        mine = permute(pre[:, total - width :], turn[:, total - width :])
        for ref in ours[1:]:
            mine = mine + ref[...].astype(jnp.float32)
        halves.append(mine)
        for n in range(2 * CAP):
            for h, half in enumerate(halves):
                first = n % 2 * time_len + h * NSPEC
                post[n // 2, first : first + NSPEC] = half[n * NSPEC : (n + 1) * NSPEC].astype(
                    jnp.bfloat16
                )

    @pl.when(part == 0)
    def _():
        mine = post[k, :, pl.ds(pl.multiple_of(where[1] * rows, LANES), rows)]
        near[...] = mine.T

    valid = jnp.where(k < counts[where[0]], 1.0, 0.0) / jnp.float32(time_len)

    def put(right):
        vis = jnp.dot(near[...], right, preferred_element_type=jnp.float32)
        out_ref[0, 0, 0] = (vis * valid).astype(jnp.bfloat16)

    @pl.when(part == 0)
    def _():
        put(post[k])

    @pl.when(part == 1)
    def _():
        put(jnp.concatenate([-post[k, time_len:], post[k, :time_len]], axis=0))


def correlate(others, ours, dest, chan_counts, where, unit):
    total = dest.shape[1]
    operands = others + ours
    most = max(a.shape[1] for a in operands if a.ndim == 3)
    rows = total // 2
    return pl.pallas_call(
        functools.partial(correlator, unit, len(ours)),
        grid_spec=pltpu.PrefetchScalarGridSpec(
            num_scalar_prefetch=2,
            grid=(CAP, 2),
            in_specs=[pl.BlockSpec((1, total), lambda k, p, c, w: (0, 0))]
            + [pl.BlockSpec(memory_space=pl.ANY)] * len(operands),
            out_specs=pl.BlockSpec((1, 1, 1, rows, total), lambda k, p, c, w: (0, k, p, 0, 0)),
            scratch_shapes=[pltpu.VMEM(a.shape, jnp.bfloat16) for a in operands]
            + [
                pltpu.VMEM((2, most * LANES // unit, LANES), jnp.float32),
                pltpu.VMEM((2 * CAP * NSPEC, total), jnp.bfloat16),
                pltpu.VMEM((CAP, 4 * NSPEC, total), jnp.bfloat16),
                pltpu.VMEM((rows, 4 * NSPEC), jnp.bfloat16),
                pltpu.SemaphoreType.DMA((len(operands),)),
            ],
        ),
        out_shape=jax.ShapeDtypeStruct((1, CAP, 2, rows, total), jnp.bfloat16),
        compiler_params=pltpu.CompilerParams(vmem_limit_bytes=32 * 1024 * 1024),
    )(chan_counts, where, dest, *operands)


def two_stages(outgoing, inner):
    dests = outgoing.shape[0]
    outer = dests // inner
    far = [[o * inner + i for o in range(outer)] for i in range(inner)]
    near = [[o * inner + i for i in range(inner)] for o in range(outer)]
    half = lax.all_to_all(
        outgoing, "stn", split_axis=0, concat_axis=0, axis_index_groups=far, tiled=True
    )
    half = half.reshape((outer, inner) + outgoing.shape[1:]).swapaxes(0, 1).reshape(outgoing.shape)
    return lax.all_to_all(
        half, "stn", split_axis=0, concat_axis=0, axis_index_groups=near, tiled=True
    )


def body(voltages, station_map, chan_counts):
    dests = lax.axis_size("stn")
    streams = voltages.shape[0]
    total = dests * streams
    unit = min(streams, 16)
    inner = 4
    plan = ((48, 4, 60), (16, 2, 32)) if streams == 64 else ((streams, 2, 60),)
    dest = (2 * station_map[:, None] + jnp.arange(2, dtype=jnp.int32)[None, :]).reshape(-1)
    dest = dest.reshape(dests, streams // unit, unit).transpose(1, 0, 2)
    where = jnp.stack([lax.axis_index("stn"), lax.axis_index("blk")]).astype(jnp.int32)
    others, settled, spots = [], [], []
    start = 0
    for size, step, room in plan:
        outgoing = channelize(voltages, chan_counts, dests, start, size, step, unit, room)
        chan_counts, outgoing = lax.optimization_barrier((chan_counts, outgoing))
        spot = dest[start // unit : (start + size) // unit]
        if start + size < streams:
            own = lax.all_to_all(outgoing, "stn", split_axis=0, concat_axis=0, tiled=True)
            spots.append(spot.reshape(1, -1))
            settled.append(settle(own, spots[-1], total, unit))
        else:
            own = two_stages(outgoing, inner)
            spot = spot.reshape(-1, dests // inner, inner, unit).swapaxes(1, 2)
            spots.append(spot.reshape(1, -1))
        others.append(lax.ppermute(own, "blk", [(0, 1), (1, 0)]))
        start = start + size
    spots = jnp.concatenate(spots, axis=1)
    return correlate(others, [own] + settled, spots, chan_counts, where, unit)


def solution(mesh):
    return jax.shard_map(
        body,
        mesh=mesh,
        in_specs=(P("stn", "blk", None, None, None), P(), P()),
        out_specs=P("stn", None, None, "blk", None),
        check_vma=False,
    )
```

```python
import functools
import math

import jax
import jax.numpy as jnp
import ml_dtypes
import numpy as np
from jax import lax
from jax.experimental import pallas as pl
from jax.experimental.pallas import tpu as pltpu
from jax.sharding import PartitionSpec as P

FFT_LEN = 4096
TAPS = 16
CAP = 3
NSPEC = 48
LANES = 128


def prototype():
    span = TAPS * FFT_LEN
    points = np.arange(span, dtype=np.float64) + 0.5
    window = 0.5 - 0.5 * np.cos(2.0 * math.pi * points / span)
    shifted = math.pi * (points - span / 2.0) / FFT_LEN
    filt = np.sin(shifted) / shifted * window
    return (filt / np.sqrt(np.sum(filt * filt))).reshape(TAPS, FFT_LEN)


def frame_basis(band, count):
    limit = math.pi * (band + 0.1)
    terms = count + int(limit) + 60
    k = np.arange(terms, dtype=np.float64)
    diagonal = k * (k + 1) + (2 * k * (k + 1) - 1) / ((2 * k + 3) * (2 * k - 1)) * limit**2
    m = k[:-2]
    beside = (m + 2) * (m + 1) / ((2 * m + 3) * np.sqrt((2 * m + 1) * (2 * m + 5))) * limit**2
    matrix = np.diag(diagonal) + np.diag(beside, 2) + np.diag(beside, -2)
    _, vectors = np.linalg.eigh(matrix)
    x = (2 * np.arange(FFT_LEN) + 1.0) / FFT_LEN - 1
    legendre = np.zeros((terms, FFT_LEN))
    legendre[0] = 1.0
    legendre[1] = x
    for j in range(2, terms):
        legendre[j] = ((2 * j - 1) * x * legendre[j - 1] - (j - 1) * legendre[j - 2]) / j
    legendre *= np.sqrt((k + 0.5) * 2.0 / FFT_LEN)[:, None]
    return legendre.T @ vectors[:, :count]


def shifts_of(band):
    return 4


def turn_lanes(value, shift):
    shift = shift % LANES
    return pltpu.roll(value, shift, axis=1) if shift else value


def packing(band):
    if 3 * (2 * band + 16) <= 2 * LANES:
        return 2 * band + 16, 2 * LANES, True
    count = -(-(2 * band + 32) // (LANES // 2)) * (LANES // 2)
    return count, -(-2 * count // LANES) * LANES, False


@functools.lru_cache(maxsize=4)
def tables(band):
    bf16 = ml_dtypes.bfloat16
    count, packed, triple = packing(band)
    shifts = shifts_of(band)
    basis = frame_basis(band, count)
    high = basis.astype(bf16)
    low = (basis - high.astype(np.float64)).astype(bf16)
    held = high.astype(np.float64) + low.astype(np.float64)
    lanes = -(-count // LANES) * LANES
    analysis = np.zeros((FFT_LEN, 2 * lanes), bf16)
    analysis[:, :count] = high
    analysis[:, lanes : lanes + count] = low

    phase = 2.0 * math.pi / FFT_LEN * (np.outer(np.arange(FFT_LEN), np.arange(band)) % FFT_LEN)
    wave = np.concatenate([np.cos(phase), -np.sin(phase)], axis=1)
    gram = held.T @ held
    taper = prototype()
    mixing = np.zeros((TAPS // shifts, 2, packed, shifts, 2 * band), bf16)
    for t in range(TAPS):
        real = np.linalg.solve(gram, held.T @ (taper[t][:, None] * wave))
        imag = np.concatenate([-real[:, band:], real[:, :band]], axis=1)
        for c, full in enumerate((real, imag)):
            part = mixing[t // shifts, c, :, t % shifts]
            top = full.astype(bf16)
            part[:count] = top
            part[count : 2 * count] = top
            if triple:
                part[2 * count : 3 * count] = (full - top.astype(np.float64)).astype(bf16)
    return analysis, mixing.reshape(-1, shifts * 2 * band)


def channelizer(
    band, dests, first, streams, step, unit, counts, v_ref, u_hbm, w_hbm, out_ref,
    held, u_ref, w_ref, y, p, x, turned, arrived,
):
    i = pl.program_id(0)
    ahead = held.shape[0]
    shifts = shifts_of(band)
    last = pl.num_programs(0) - 1
    count, packed, triple = packing(band)
    lanes = u_ref.shape[1] // 2
    rows = 2 * v_ref.shape[2]
    reach = NSPEC + 8
    wide = max(1, 2 * band // LANES)
    tables_in = [
        pltpu.make_async_copy(u_hbm, u_ref, arrived.at[ahead, 0]),
        pltpu.make_async_copy(w_hbm, w_ref, arrived.at[ahead, 1]),
    ]

    def fetch(block):
        slot = block % ahead
        return [
            pltpu.make_async_copy(
                v_ref.at[first + block * step + r, 0], held.at[slot, r], arrived.at[slot, r]
            )
            for r in range(step)
        ]

    def begin(block):
        for copy in fetch(block):
            copy.start()

    def analyse():
        signal = held[i % ahead].reshape(step * rows, FFT_LEN)
        coeff = jnp.dot(signal, u_ref[...], preferred_element_type=jnp.float32)
        coeff = coeff[:, :lanes] + coeff[:, lanes:]
        high = coeff.astype(jnp.bfloat16).astype(jnp.float32)
        low = coeff - high
        if triple:
            lane = lax.broadcasted_iota(jnp.int32, coeff.shape, 1)
            low = turn_lanes(low, count)
            spare = 2 * count - LANES
            y[0, : step * rows] = jnp.where(lane < count, high, low)
            y[1, : step * rows] = jnp.where(lane < spare, low, turn_lanes(high, spare))
        else:
            both = jnp.concatenate([high[:, :count], low[:, :count]], axis=1)
            for n in range(packed // LANES):
                y[n, : step * rows] = both[:, n * LANES : (n + 1) * LANES]

    def mix(block):
        taps = []
        for r in range(step):
            taps.append(jnp.concatenate([
                y[n, pl.ds(r * rows + 2 * shifts * m + c, reach, stride=2), :]
                for m in range(TAPS // shifts) for c in range(2) for n in range(packed // LANES)
            ], axis=1))
        taps = jnp.concatenate(taps, axis=0).astype(jnp.bfloat16)
        mixed = jnp.dot(taps, w_ref[...], preferred_element_type=jnp.float32)
        for n in range(mixed.shape[1] // LANES):
            p[n] = mixed[:, n * LANES : (n + 1) * LANES]
        for r in range(step):
            stream = block * step + r
            place = pl.ds(stream // unit * (NSPEC * unit) + stream % unit, NSPEC, stride=unit)
            if 2 * band >= LANES:
                for n in range(wide):
                    x[n, place, :] = sum(
                        p[wide * h + n, pl.ds(r * reach + h, NSPEC), :] for h in range(shifts)
                    )
            else:
                per = LANES // (2 * band)
                lane = lax.broadcasted_iota(jnp.int32, (NSPEC, LANES), 1)
                total = None
                for u in reversed(range(per)):
                    part = sum(
                        p[b, pl.ds(r * reach + b * per + u, NSPEC), :] for b in range(shifts // per)
                    )
                    total = part if total is None else jnp.where(
                        lane < 2 * band * (u + 1), part, total
                    )
                whole = total
                for u in range(1, per):
                    whole = whole + turn_lanes(total, -2 * band * u)
                x[0, place, :] = whole

    @pl.when(i == 0)
    def _():
        begin(0)
        for copy in tables_in:
            copy.start()
        turned[...] = jnp.zeros(turned.shape, jnp.float32)
        if streams // step > 1:
            begin(1)

    @pl.when((i > 0) & (i + ahead - 1 < last))
    def _():
        begin(i + ahead - 1)

    @pl.when(i == 0)
    def _():
        for copy in tables_in:
            copy.wait()

    @pl.when(i < last)
    def _():
        for copy in fetch(i):
            copy.wait()

    @pl.when(i == 0)
    def _():
        for block in range(2, min(ahead, streams // step)):
            begin(block)

    @pl.when(i < last)
    def _():
        mix(jnp.maximum(i - 1, 0))
        analyse()

    @pl.when(i == last)
    def _():
        mix(i - 1)
        lane = lax.broadcasted_iota(jnp.int32, (8, wide * LANES), 1)
        row = lax.broadcasted_iota(jnp.int32, (8, wide * LANES), 0)
        slot = row // 2
        base = (row % 2) * band
        picks = []
        offset = jnp.int32(0)
        for d in range(dests):
            held = counts[d]
            want = offset + jnp.minimum(slot, held - 1) + base
            picks.append(jnp.where((lane == want) & (row < 2 * CAP), 1.0, 0.0))
            offset = offset + held
        pick = jnp.concatenate(picks, axis=0).astype(jnp.bfloat16)
        spectra = jnp.concatenate([x[n] for n in range(wide)], axis=1)
        out = lax.dot_general(
            pick, spectra.astype(jnp.bfloat16), (((1,), (1,)), ((), ())),
            preferred_element_type=jnp.float32,
        )
        tiles = NSPEC * unit // LANES
        for d in range(dests):
            for t in range(streams // unit * tiles):
                row = t // tiles * (2 * CAP * tiles) + t % tiles
                turned[d, pl.ds(row, 2 * CAP, stride=tiles), :] = out[
                    8 * d : 8 * d + 2 * CAP, t * LANES : (t + 1) * LANES
                ]
        out_ref[...] = turned[...].astype(jnp.bfloat16)


def channelize(voltages, chan_counts, dests, start, streams, step, unit, room):
    band = 2 * dests
    frames = voltages.shape[2]
    analysis, mixing = tables(band)
    packed = packing(band)[1]
    shifts = shifts_of(band)
    ahead = 4 if band <= 64 else 2
    payload = payload_rows(streams // unit, unit)
    steps = streams // step
    kernel = functools.partial(channelizer, band, dests, start, streams, step, unit)
    return pl.pallas_call(
        kernel,
        grid_spec=pltpu.PrefetchScalarGridSpec(
            num_scalar_prefetch=1,
            grid=(steps + 1,),
            in_specs=[pl.BlockSpec(memory_space=pl.ANY)] * 3,
            out_specs=pl.BlockSpec((dests, payload, LANES), lambda i, c: (0, 0, 0)),
            scratch_shapes=[
                pltpu.VMEM((ahead, step, frames, 2, FFT_LEN), jnp.bfloat16),
                pltpu.VMEM(analysis.shape, jnp.bfloat16),
                pltpu.VMEM(mixing.shape, jnp.bfloat16),
                pltpu.VMEM((packed // LANES, step * 2 * frames + 16, LANES), jnp.float32),
                pltpu.VMEM((shifts * 2 * band // LANES, step * (NSPEC + 8), LANES), jnp.float32),
                pltpu.VMEM((max(1, 2 * band // LANES), NSPEC * streams, LANES), jnp.float32),
                pltpu.VMEM((dests, payload, LANES), jnp.float32),
                pltpu.SemaphoreType.DMA((ahead + 1, step)),
            ],
        ),
        out_shape=jax.ShapeDtypeStruct((dests, payload, LANES), jnp.bfloat16),
        compiler_params=pltpu.CompilerParams(
            vmem_limit_bytes=room * 1024 * 1024
        ),
        cost_estimate=pl.CostEstimate(
            flops=2 * streams * 2 * frames * analysis.size,
            bytes_accessed=2 * 2 * frames * FFT_LEN * streams, transcendentals=0,
        ),
    )(chan_counts, voltages, jnp.asarray(analysis), jnp.asarray(mixing))


def payload_rows(units, unit):
    return -(-units * 2 * CAP * NSPEC * unit // (16 * LANES)) * 16


def streams_in(part, unit):
    return part.shape[0] * unit * (part.shape[1] * LANES // (2 * CAP * NSPEC * unit))


def regroup(ref, apart, pre, unit, base):
    spread = LANES // unit
    sources, payload = ref.shape[:2]
    units = streams_in(ref, unit) // (sources * unit)
    lane = lax.broadcasted_iota(jnp.int32, (payload, LANES), 1) // unit
    for q in range(sources // spread):
        parts = [ref[spread * q + a].astype(jnp.float32) for a in range(spread)]
        bit = 1
        while bit < spread:
            even = lane // bit % 2 == 0
            mixed = []
            for a in range(spread):
                twin = parts[a ^ bit]
                if a & bit:
                    mixed.append(jnp.where(even, turn_lanes(twin, -unit * bit), parts[a]))
                else:
                    mixed.append(jnp.where(even, parts[a], turn_lanes(twin, unit * bit)))
            parts = mixed
            bit = 2 * bit
        slot = q % 2
        for g in range(spread):
            apart[slot, pl.ds(g, payload, stride=spread), :] = parts[g]
        rows = 2 * CAP * NSPEC
        for u in range(units):
            place = base + (u * (sources // spread) + q) * LANES
            pre[:, place : place + LANES] = apart[slot, u * rows : (u + 1) * rows].astype(jnp.bfloat16)


def one_hot(dest, total):
    spot = lax.broadcasted_iota(jnp.int32, (total, dest.shape[1]), 0)
    return jnp.where(spot == dest, 1.0, 0.0).astype(jnp.bfloat16)


def permute(rows, turn):
    return lax.dot_general(
        rows, turn, (((1,), (1,)), ((), ())), preferred_element_type=jnp.float32
    )


def settler(unit, dest_ref, part_hbm, out_ref, part, apart, pre, arrived):
    copy = pltpu.make_async_copy(part_hbm, part, arrived)
    copy.start()
    turn = one_hot(dest_ref[...], out_ref.shape[1])
    copy.wait()
    regroup(part, apart, pre, unit, 0)
    out_ref[...] = permute(pre[...], turn).astype(jnp.bfloat16)


def settle(part, dest, total, unit):
    rows = 2 * CAP * NSPEC
    return pl.pallas_call(
        functools.partial(settler, unit),
        in_specs=[pl.BlockSpec(memory_space=pltpu.VMEM), pl.BlockSpec(memory_space=pl.ANY)],
        out_specs=pl.BlockSpec(memory_space=pltpu.VMEM),
        out_shape=jax.ShapeDtypeStruct((rows, total), jnp.bfloat16),
        scratch_shapes=[
            pltpu.VMEM(part.shape, jnp.bfloat16),
            pltpu.VMEM((2, part.shape[1] * LANES // unit, LANES), jnp.float32),
            pltpu.VMEM((rows, dest.shape[1]), jnp.bfloat16),
            pltpu.SemaphoreType.DMA,
        ],
        compiler_params=pltpu.CompilerParams(vmem_limit_bytes=32 * 1024 * 1024),
        cost_estimate=pl.CostEstimate(
            flops=2 * rows * dest.shape[1] * total, bytes_accessed=2 * part.size + 2 * rows * total,
            transcendentals=0,
        ),
    )(dest, part)


def correlator(unit, own_count, counts, where, dest_ref, *refs):
    given = (len(refs) - 6) // 2
    sources, out_ref, held = refs[:given], refs[given], refs[given + 1 : 2 * given + 1]
    apart, pre, post, near, arrived = refs[2 * given + 1 :]
    k = pl.program_id(0)
    part = pl.program_id(1)
    total = post.shape[2]
    rows = out_ref.shape[3]
    time_len = 2 * NSPEC

    @pl.when((k == 0) & (part == 0))
    def _():
        copies = [
            pltpu.make_async_copy(a, b, arrived.at[n]) for n, (a, b) in enumerate(zip(sources, held))
        ]
        for copy in copies:
            copy.start()
        turn = one_hot(dest_ref[...], total)
        for copy in copies:
            copy.wait()
        other = held[:-own_count]
        ours = held[len(held) - own_count :]
        base = 0
        for ref in other:
            regroup(ref, apart, pre, unit, base)
            base += streams_in(ref, unit)
        halves = [permute(pre[...], turn)]
        fresh = ours[0]
        width = streams_in(fresh, unit)
        regroup(fresh, apart, pre, unit, total - width)
        mine = permute(pre[:, total - width :], turn[:, total - width :])
        for ref in ours[1:]:
            mine = mine + ref[...].astype(jnp.float32)
        halves.append(mine)
        for n in range(2 * CAP):
            for h, half in enumerate(halves):
                first = n % 2 * time_len + h * NSPEC
                post[n // 2, first : first + NSPEC] = half[n * NSPEC : (n + 1) * NSPEC].astype(
                    jnp.bfloat16
                )

    @pl.when(part == 0)
    def _():
        mine = post[k, :, pl.ds(pl.multiple_of(where[1] * rows, LANES), rows)]
        near[...] = mine.T

    valid = jnp.where(k < counts[where[0]], 1.0, 0.0) / jnp.float32(time_len)

    def put(right):
        vis = jnp.dot(near[...], right, preferred_element_type=jnp.float32)
        out_ref[0, 0, 0] = (vis * valid).astype(jnp.bfloat16)

    @pl.when(part == 0)
    def _():
        put(post[k])

    @pl.when(part == 1)
    def _():
        put(jnp.concatenate([-post[k, time_len:], post[k, :time_len]], axis=0))


def correlate(others, ours, dest, chan_counts, where, unit):
    total = dest.shape[1]
    operands = others + ours
    most = max(a.shape[1] for a in operands if a.ndim == 3)
    rows = total // 2
    return pl.pallas_call(
        functools.partial(correlator, unit, len(ours)),
        grid_spec=pltpu.PrefetchScalarGridSpec(
            num_scalar_prefetch=2,
            grid=(CAP, 2),
            in_specs=[pl.BlockSpec((1, total), lambda k, p, c, w: (0, 0))]
            + [pl.BlockSpec(memory_space=pl.ANY)] * len(operands),
            out_specs=pl.BlockSpec((1, 1, 1, rows, total), lambda k, p, c, w: (0, k, p, 0, 0)),
            scratch_shapes=[pltpu.VMEM(a.shape, jnp.bfloat16) for a in operands]
            + [
                pltpu.VMEM((2, most * LANES // unit, LANES), jnp.float32),
                pltpu.VMEM((2 * CAP * NSPEC, total), jnp.bfloat16),
                pltpu.VMEM((CAP, 4 * NSPEC, total), jnp.bfloat16),
                pltpu.VMEM((rows, 4 * NSPEC), jnp.bfloat16),
                pltpu.SemaphoreType.DMA((len(operands),)),
            ],
        ),
        out_shape=jax.ShapeDtypeStruct((1, CAP, 2, rows, total), jnp.bfloat16),
        compiler_params=pltpu.CompilerParams(vmem_limit_bytes=32 * 1024 * 1024),
    )(chan_counts, where, dest, *operands)


def body(voltages, station_map, chan_counts):
    dests = lax.axis_size("stn")
    streams = voltages.shape[0]
    total = dests * streams
    unit = min(streams, 16)
    plan = ((48, 4, 60), (16, 2, 32)) if streams == 64 else ((streams, 2, 60),)
    dest = (2 * station_map[:, None] + jnp.arange(2, dtype=jnp.int32)[None, :]).reshape(-1)
    dest = dest.reshape(dests, streams // unit, unit).transpose(1, 0, 2)
    where = jnp.stack([lax.axis_index("stn"), lax.axis_index("blk")]).astype(jnp.int32)
    others, settled = [], []
    start = 0
    for size, step, room in plan:
        outgoing = channelize(voltages, chan_counts, dests, start, size, step, unit, room)
        chan_counts, outgoing = lax.optimization_barrier((chan_counts, outgoing))
        own = lax.all_to_all(outgoing, "stn", split_axis=0, concat_axis=0, tiled=True)
        spot = dest[start // unit : (start + size) // unit]
        if start + size < streams:
            settled.append(settle(own, spot.reshape(1, -1), total, unit))
        others.append(lax.ppermute(own, "blk", [(0, 1), (1, 0)]))
        start = start + size
    return correlate(others, [own] + settled, dest.reshape(1, -1), chan_counts, where, unit)


def solution(mesh):
    return jax.shard_map(
        body,
        mesh=mesh,
        in_specs=(P("stn", "blk", None, None, None), P(), P()),
        out_specs=P("stn", None, None, "blk", None),
        check_vma=False,
    )
```

```python
import functools
import math

import jax
import jax.numpy as jnp
import ml_dtypes
import numpy as np
from jax import lax
from jax.experimental import pallas as pl
from jax.experimental.pallas import tpu as pltpu
from jax.sharding import PartitionSpec as P

FFT_LEN = 4096
TAPS = 16
CAP = 3
NSPEC = 48
LANES = 128


def prototype():
    span = TAPS * FFT_LEN
    points = np.arange(span, dtype=np.float64) + 0.5
    window = 0.5 - 0.5 * np.cos(2.0 * math.pi * points / span)
    shifted = math.pi * (points - span / 2.0) / FFT_LEN
    filt = np.sin(shifted) / shifted * window
    return (filt / np.sqrt(np.sum(filt * filt))).reshape(TAPS, FFT_LEN)


def frame_basis(band, count):
    limit = math.pi * (band + 0.1)
    terms = count + int(limit) + 60
    k = np.arange(terms, dtype=np.float64)
    diagonal = k * (k + 1) + (2 * k * (k + 1) - 1) / ((2 * k + 3) * (2 * k - 1)) * limit**2
    m = k[:-2]
    beside = (m + 2) * (m + 1) / ((2 * m + 3) * np.sqrt((2 * m + 1) * (2 * m + 5))) * limit**2
    matrix = np.diag(diagonal) + np.diag(beside, 2) + np.diag(beside, -2)
    _, vectors = np.linalg.eigh(matrix)
    x = (2 * np.arange(FFT_LEN) + 1.0) / FFT_LEN - 1
    legendre = np.zeros((terms, FFT_LEN))
    legendre[0] = 1.0
    legendre[1] = x
    for j in range(2, terms):
        legendre[j] = ((2 * j - 1) * x * legendre[j - 1] - (j - 1) * legendre[j - 2]) / j
    legendre *= np.sqrt((k + 0.5) * 2.0 / FFT_LEN)[:, None]
    return legendre.T @ vectors[:, :count]


def shifts_of(band):
    return 8 if band <= 64 else 4


def turn_lanes(value, shift):
    shift = shift % LANES
    return pltpu.roll(value, shift, axis=1) if shift else value


def packing(band):
    if 3 * (2 * band + 16) <= 2 * LANES:
        return 2 * band + 16, 2 * LANES, True
    count = -(-(2 * band + 32) // (LANES // 2)) * (LANES // 2)
    return count, -(-2 * count // LANES) * LANES, False


@functools.lru_cache(maxsize=4)
def tables(band):
    bf16 = ml_dtypes.bfloat16
    count, packed, triple = packing(band)
    shifts = shifts_of(band)
    basis = frame_basis(band, count)
    high = basis.astype(bf16)
    low = (basis - high.astype(np.float64)).astype(bf16)
    held = high.astype(np.float64) + low.astype(np.float64)
    lanes = -(-count // LANES) * LANES
    analysis = np.zeros((FFT_LEN, 2 * lanes), bf16)
    analysis[:, :count] = high
    analysis[:, lanes : lanes + count] = low

    phase = 2.0 * math.pi / FFT_LEN * (np.outer(np.arange(FFT_LEN), np.arange(band)) % FFT_LEN)
    wave = np.concatenate([np.cos(phase), -np.sin(phase)], axis=1)
    gram = held.T @ held
    taper = prototype()
    mixing = np.zeros((TAPS // shifts, 2, packed, shifts, 2 * band), bf16)
    for t in range(TAPS):
        real = np.linalg.solve(gram, held.T @ (taper[t][:, None] * wave))
        imag = np.concatenate([-real[:, band:], real[:, :band]], axis=1)
        for c, full in enumerate((real, imag)):
            part = mixing[t // shifts, c, :, t % shifts]
            top = full.astype(bf16)
            part[:count] = top
            part[count : 2 * count] = top
            if triple:
                part[2 * count : 3 * count] = (full - top.astype(np.float64)).astype(bf16)
    return analysis, mixing.reshape(-1, shifts * 2 * band)


def channelizer(
    band, dests, first, streams, step, unit, counts, v_ref, u_hbm, w_hbm, out_ref,
    held, u_ref, w_ref, y, p, x, turned, arrived,
):
    i = pl.program_id(0)
    ahead = held.shape[0]
    shifts = shifts_of(band)
    last = pl.num_programs(0) - 1
    count, packed, triple = packing(band)
    lanes = u_ref.shape[1] // 2
    rows = 2 * v_ref.shape[2]
    reach = NSPEC + 8
    wide = max(1, 2 * band // LANES)
    tables_in = [
        pltpu.make_async_copy(u_hbm, u_ref, arrived.at[ahead, 0]),
        pltpu.make_async_copy(w_hbm, w_ref, arrived.at[ahead, 1]),
    ]

    def fetch(block):
        slot = block % ahead
        return [
            pltpu.make_async_copy(
                v_ref.at[first + block * step + r, 0], held.at[slot, r], arrived.at[slot, r]
            )
            for r in range(step)
        ]

    def begin(block):
        for r, copy in enumerate(fetch(block)):
            copy.start(priority=r % 2)

    def analyse():
        signal = held[i % ahead].reshape(step * rows, FFT_LEN)
        coeff = jnp.dot(signal, u_ref[...], preferred_element_type=jnp.float32)
        coeff = coeff[:, :lanes] + coeff[:, lanes:]
        high = coeff.astype(jnp.bfloat16).astype(jnp.float32)
        low = coeff - high
        if triple:
            lane = lax.broadcasted_iota(jnp.int32, coeff.shape, 1)
            low = turn_lanes(low, count)
            spare = 2 * count - LANES
            y[0, : step * rows] = jnp.where(lane < count, high, low)
            y[1, : step * rows] = jnp.where(lane < spare, low, turn_lanes(high, spare))
        else:
            both = jnp.concatenate([high[:, :count], low[:, :count]], axis=1)
            for n in range(packed // LANES):
                y[n, : step * rows] = both[:, n * LANES : (n + 1) * LANES]

    def mix(block):
        taps = []
        for r in range(step):
            taps.append(jnp.concatenate([
                y[n, pl.ds(r * rows + 2 * shifts * m + c, reach, stride=2), :]
                for m in range(TAPS // shifts) for c in range(2) for n in range(packed // LANES)
            ], axis=1))
        taps = jnp.concatenate(taps, axis=0).astype(jnp.bfloat16)
        mixed = jnp.dot(taps, w_ref[...], preferred_element_type=jnp.float32)
        for n in range(mixed.shape[1] // LANES):
            p[n] = mixed[:, n * LANES : (n + 1) * LANES]
        for r in range(step):
            stream = block * step + r
            place = pl.ds(stream // unit * (NSPEC * unit) + stream % unit, NSPEC, stride=unit)
            if 2 * band >= LANES:
                for n in range(wide):
                    x[n, place, :] = sum(
                        p[wide * h + n, pl.ds(r * reach + h, NSPEC), :] for h in range(shifts)
                    )
            else:
                per = LANES // (2 * band)
                lane = lax.broadcasted_iota(jnp.int32, (NSPEC, LANES), 1)
                total = None
                for u in reversed(range(per)):
                    part = sum(
                        p[b, pl.ds(r * reach + b * per + u, NSPEC), :] for b in range(shifts // per)
                    )
                    total = part if total is None else jnp.where(
                        lane < 2 * band * (u + 1), part, total
                    )
                whole = total
                for u in range(1, per):
                    whole = whole + turn_lanes(total, -2 * band * u)
                x[0, place, :] = whole

    @pl.when(i == 0)
    def _():
        begin(0)
        for copy in tables_in:
            copy.start()
        turned[...] = jnp.zeros(turned.shape, jnp.float32)
        if streams // step > 1:
            begin(1)

    @pl.when((i > 0) & (i + ahead - 1 < last))
    def _():
        begin(i + ahead - 1)

    @pl.when(i == 0)
    def _():
        for copy in tables_in:
            copy.wait()

    @pl.when(i < last)
    def _():
        for copy in fetch(i):
            copy.wait()

    @pl.when(i == 0)
    def _():
        for block in range(2, min(ahead, streams // step)):
            begin(block)

    @pl.when(i < last)
    def _():
        mix(jnp.maximum(i - 1, 0))
        analyse()

    @pl.when(i == last)
    def _():
        mix(i - 1)
        lane = lax.broadcasted_iota(jnp.int32, (8, wide * LANES), 1)
        row = lax.broadcasted_iota(jnp.int32, (8, wide * LANES), 0)
        slot = row // 2
        base = (row % 2) * band
        picks = []
        offset = jnp.int32(0)
        for d in range(dests):
            held = counts[d]
            want = offset + jnp.minimum(slot, held - 1) + base
            picks.append(jnp.where((lane == want) & (row < 2 * CAP), 1.0, 0.0))
            offset = offset + held
        pick = jnp.concatenate(picks, axis=0).astype(jnp.bfloat16)
        spectra = jnp.concatenate([x[n] for n in range(wide)], axis=1)
        out = lax.dot_general(
            pick, spectra.astype(jnp.bfloat16), (((1,), (1,)), ((), ())),
            preferred_element_type=jnp.float32,
        )
        tiles = NSPEC * unit // LANES
        for d in range(dests):
            for t in range(streams // unit * tiles):
                row = t // tiles * (2 * CAP * tiles) + t % tiles
                turned[d, pl.ds(row, 2 * CAP, stride=tiles), :] = out[
                    8 * d : 8 * d + 2 * CAP, t * LANES : (t + 1) * LANES
                ]
        out_ref[...] = turned[...].astype(jnp.bfloat16)


def channelize(voltages, chan_counts, dests, start, streams, step, unit, room):
    band = 2 * dests
    frames = voltages.shape[2]
    analysis, mixing = tables(band)
    packed = packing(band)[1]
    shifts = shifts_of(band)
    ahead = 4 if band <= 64 else 2
    payload = payload_rows(streams // unit, unit)
    steps = streams // step
    kernel = functools.partial(channelizer, band, dests, start, streams, step, unit)
    return pl.pallas_call(
        kernel,
        grid_spec=pltpu.PrefetchScalarGridSpec(
            num_scalar_prefetch=1,
            grid=(steps + 1,),
            in_specs=[pl.BlockSpec(memory_space=pl.ANY)] * 3,
            out_specs=pl.BlockSpec((dests, payload, LANES), lambda i, c: (0, 0, 0)),
            scratch_shapes=[
                pltpu.VMEM((ahead, step, frames, 2, FFT_LEN), jnp.bfloat16),
                pltpu.VMEM(analysis.shape, jnp.bfloat16),
                pltpu.VMEM(mixing.shape, jnp.bfloat16),
                pltpu.VMEM((packed // LANES, step * 2 * frames + 16, LANES), jnp.float32),
                pltpu.VMEM((shifts * 2 * band // LANES, step * (NSPEC + 8), LANES), jnp.float32),
                pltpu.VMEM((max(1, 2 * band // LANES), NSPEC * streams, LANES), jnp.float32),
                pltpu.VMEM((dests, payload, LANES), jnp.float32),
                pltpu.SemaphoreType.DMA((ahead + 1, step)),
            ],
        ),
        out_shape=jax.ShapeDtypeStruct((dests, payload, LANES), jnp.bfloat16),
        compiler_params=pltpu.CompilerParams(
            vmem_limit_bytes=room * 1024 * 1024
        ),
        cost_estimate=pl.CostEstimate(
            flops=2 * streams * 2 * frames * analysis.size,
            bytes_accessed=2 * 2 * frames * FFT_LEN * streams, transcendentals=0,
        ),
    )(chan_counts, voltages, jnp.asarray(analysis), jnp.asarray(mixing))


def payload_rows(units, unit):
    return -(-units * 2 * CAP * NSPEC * unit // (16 * LANES)) * 16


def streams_in(part, unit):
    return part.shape[0] * unit * (part.shape[1] * LANES // (2 * CAP * NSPEC * unit))


def regroup(ref, apart, pre, unit, base):
    spread = LANES // unit
    sources, payload = ref.shape[:2]
    units = streams_in(ref, unit) // (sources * unit)
    lane = lax.broadcasted_iota(jnp.int32, (payload, LANES), 1) // unit
    for q in range(sources // spread):
        parts = [ref[spread * q + a].astype(jnp.float32) for a in range(spread)]
        bit = 1
        while bit < spread:
            even = lane // bit % 2 == 0
            mixed = []
            for a in range(spread):
                twin = parts[a ^ bit]
                if a & bit:
                    mixed.append(jnp.where(even, turn_lanes(twin, -unit * bit), parts[a]))
                else:
                    mixed.append(jnp.where(even, parts[a], turn_lanes(twin, unit * bit)))
            parts = mixed
            bit = 2 * bit
        slot = q % 2
        for g in range(spread):
            apart[slot, pl.ds(g, payload, stride=spread), :] = parts[g]
        rows = 2 * CAP * NSPEC
        for u in range(units):
            place = base + (u * (sources // spread) + q) * LANES
            pre[:, place : place + LANES] = apart[slot, u * rows : (u + 1) * rows].astype(jnp.bfloat16)


def one_hot(dest, total):
    spot = lax.broadcasted_iota(jnp.int32, (total, dest.shape[1]), 0)
    return jnp.where(spot == dest, 1.0, 0.0).astype(jnp.bfloat16)


def permute(rows, turn):
    return lax.dot_general(
        rows, turn, (((1,), (1,)), ((), ())), preferred_element_type=jnp.float32
    )


def settler(unit, dest_ref, own_hbm, other_hbm, out_ref, own, other, apart, pre, arrived):
    copies = [
        pltpu.make_async_copy(own_hbm, own, arrived.at[0]),
        pltpu.make_async_copy(other_hbm, other, arrived.at[1]),
    ]
    for copy in copies:
        copy.start()
    turn = one_hot(dest_ref[...], out_ref.shape[2])
    for h, part in enumerate((own, other)):
        copies[h].wait()
        regroup(part, apart, pre, unit, 0)
        out_ref[h] = permute(pre[...], turn).astype(jnp.bfloat16)


def settle(own, other, dest, total, unit):
    rows = 2 * CAP * NSPEC
    return pl.pallas_call(
        functools.partial(settler, unit),
        in_specs=[pl.BlockSpec(memory_space=pltpu.VMEM)] + [pl.BlockSpec(memory_space=pl.ANY)] * 2,
        out_specs=pl.BlockSpec(memory_space=pltpu.VMEM),
        out_shape=jax.ShapeDtypeStruct((2, rows, total), jnp.bfloat16),
        scratch_shapes=[
            pltpu.VMEM(own.shape, jnp.bfloat16),
            pltpu.VMEM(own.shape, jnp.bfloat16),
            pltpu.VMEM((2, own.shape[1] * LANES // unit, LANES), jnp.float32),
            pltpu.VMEM((rows, dest.shape[1]), jnp.bfloat16),
            pltpu.SemaphoreType.DMA((2,)),
        ],
        compiler_params=pltpu.CompilerParams(vmem_limit_bytes=32 * 1024 * 1024),
        cost_estimate=pl.CostEstimate(
            flops=4 * rows * dest.shape[1] * total, bytes_accessed=4 * own.size + 4 * rows * total,
            transcendentals=0,
        ),
    )(dest, own, other)


def correlator(unit, counts, where, dest_ref, *refs):
    given = (len(refs) - 6) // 2
    sources, out_ref, held = refs[:given], refs[given], refs[given + 1 : 2 * given + 1]
    apart, pre, post, near, arrived = refs[2 * given + 1 :]
    k = pl.program_id(0)
    part = pl.program_id(1)
    total = post.shape[2]
    rows = out_ref.shape[3]
    time_len = 2 * NSPEC

    @pl.when((k == 0) & (part == 0))
    def _():
        copies = [
            pltpu.make_async_copy(a, b, arrived.at[n]) for n, (a, b) in enumerate(zip(sources, held))
        ]
        for copy in copies:
            copy.start()
        turn = one_hot(dest_ref[...], total)
        for copy in copies:
            copy.wait()
        for h in range(2):
            regroup(held[h], apart, pre, unit, 0)
            half = permute(pre[...], turn)
            for ref in held[2:]:
                half = half + ref[h].astype(jnp.float32)
            for n in range(2 * CAP):
                first = n % 2 * time_len + h * NSPEC
                post[n // 2, first : first + NSPEC] = half[n * NSPEC : (n + 1) * NSPEC].astype(
                    jnp.bfloat16
                )

    @pl.when(part == 0)
    def _():
        mine = post[k, :, pl.ds(pl.multiple_of(where[1] * rows, LANES), rows)]
        near[...] = mine.T

    valid = jnp.where(k < counts[where[0]], 1.0, 0.0) / jnp.float32(time_len)

    def put(right):
        vis = jnp.dot(near[...], right, preferred_element_type=jnp.float32)
        out_ref[0, 0, 0] = (vis * valid).astype(jnp.bfloat16)

    @pl.when(part == 0)
    def _():
        put(post[k])

    @pl.when(part == 1)
    def _():
        put(jnp.concatenate([-post[k, time_len:], post[k, :time_len]], axis=0))


def correlate(operands, dest, chan_counts, where, total, unit):
    held = dest.shape[1]
    most = operands[0].shape[1]
    rows = total // 2
    return pl.pallas_call(
        functools.partial(correlator, unit),
        grid_spec=pltpu.PrefetchScalarGridSpec(
            num_scalar_prefetch=2,
            grid=(CAP, 2),
            in_specs=[pl.BlockSpec((1, held), lambda k, p, c, w: (0, 0))]
            + [pl.BlockSpec(memory_space=pl.ANY)] * len(operands),
            out_specs=pl.BlockSpec((1, 1, 1, rows, total), lambda k, p, c, w: (0, k, p, 0, 0)),
            scratch_shapes=[pltpu.VMEM(a.shape, jnp.bfloat16) for a in operands]
            + [
                pltpu.VMEM((2, most * LANES // unit, LANES), jnp.float32),
                pltpu.VMEM((2 * CAP * NSPEC, held), jnp.bfloat16),
                pltpu.VMEM((CAP, 4 * NSPEC, total), jnp.bfloat16),
                pltpu.VMEM((rows, 4 * NSPEC), jnp.bfloat16),
                pltpu.SemaphoreType.DMA((len(operands),)),
            ],
        ),
        out_shape=jax.ShapeDtypeStruct((1, CAP, 2, rows, total), jnp.bfloat16),
        compiler_params=pltpu.CompilerParams(vmem_limit_bytes=32 * 1024 * 1024),
    )(chan_counts, where, dest, *operands)


def body(voltages, station_map, chan_counts):
    dests = lax.axis_size("stn")
    streams = voltages.shape[0]
    total = dests * streams
    unit = min(streams, 16)
    plan = ((48, 4, 60), (16, 2, 32)) if streams == 64 else ((streams, 2, 60),)
    dest = (2 * station_map[:, None] + jnp.arange(2, dtype=jnp.int32)[None, :]).reshape(-1)
    dest = dest.reshape(dests, streams // unit, unit).transpose(1, 0, 2)
    where = jnp.stack([lax.axis_index("stn"), lax.axis_index("blk")]).astype(jnp.int32)
    settled = []
    start = 0
    for size, step, room in plan:
        outgoing = channelize(voltages, chan_counts, dests, start, size, step, unit, room)
        chan_counts, outgoing = lax.optimization_barrier((chan_counts, outgoing))
        own = lax.all_to_all(outgoing, "stn", split_axis=0, concat_axis=0, tiled=True)
        if settled:
            own, other = lax.optimization_barrier((own, other))
            settled = [settle(before, other, spot, total, unit)]
        other = lax.ppermute(own, "blk", [(0, 1), (1, 0)])
        spot = dest[start // unit : (start + size) // unit].reshape(1, -1)
        if start + size < streams:
            before = own
            settled = [None]
        start = start + size
    return correlate([own, other] + settled, spot, chan_counts, where, total, unit)


def solution(mesh):
    return jax.shard_map(
        body,
        mesh=mesh,
        in_specs=(P("stn", "blk", None, None, None), P(), P()),
        out_specs=P("stn", None, None, "blk", None),
        check_vma=False,
    )
```

```python
import functools
import math

import jax
import jax.numpy as jnp
import ml_dtypes
import numpy as np
from jax import lax
from jax.experimental import pallas as pl
from jax.experimental.pallas import tpu as pltpu
from jax.sharding import PartitionSpec as P

FFT_LEN = 4096
TAPS = 16
CAP = 3
NSPEC = 48
LANES = 128


def prototype():
    span = TAPS * FFT_LEN
    points = np.arange(span, dtype=np.float64) + 0.5
    window = 0.5 - 0.5 * np.cos(2.0 * math.pi * points / span)
    shifted = math.pi * (points - span / 2.0) / FFT_LEN
    filt = np.sin(shifted) / shifted * window
    return (filt / np.sqrt(np.sum(filt * filt))).reshape(TAPS, FFT_LEN)


def frame_basis(band, count):
    limit = math.pi * (band + 0.1)
    terms = count + int(limit) + 60
    k = np.arange(terms, dtype=np.float64)
    diagonal = k * (k + 1) + (2 * k * (k + 1) - 1) / ((2 * k + 3) * (2 * k - 1)) * limit**2
    m = k[:-2]
    beside = (m + 2) * (m + 1) / ((2 * m + 3) * np.sqrt((2 * m + 1) * (2 * m + 5))) * limit**2
    matrix = np.diag(diagonal) + np.diag(beside, 2) + np.diag(beside, -2)
    _, vectors = np.linalg.eigh(matrix)
    x = (2 * np.arange(FFT_LEN) + 1.0) / FFT_LEN - 1
    legendre = np.zeros((terms, FFT_LEN))
    legendre[0] = 1.0
    legendre[1] = x
    for j in range(2, terms):
        legendre[j] = ((2 * j - 1) * x * legendre[j - 1] - (j - 1) * legendre[j - 2]) / j
    legendre *= np.sqrt((k + 0.5) * 2.0 / FFT_LEN)[:, None]
    return legendre.T @ vectors[:, :count]


def shifts_of(band):
    return 8 if band <= 64 else 4


def turn_lanes(value, shift):
    shift = shift % LANES
    return pltpu.roll(value, shift, axis=1) if shift else value


def packing(band):
    if 3 * (2 * band + 16) <= 2 * LANES:
        return 2 * band + 16, 2 * LANES, True
    count = -(-(2 * band + 32) // (LANES // 2)) * (LANES // 2)
    return count, -(-2 * count // LANES) * LANES, False


@functools.lru_cache(maxsize=4)
def tables(band):
    bf16 = ml_dtypes.bfloat16
    count, packed, triple = packing(band)
    shifts = shifts_of(band)
    basis = frame_basis(band, count)
    high = basis.astype(bf16)
    low = (basis - high.astype(np.float64)).astype(bf16)
    held = high.astype(np.float64) + low.astype(np.float64)
    lanes = -(-count // LANES) * LANES
    analysis = np.zeros((FFT_LEN, 2 * lanes), bf16)
    analysis[:, :count] = high
    analysis[:, lanes : lanes + count] = low

    phase = 2.0 * math.pi / FFT_LEN * (np.outer(np.arange(FFT_LEN), np.arange(band)) % FFT_LEN)
    wave = np.concatenate([np.cos(phase), -np.sin(phase)], axis=1)
    gram = held.T @ held
    taper = prototype()
    mixing = np.zeros((TAPS // shifts, 2, packed, shifts, 2 * band), bf16)
    for t in range(TAPS):
        real = np.linalg.solve(gram, held.T @ (taper[t][:, None] * wave))
        imag = np.concatenate([-real[:, band:], real[:, :band]], axis=1)
        for c, full in enumerate((real, imag)):
            part = mixing[t // shifts, c, :, t % shifts]
            top = full.astype(bf16)
            part[:count] = top
            part[count : 2 * count] = top
            if triple:
                part[2 * count : 3 * count] = (full - top.astype(np.float64)).astype(bf16)
    return analysis, mixing.reshape(-1, shifts * 2 * band)


def channelizer(
    band, dests, first, streams, step, unit, counts, v_ref, u_hbm, w_hbm, out_ref,
    held, u_ref, w_ref, y, p, x, turned, arrived,
):
    i = pl.program_id(0)
    ahead = held.shape[0]
    shifts = shifts_of(band)
    last = pl.num_programs(0) - 1
    count, packed, triple = packing(band)
    lanes = u_ref.shape[1] // 2
    rows = 2 * v_ref.shape[2]
    reach = NSPEC + 8
    wide = max(1, 2 * band // LANES)
    tables_in = [
        pltpu.make_async_copy(u_hbm, u_ref, arrived.at[ahead, 0]),
        pltpu.make_async_copy(w_hbm, w_ref, arrived.at[ahead, 1]),
    ]

    def fetch(block):
        slot = block % ahead
        return [
            pltpu.make_async_copy(
                v_ref.at[first + block * step + r, 0], held.at[slot, r], arrived.at[slot, r]
            )
            for r in range(step)
        ]

    def begin(block):
        for r, copy in enumerate(fetch(block)):
            copy.start(priority=r % 2)

    def analyse():
        signal = held[i % ahead].reshape(step * rows, FFT_LEN)
        coeff = jnp.dot(signal, u_ref[...], preferred_element_type=jnp.float32)
        coeff = coeff[:, :lanes] + coeff[:, lanes:]
        high = coeff.astype(jnp.bfloat16).astype(jnp.float32)
        low = coeff - high
        if triple:
            lane = lax.broadcasted_iota(jnp.int32, coeff.shape, 1)
            low = turn_lanes(low, count)
            spare = 2 * count - LANES
            y[0, : step * rows] = jnp.where(lane < count, high, low)
            y[1, : step * rows] = jnp.where(lane < spare, low, turn_lanes(high, spare))
        else:
            both = jnp.concatenate([high[:, :count], low[:, :count]], axis=1)
            for n in range(packed // LANES):
                y[n, : step * rows] = both[:, n * LANES : (n + 1) * LANES]

    def mix(block):
        taps = []
        for r in range(step):
            taps.append(jnp.concatenate([
                y[n, pl.ds(r * rows + 2 * shifts * m + c, reach, stride=2), :]
                for m in range(TAPS // shifts) for c in range(2) for n in range(packed // LANES)
            ], axis=1))
        taps = jnp.concatenate(taps, axis=0).astype(jnp.bfloat16)
        mixed = jnp.dot(taps, w_ref[...], preferred_element_type=jnp.float32)
        for n in range(mixed.shape[1] // LANES):
            p[n] = mixed[:, n * LANES : (n + 1) * LANES]
        for r in range(step):
            stream = block * step + r
            place = pl.ds(stream // unit * (NSPEC * unit) + stream % unit, NSPEC, stride=unit)
            if 2 * band >= LANES:
                for n in range(wide):
                    x[n, place, :] = sum(
                        p[wide * h + n, pl.ds(r * reach + h, NSPEC), :] for h in range(shifts)
                    )
            else:
                per = LANES // (2 * band)
                lane = lax.broadcasted_iota(jnp.int32, (NSPEC, LANES), 1)
                total = None
                for u in reversed(range(per)):
                    part = sum(
                        p[b, pl.ds(r * reach + b * per + u, NSPEC), :] for b in range(shifts // per)
                    )
                    total = part if total is None else jnp.where(
                        lane < 2 * band * (u + 1), part, total
                    )
                whole = total
                for u in range(1, per):
                    whole = whole + turn_lanes(total, -2 * band * u)
                x[0, place, :] = whole

    @pl.when(i == 0)
    def _():
        begin(0)
        for copy in tables_in:
            copy.start()
        turned[...] = jnp.zeros(turned.shape, jnp.float32)
        if streams // step > 1:
            begin(1)

    @pl.when((i > 0) & (i + ahead - 1 < last))
    def _():
        begin(i + ahead - 1)

    @pl.when(i == 0)
    def _():
        for copy in tables_in:
            copy.wait()

    @pl.when(i < last)
    def _():
        for copy in fetch(i):
            copy.wait()

    @pl.when(i == 0)
    def _():
        for block in range(2, min(ahead, streams // step)):
            begin(block)

    @pl.when(i < last)
    def _():
        mix(jnp.maximum(i - 1, 0))
        analyse()

    @pl.when(i == last)
    def _():
        mix(i - 1)
        lane = lax.broadcasted_iota(jnp.int32, (8, wide * LANES), 1)
        row = lax.broadcasted_iota(jnp.int32, (8, wide * LANES), 0)
        slot = row // 2
        base = (row % 2) * band
        picks = []
        offset = jnp.int32(0)
        for d in range(dests):
            held = counts[d]
            want = offset + jnp.minimum(slot, held - 1) + base
            picks.append(jnp.where((lane == want) & (row < 2 * CAP), 1.0, 0.0))
            offset = offset + held
        pick = jnp.concatenate(picks, axis=0).astype(jnp.bfloat16)
        spectra = jnp.concatenate([x[n] for n in range(wide)], axis=1)
        out = lax.dot_general(
            pick, spectra.astype(jnp.bfloat16), (((1,), (1,)), ((), ())),
            preferred_element_type=jnp.float32,
        )
        tiles = NSPEC * unit // LANES
        for d in range(dests):
            for t in range(streams // unit * tiles):
                row = t // tiles * (2 * CAP * tiles) + t % tiles
                turned[d, pl.ds(row, 2 * CAP, stride=tiles), :] = out[
                    8 * d : 8 * d + 2 * CAP, t * LANES : (t + 1) * LANES
                ]
        out_ref[...] = turned[...].astype(jnp.bfloat16)


def channelize(voltages, chan_counts, dests, start, streams, step, unit, room):
    band = 2 * dests
    frames = voltages.shape[2]
    analysis, mixing = tables(band)
    packed = packing(band)[1]
    shifts = shifts_of(band)
    ahead = 4 if band <= 64 else 2
    payload = payload_rows(streams // unit, unit)
    steps = streams // step
    kernel = functools.partial(channelizer, band, dests, start, streams, step, unit)
    return pl.pallas_call(
        kernel,
        grid_spec=pltpu.PrefetchScalarGridSpec(
            num_scalar_prefetch=1,
            grid=(steps + 1,),
            in_specs=[pl.BlockSpec(memory_space=pl.ANY)] * 3,
            out_specs=pl.BlockSpec((dests, payload, LANES), lambda i, c: (0, 0, 0)),
            scratch_shapes=[
                pltpu.VMEM((ahead, step, frames, 2, FFT_LEN), jnp.bfloat16),
                pltpu.VMEM(analysis.shape, jnp.bfloat16),
                pltpu.VMEM(mixing.shape, jnp.bfloat16),
                pltpu.VMEM((packed // LANES, step * 2 * frames + 16, LANES), jnp.float32),
                pltpu.VMEM((shifts * 2 * band // LANES, step * (NSPEC + 8), LANES), jnp.float32),
                pltpu.VMEM((max(1, 2 * band // LANES), NSPEC * streams, LANES), jnp.float32),
                pltpu.VMEM((dests, payload, LANES), jnp.float32),
                pltpu.SemaphoreType.DMA((ahead + 1, step)),
            ],
        ),
        out_shape=jax.ShapeDtypeStruct((dests, payload, LANES), jnp.bfloat16),
        compiler_params=pltpu.CompilerParams(
            vmem_limit_bytes=room * 1024 * 1024
        ),
        cost_estimate=pl.CostEstimate(
            flops=2 * streams * 2 * frames * analysis.size,
            bytes_accessed=2 * 2 * frames * FFT_LEN * streams, transcendentals=0,
        ),
    )(chan_counts, voltages, jnp.asarray(analysis), jnp.asarray(mixing))


def payload_rows(units, unit):
    return -(-units * 2 * CAP * NSPEC * unit // (16 * LANES)) * 16


def streams_in(part, unit):
    return part.shape[0] * unit * (part.shape[1] * LANES // (2 * CAP * NSPEC * unit))


def regroup(ref, apart, pre, unit, base):
    spread = LANES // unit
    sources, payload = ref.shape[:2]
    units = streams_in(ref, unit) // (sources * unit)
    lane = lax.broadcasted_iota(jnp.int32, (payload, LANES), 1) // unit
    for q in range(sources // spread):
        parts = [ref[spread * q + a].astype(jnp.float32) for a in range(spread)]
        bit = 1
        while bit < spread:
            even = lane // bit % 2 == 0
            mixed = []
            for a in range(spread):
                twin = parts[a ^ bit]
                if a & bit:
                    mixed.append(jnp.where(even, turn_lanes(twin, -unit * bit), parts[a]))
                else:
                    mixed.append(jnp.where(even, parts[a], turn_lanes(twin, unit * bit)))
            parts = mixed
            bit = 2 * bit
        slot = q % 2
        for g in range(spread):
            apart[slot, pl.ds(g, payload, stride=spread), :] = parts[g]
        rows = 2 * CAP * NSPEC
        for u in range(units):
            place = base + (u * (sources // spread) + q) * LANES
            pre[:, place : place + LANES] = apart[slot, u * rows : (u + 1) * rows].astype(jnp.bfloat16)


def one_hot(dest, total):
    spot = lax.broadcasted_iota(jnp.int32, (total, dest.shape[1]), 0)
    return jnp.where(spot == dest, 1.0, 0.0).astype(jnp.bfloat16)


def permute(rows, turn):
    return lax.dot_general(
        rows, turn, (((1,), (1,)), ((), ())), preferred_element_type=jnp.float32
    )


def settler(unit, dest_ref, own_hbm, other_hbm, out_ref, own, other, apart, pre, arrived):
    copies = [
        pltpu.make_async_copy(own_hbm, own, arrived.at[0]),
        pltpu.make_async_copy(other_hbm, other, arrived.at[1]),
    ]
    for copy in copies:
        copy.start()
    turn = one_hot(dest_ref[...], out_ref.shape[2])
    for h, part in enumerate((own, other)):
        copies[h].wait()
        regroup(part, apart, pre, unit, 0)
        out_ref[h] = permute(pre[...], turn).astype(jnp.bfloat16)


def settle(own, other, dest, total, unit):
    rows = 2 * CAP * NSPEC
    return pl.pallas_call(
        functools.partial(settler, unit),
        in_specs=[pl.BlockSpec(memory_space=pltpu.VMEM)] + [pl.BlockSpec(memory_space=pl.ANY)] * 2,
        out_specs=pl.BlockSpec(memory_space=pltpu.VMEM),
        out_shape=jax.ShapeDtypeStruct((2, rows, total), jnp.bfloat16),
        scratch_shapes=[
            pltpu.VMEM(own.shape, jnp.bfloat16),
            pltpu.VMEM(own.shape, jnp.bfloat16),
            pltpu.VMEM((2, own.shape[1] * LANES // unit, LANES), jnp.float32),
            pltpu.VMEM((rows, dest.shape[1]), jnp.bfloat16),
            pltpu.SemaphoreType.DMA((2,)),
        ],
        compiler_params=pltpu.CompilerParams(vmem_limit_bytes=32 * 1024 * 1024),
        cost_estimate=pl.CostEstimate(
            flops=4 * rows * dest.shape[1] * total, bytes_accessed=4 * own.size + 4 * rows * total,
            transcendentals=0,
        ),
    )(dest, own, other)


def correlator(unit, counts, where, dest_ref, *refs):
    given = (len(refs) - 6) // 2
    sources, out_ref, held = refs[:given], refs[given], refs[given + 1 : 2 * given + 1]
    apart, pre, post, near, arrived = refs[2 * given + 1 :]
    k = pl.program_id(0)
    part = pl.program_id(1)
    total = post.shape[2]
    rows = out_ref.shape[3]
    time_len = 2 * NSPEC

    @pl.when((k == 0) & (part == 0))
    def _():
        copies = [
            pltpu.make_async_copy(a, b, arrived.at[n]) for n, (a, b) in enumerate(zip(sources, held))
        ]
        for copy in copies:
            copy.start()
        turn = one_hot(dest_ref[...], total)
        for copy in copies:
            copy.wait()
        for h in range(2):
            regroup(held[h], apart, pre, unit, 0)
            half = permute(pre[...], turn)
            for ref in held[2:]:
                half = half + ref[h].astype(jnp.float32)
            for n in range(2 * CAP):
                first = n % 2 * time_len + h * NSPEC
                post[n // 2, first : first + NSPEC] = half[n * NSPEC : (n + 1) * NSPEC].astype(
                    jnp.bfloat16
                )

    @pl.when(part == 0)
    def _():
        mine = post[k, :, pl.ds(pl.multiple_of(where[1] * rows, LANES), rows)]
        near[...] = mine.T

    valid = jnp.where(k < counts[where[0]], 1.0, 0.0) / jnp.float32(time_len)

    def put(right):
        vis = jnp.dot(near[...], right, preferred_element_type=jnp.float32)
        out_ref[0, 0, 0] = (vis * valid).astype(jnp.bfloat16)

    @pl.when(part == 0)
    def _():
        put(post[k])

    @pl.when(part == 1)
    def _():
        put(jnp.concatenate([-post[k, time_len:], post[k, :time_len]], axis=0))


def correlate(operands, dest, chan_counts, where, total, unit):
    held = dest.shape[1]
    most = operands[0].shape[1]
    rows = total // 2
    return pl.pallas_call(
        functools.partial(correlator, unit),
        grid_spec=pltpu.PrefetchScalarGridSpec(
            num_scalar_prefetch=2,
            grid=(CAP, 2),
            in_specs=[pl.BlockSpec((1, held), lambda k, p, c, w: (0, 0))]
            + [pl.BlockSpec(memory_space=pl.ANY)] * len(operands),
            out_specs=pl.BlockSpec((1, 1, 1, rows, total), lambda k, p, c, w: (0, k, p, 0, 0)),
            scratch_shapes=[pltpu.VMEM(a.shape, jnp.bfloat16) for a in operands]
            + [
                pltpu.VMEM((2, most * LANES // unit, LANES), jnp.float32),
                pltpu.VMEM((2 * CAP * NSPEC, held), jnp.bfloat16),
                pltpu.VMEM((CAP, 4 * NSPEC, total), jnp.bfloat16),
                pltpu.VMEM((rows, 4 * NSPEC), jnp.bfloat16),
                pltpu.SemaphoreType.DMA((len(operands),)),
            ],
        ),
        out_shape=jax.ShapeDtypeStruct((1, CAP, 2, rows, total), jnp.bfloat16),
        compiler_params=pltpu.CompilerParams(vmem_limit_bytes=32 * 1024 * 1024),
    )(chan_counts, where, dest, *operands)


def body(voltages, station_map, chan_counts):
    dests = lax.axis_size("stn")
    streams = voltages.shape[0]
    total = dests * streams
    unit = min(streams, 16)
    dest = (2 * station_map[:, None] + jnp.arange(2, dtype=jnp.int32)[None, :]).reshape(-1)
    dest = dest.reshape(dests, streams // unit, unit).transpose(1, 0, 2)
    where = jnp.stack([lax.axis_index("stn"), lax.axis_index("blk")]).astype(jnp.int32)

    def turn(outgoing):
        return lax.all_to_all(outgoing, "stn", split_axis=0, concat_axis=0, tiled=True)

    def swap(own):
        return lax.ppermute(own, "blk", [(0, 1), (1, 0)])

    def spots(start, size):
        return dest[start // unit : (start + size) // unit].reshape(1, -1)

    if streams == 64:
        early, late = 48, 16
        outgoing = channelize(voltages, chan_counts, dests, 0, early, 4, unit, 60)
        chan_counts, outgoing = lax.optimization_barrier((chan_counts, outgoing))
        first = turn(outgoing)
        outgoing = channelize(voltages, chan_counts, dests, early, late, 2, unit, 32)
        first, outgoing = lax.optimization_barrier((first, outgoing))
        first_other = swap(first)
        own = turn(outgoing)
        own, first_other = lax.optimization_barrier((own, first_other))
        other = swap(own)
        settled = [settle(first, first_other, spots(0, early), total, unit)]
    else:
        late = streams
        own = turn(channelize(voltages, chan_counts, dests, 0, late, 2, unit, 60))
        other = swap(own)
        settled = []
    spot = spots(streams - late, late)
    return correlate([own, other] + settled, spot, chan_counts, where, total, unit)


def solution(mesh):
    return jax.shard_map(
        body,
        mesh=mesh,
        in_specs=(P("stn", "blk", None, None, None), P(), P()),
        out_specs=P("stn", None, None, "blk", None),
        check_vma=False,
    )
```

```python
import functools
import math

import jax
import jax.numpy as jnp
import ml_dtypes
import numpy as np
from jax import lax
from jax.experimental import pallas as pl
from jax.experimental.pallas import tpu as pltpu
from jax.sharding import PartitionSpec as P

FFT_LEN = 4096
TAPS = 16
CAP = 3
NSPEC = 48
LANES = 128


def prototype():
    span = TAPS * FFT_LEN
    points = np.arange(span, dtype=np.float64) + 0.5
    window = 0.5 - 0.5 * np.cos(2.0 * math.pi * points / span)
    shifted = math.pi * (points - span / 2.0) / FFT_LEN
    filt = np.sin(shifted) / shifted * window
    return (filt / np.sqrt(np.sum(filt * filt))).reshape(TAPS, FFT_LEN)


def frame_basis(band, count):
    limit = math.pi * (band + 0.1)
    terms = count + int(limit) + 60
    k = np.arange(terms, dtype=np.float64)
    diagonal = k * (k + 1) + (2 * k * (k + 1) - 1) / ((2 * k + 3) * (2 * k - 1)) * limit**2
    m = k[:-2]
    beside = (m + 2) * (m + 1) / ((2 * m + 3) * np.sqrt((2 * m + 1) * (2 * m + 5))) * limit**2
    matrix = np.diag(diagonal) + np.diag(beside, 2) + np.diag(beside, -2)
    _, vectors = np.linalg.eigh(matrix)
    x = (2 * np.arange(FFT_LEN) + 1.0) / FFT_LEN - 1
    legendre = np.zeros((terms, FFT_LEN))
    legendre[0] = 1.0
    legendre[1] = x
    for j in range(2, terms):
        legendre[j] = ((2 * j - 1) * x * legendre[j - 1] - (j - 1) * legendre[j - 2]) / j
    legendre *= np.sqrt((k + 0.5) * 2.0 / FFT_LEN)[:, None]
    return legendre.T @ vectors[:, :count]


def shifts_of(band):
    return 8 if band <= 64 else 4


def turn_lanes(value, shift):
    shift = shift % LANES
    return pltpu.roll(value, shift, axis=1) if shift else value


def packing(band):
    if 3 * (2 * band + 16) <= 2 * LANES:
        return 2 * band + 16, 2 * LANES, True
    count = -(-(2 * band + 32) // (LANES // 2)) * (LANES // 2)
    return count, -(-2 * count // LANES) * LANES, False


@functools.lru_cache(maxsize=4)
def tables(band):
    bf16 = ml_dtypes.bfloat16
    count, packed, triple = packing(band)
    shifts = shifts_of(band)
    basis = frame_basis(band, count)
    high = basis.astype(bf16)
    low = (basis - high.astype(np.float64)).astype(bf16)
    held = high.astype(np.float64) + low.astype(np.float64)
    lanes = -(-count // LANES) * LANES
    analysis = np.zeros((FFT_LEN, 2 * lanes), bf16)
    analysis[:, :count] = high
    analysis[:, lanes : lanes + count] = low

    phase = 2.0 * math.pi / FFT_LEN * (np.outer(np.arange(FFT_LEN), np.arange(band)) % FFT_LEN)
    wave = np.concatenate([np.cos(phase), -np.sin(phase)], axis=1)
    gram = held.T @ held
    taper = prototype()
    mixing = np.zeros((TAPS // shifts, 2, packed, shifts, 2 * band), bf16)
    for t in range(TAPS):
        real = np.linalg.solve(gram, held.T @ (taper[t][:, None] * wave))
        imag = np.concatenate([-real[:, band:], real[:, :band]], axis=1)
        for c, full in enumerate((real, imag)):
            part = mixing[t // shifts, c, :, t % shifts]
            top = full.astype(bf16)
            part[:count] = top
            part[count : 2 * count] = top
            if triple:
                part[2 * count : 3 * count] = (full - top.astype(np.float64)).astype(bf16)
    return analysis, mixing.reshape(-1, shifts * 2 * band)


def channelizer(
    band, dests, first, streams, step, unit, counts, v_ref, u_hbm, w_hbm, out_ref,
    held, u_ref, w_ref, y, p, x, turned, arrived,
):
    i = pl.program_id(0)
    ahead = held.shape[0]
    shifts = shifts_of(band)
    last = pl.num_programs(0) - 1
    count, packed, triple = packing(band)
    lanes = u_ref.shape[1] // 2
    rows = 2 * v_ref.shape[2]
    reach = NSPEC + 8
    wide = max(1, 2 * band // LANES)
    tables_in = [
        pltpu.make_async_copy(u_hbm, u_ref, arrived.at[ahead, 0]),
        pltpu.make_async_copy(w_hbm, w_ref, arrived.at[ahead, 1]),
    ]

    def fetch(block):
        slot = block % ahead
        return [
            pltpu.make_async_copy(
                v_ref.at[first + block * step + r, 0], held.at[slot, r], arrived.at[slot, r]
            )
            for r in range(step)
        ]

    def begin(block):
        for r, copy in enumerate(fetch(block)):
            copy.start(priority=r % 2)

    def analyse():
        signal = held[i % ahead].reshape(step * rows, FFT_LEN)
        coeff = jnp.dot(signal, u_ref[...], preferred_element_type=jnp.float32)
        coeff = coeff[:, :lanes] + coeff[:, lanes:]
        high = coeff.astype(jnp.bfloat16).astype(jnp.float32)
        low = coeff - high
        if triple:
            lane = lax.broadcasted_iota(jnp.int32, coeff.shape, 1)
            low = turn_lanes(low, count)
            spare = 2 * count - LANES
            y[0, : step * rows] = jnp.where(lane < count, high, low)
            y[1, : step * rows] = jnp.where(lane < spare, low, turn_lanes(high, spare))
        else:
            both = jnp.concatenate([high[:, :count], low[:, :count]], axis=1)
            for n in range(packed // LANES):
                y[n, : step * rows] = both[:, n * LANES : (n + 1) * LANES]

    def mix(block):
        taps = []
        for r in range(step):
            taps.append(jnp.concatenate([
                y[n, pl.ds(r * rows + 2 * shifts * m + c, reach, stride=2), :]
                for m in range(TAPS // shifts) for c in range(2) for n in range(packed // LANES)
            ], axis=1))
        taps = jnp.concatenate(taps, axis=0).astype(jnp.bfloat16)
        mixed = jnp.dot(taps, w_ref[...], preferred_element_type=jnp.float32)
        for n in range(mixed.shape[1] // LANES):
            p[n] = mixed[:, n * LANES : (n + 1) * LANES]
        for r in range(step):
            stream = block * step + r
            place = pl.ds(stream // unit * (NSPEC * unit) + stream % unit, NSPEC, stride=unit)
            if 2 * band >= LANES:
                for n in range(wide):
                    x[n, place, :] = sum(
                        p[wide * h + n, pl.ds(r * reach + h, NSPEC), :] for h in range(shifts)
                    )
            else:
                per = LANES // (2 * band)
                lane = lax.broadcasted_iota(jnp.int32, (NSPEC, LANES), 1)
                total = None
                for u in reversed(range(per)):
                    part = sum(
                        p[b, pl.ds(r * reach + b * per + u, NSPEC), :] for b in range(shifts // per)
                    )
                    total = part if total is None else jnp.where(
                        lane < 2 * band * (u + 1), part, total
                    )
                whole = total
                for u in range(1, per):
                    whole = whole + turn_lanes(total, -2 * band * u)
                x[0, place, :] = whole

    @pl.when(i == 0)
    def _():
        begin(0)
        for copy in tables_in:
            copy.start()
        turned[...] = jnp.zeros(turned.shape, jnp.float32)
        if streams // step > 1:
            begin(1)

    @pl.when((i > 0) & (i + ahead - 1 < last))
    def _():
        begin(i + ahead - 1)

    @pl.when(i == 0)
    def _():
        for copy in tables_in:
            copy.wait()

    @pl.when(i < last)
    def _():
        for copy in fetch(i):
            copy.wait()

    @pl.when(i == 0)
    def _():
        for block in range(2, min(ahead, streams // step)):
            begin(block)

    @pl.when(i < last)
    def _():
        mix(jnp.maximum(i - 1, 0))
        analyse()

    @pl.when(i == last)
    def _():
        mix(i - 1)

    def finish(u):
        lane = lax.broadcasted_iota(jnp.int32, (8, wide * LANES), 1)
        row = lax.broadcasted_iota(jnp.int32, (8, wide * LANES), 0)
        slot = row // 2
        base = (row % 2) * band
        picks = []
        offset = jnp.int32(0)
        for d in range(dests):
            held_here = counts[d]
            want = offset + jnp.minimum(slot, held_here - 1) + base
            picks.append(jnp.where((lane == want) & (row < 2 * CAP), 1.0, 0.0))
            offset = offset + held_here
        pick = jnp.concatenate(picks, axis=0).astype(jnp.bfloat16)
        size = NSPEC * unit
        from_row = pl.multiple_of(u * size, 8)
        spectra = jnp.concatenate([x[n, pl.ds(from_row, size), :] for n in range(wide)], axis=1)
        out = lax.dot_general(
            pick, spectra.astype(jnp.bfloat16), (((1,), (1,)), ((), ())),
            preferred_element_type=jnp.float32,
        )
        tiles = size // LANES
        for d in range(dests):
            for t in range(tiles):
                turned[d, pl.ds(u * (2 * CAP * tiles) + t, 2 * CAP, stride=tiles), :] = out[
                    8 * d : 8 * d + 2 * CAP, t * LANES : (t + 1) * LANES
                ]

    @pl.when((i > 0) & (i % (unit // step) == 0))
    def _():
        finish(i // (unit // step) - 1)

    @pl.when(i == last)
    def _():
        whole = turned[...].astype(jnp.bfloat16)
        for n in range(out_ref.shape[1]):
            out_ref[:, n] = whole


def channelize(voltages, chan_counts, dests, start, streams, step, unit, room, copies):
    band = 2 * dests
    frames = voltages.shape[2]
    analysis, mixing = tables(band)
    packed = packing(band)[1]
    shifts = shifts_of(band)
    ahead = 4 if band <= 64 else 2
    payload = payload_rows(streams // unit, unit)
    steps = streams // step
    kernel = functools.partial(channelizer, band, dests, start, streams, step, unit)
    return pl.pallas_call(
        kernel,
        grid_spec=pltpu.PrefetchScalarGridSpec(
            num_scalar_prefetch=1,
            grid=(steps + 1,),
            in_specs=[pl.BlockSpec(memory_space=pl.ANY)] * 3,
            out_specs=pl.BlockSpec((dests, copies, payload, LANES), lambda i, c: (0, 0, 0, 0)),
            scratch_shapes=[
                pltpu.VMEM((ahead, step, frames, 2, FFT_LEN), jnp.bfloat16),
                pltpu.VMEM(analysis.shape, jnp.bfloat16),
                pltpu.VMEM(mixing.shape, jnp.bfloat16),
                pltpu.VMEM((packed // LANES, step * 2 * frames + 16, LANES), jnp.float32),
                pltpu.VMEM((shifts * 2 * band // LANES, step * (NSPEC + 8), LANES), jnp.float32),
                pltpu.VMEM((max(1, 2 * band // LANES), NSPEC * streams, LANES), jnp.float32),
                pltpu.VMEM((dests, payload, LANES), jnp.float32),
                pltpu.SemaphoreType.DMA((ahead + 1, step)),
            ],
        ),
        out_shape=jax.ShapeDtypeStruct((dests, copies, payload, LANES), jnp.bfloat16),
        compiler_params=pltpu.CompilerParams(
            vmem_limit_bytes=room * 1024 * 1024
        ),
        cost_estimate=pl.CostEstimate(
            flops=2 * streams * 2 * frames * analysis.size,
            bytes_accessed=2 * 2 * frames * FFT_LEN * streams, transcendentals=0,
        ),
    )(chan_counts, voltages, jnp.asarray(analysis), jnp.asarray(mixing)).reshape(-1, payload, LANES)


def payload_rows(units, unit):
    return -(-units * 2 * CAP * NSPEC * unit // (16 * LANES)) * 16


def regroup(ref, apart, pre, unit, every=1, first=0):
    spread = LANES // unit
    sources, payload = ref.shape[0] // every, ref.shape[1]
    units = payload * LANES // (2 * CAP * NSPEC * unit)
    lane = lax.broadcasted_iota(jnp.int32, (payload, LANES), 1) // unit
    for q in range(sources // spread):
        parts = [
            ref[every * (spread * q + a) + first].astype(jnp.float32) for a in range(spread)
        ]
        bit = 1
        while bit < spread:
            even = lane // bit % 2 == 0
            mixed = []
            for a in range(spread):
                twin = parts[a ^ bit]
                if a & bit:
                    mixed.append(jnp.where(even, turn_lanes(twin, -unit * bit), parts[a]))
                else:
                    mixed.append(jnp.where(even, parts[a], turn_lanes(twin, unit * bit)))
            parts = mixed
            bit = 2 * bit
        slot = q % 2
        for g in range(spread):
            apart[slot, pl.ds(g, payload, stride=spread), :] = parts[g]
        rows = 2 * CAP * NSPEC
        for u in range(units):
            place = (u * (sources // spread) + q) * LANES
            pre[:, place : place + LANES] = apart[slot, u * rows : (u + 1) * rows].astype(jnp.bfloat16)


def one_hot(dest, total):
    spot = lax.broadcasted_iota(jnp.int32, (total, dest.shape[1]), 0)
    return jnp.where(spot == dest, 1.0, 0.0).astype(jnp.bfloat16)


def permute(rows, turn):
    return lax.dot_general(
        rows, turn, (((1,), (1,)), ((), ())), preferred_element_type=jnp.float32
    )


def settler(unit, dest_ref, own_hbm, other_hbm, out_ref, own, other, apart, pre, arrived):
    copies = [
        pltpu.make_async_copy(own_hbm, own, arrived.at[0]),
        pltpu.make_async_copy(other_hbm, other, arrived.at[1]),
    ]
    for copy in copies:
        copy.start()
    turn = one_hot(dest_ref[...], out_ref.shape[2])
    for h, part in enumerate((own, other)):
        copies[h].wait()
        regroup(part, apart, pre, unit)
        out_ref[h] = permute(pre[...], turn).astype(jnp.bfloat16)


def settle(own, other, dest, total, unit):
    rows = 2 * CAP * NSPEC
    return pl.pallas_call(
        functools.partial(settler, unit),
        in_specs=[pl.BlockSpec(memory_space=pltpu.VMEM)] + [pl.BlockSpec(memory_space=pl.ANY)] * 2,
        out_specs=pl.BlockSpec(memory_space=pltpu.VMEM),
        out_shape=jax.ShapeDtypeStruct((2, rows, total), jnp.bfloat16),
        scratch_shapes=[
            pltpu.VMEM(own.shape, jnp.bfloat16),
            pltpu.VMEM(own.shape, jnp.bfloat16),
            pltpu.VMEM((2, own.shape[1] * LANES // unit, LANES), jnp.float32),
            pltpu.VMEM((rows, dest.shape[1]), jnp.bfloat16),
            pltpu.SemaphoreType.DMA((2,)),
        ],
        compiler_params=pltpu.CompilerParams(vmem_limit_bytes=32 * 1024 * 1024),
        cost_estimate=pl.CostEstimate(
            flops=4 * rows * dest.shape[1] * total, bytes_accessed=4 * own.size + 4 * rows * total,
            transcendentals=0,
        ),
    )(dest, own, other)


def correlator(unit, counts, where, dest_ref, *refs):
    given = (len(refs) - 6) // 2
    sources, out_ref, held = refs[:given], refs[given], refs[given + 1 : 2 * given + 1]
    apart, pre, post, near, arrived = refs[2 * given + 1 :]
    k = pl.program_id(0)
    part = pl.program_id(1)
    total = post.shape[2]
    rows = out_ref.shape[3]
    time_len = 2 * NSPEC

    @pl.when((k == 0) & (part == 0))
    def _():
        copies = [
            pltpu.make_async_copy(a, b, arrived.at[n]) for n, (a, b) in enumerate(zip(sources, held))
        ]
        for copy in copies:
            copy.start()
        turn = one_hot(dest_ref[...], total)
        for copy in copies:
            copy.wait()
        for h in range(2):
            regroup(held[0], apart, pre, unit, 2, where[1] if h == 0 else 1 - where[1])
            half = permute(pre[...], turn)
            for ref in held[1:]:
                half = half + ref[h].astype(jnp.float32)
            for n in range(2 * CAP):
                first = n % 2 * time_len + h * NSPEC
                post[n // 2, first : first + NSPEC] = half[n * NSPEC : (n + 1) * NSPEC].astype(
                    jnp.bfloat16
                )

    @pl.when(part == 0)
    def _():
        mine = post[k, :, pl.ds(pl.multiple_of(where[1] * rows, LANES), rows)]
        near[...] = mine.T

    valid = jnp.where(k < counts[where[0]], 1.0, 0.0) / jnp.float32(time_len)

    def put(right):
        vis = jnp.dot(near[...], right, preferred_element_type=jnp.float32)
        out_ref[0, 0, 0] = (vis * valid).astype(jnp.bfloat16)

    @pl.when(part == 0)
    def _():
        put(post[k])

    @pl.when(part == 1)
    def _():
        put(jnp.concatenate([-post[k, time_len:], post[k, :time_len]], axis=0))


def correlate(operands, dest, chan_counts, where, total, unit):
    held = dest.shape[1]
    most = operands[0].shape[1]
    rows = total // 2
    return pl.pallas_call(
        functools.partial(correlator, unit),
        grid_spec=pltpu.PrefetchScalarGridSpec(
            num_scalar_prefetch=2,
            grid=(CAP, 2),
            in_specs=[pl.BlockSpec((1, held), lambda k, p, c, w: (0, 0))]
            + [pl.BlockSpec(memory_space=pl.ANY)] * len(operands),
            out_specs=pl.BlockSpec((1, 1, 1, rows, total), lambda k, p, c, w: (0, k, p, 0, 0)),
            scratch_shapes=[pltpu.VMEM(a.shape, jnp.bfloat16) for a in operands]
            + [
                pltpu.VMEM((2, most * LANES // unit, LANES), jnp.float32),
                pltpu.VMEM((2 * CAP * NSPEC, held), jnp.bfloat16),
                pltpu.VMEM((CAP, 4 * NSPEC, total), jnp.bfloat16),
                pltpu.VMEM((rows, 4 * NSPEC), jnp.bfloat16),
                pltpu.SemaphoreType.DMA((len(operands),)),
            ],
        ),
        out_shape=jax.ShapeDtypeStruct((1, CAP, 2, rows, total), jnp.bfloat16),
        compiler_params=pltpu.CompilerParams(vmem_limit_bytes=32 * 1024 * 1024),
    )(chan_counts, where, dest, *operands)


def body(voltages, station_map, chan_counts):
    dests = lax.axis_size("stn")
    streams = voltages.shape[0]
    total = dests * streams
    unit = min(streams, 16)
    dest = (2 * station_map[:, None] + jnp.arange(2, dtype=jnp.int32)[None, :]).reshape(-1)
    dest = dest.reshape(dests, streams // unit, unit).transpose(1, 0, 2)
    where = jnp.stack([lax.axis_index("stn"), lax.axis_index("blk")]).astype(jnp.int32)

    def turn(outgoing, axes):
        return lax.all_to_all(outgoing, axes, split_axis=0, concat_axis=0, tiled=True)

    def spots(start, size):
        return dest[start // unit : (start + size) // unit].reshape(1, -1)

    settled = []
    early = 48 if streams == 64 else 0
    late = streams - early
    if early:
        outgoing = channelize(voltages, chan_counts, dests, 0, early, 4, unit, 60, 1)
        chan_counts, outgoing = lax.optimization_barrier((chan_counts, outgoing))
        first = turn(outgoing, "stn")
        outgoing = channelize(voltages, chan_counts, dests, early, late, 2, unit, 32, 2)
        first, outgoing = lax.optimization_barrier((first, outgoing))
        first_other = lax.ppermute(first, "blk", [(0, 1), (1, 0)])
        settled.append(settle(first, first_other, spots(0, early), total, unit))
    else:
        outgoing = channelize(voltages, chan_counts, dests, 0, late, 2, unit, 60, 2)
    both = turn(outgoing, ("stn", "blk"))
    spot = spots(early, late)
    return correlate([both] + settled, spot, chan_counts, where, total, unit)


def solution(mesh):
    return jax.shard_map(
        body,
        mesh=mesh,
        in_specs=(P("stn", "blk", None, None, None), P(), P()),
        out_specs=P("stn", None, None, "blk", None),
        check_vma=False,
    )
```

```python
import functools
import math

import jax
import jax.numpy as jnp
import ml_dtypes
import numpy as np
from jax import lax
from jax.experimental import pallas as pl
from jax.experimental.pallas import tpu as pltpu
from jax.sharding import PartitionSpec as P

FFT_LEN = 4096
TAPS = 16
CAP = 3
NSPEC = 48
LANES = 128


def prototype():
    span = TAPS * FFT_LEN
    points = np.arange(span, dtype=np.float64) + 0.5
    window = 0.5 - 0.5 * np.cos(2.0 * math.pi * points / span)
    shifted = math.pi * (points - span / 2.0) / FFT_LEN
    filt = np.sin(shifted) / shifted * window
    return (filt / np.sqrt(np.sum(filt * filt))).reshape(TAPS, FFT_LEN)


def frame_basis(band, count):
    limit = math.pi * (band + 0.1)
    terms = count + int(limit) + 60
    k = np.arange(terms, dtype=np.float64)
    diagonal = k * (k + 1) + (2 * k * (k + 1) - 1) / ((2 * k + 3) * (2 * k - 1)) * limit**2
    m = k[:-2]
    beside = (m + 2) * (m + 1) / ((2 * m + 3) * np.sqrt((2 * m + 1) * (2 * m + 5))) * limit**2
    matrix = np.diag(diagonal) + np.diag(beside, 2) + np.diag(beside, -2)
    _, vectors = np.linalg.eigh(matrix)
    x = (2 * np.arange(FFT_LEN) + 1.0) / FFT_LEN - 1
    legendre = np.zeros((terms, FFT_LEN))
    legendre[0] = 1.0
    legendre[1] = x
    for j in range(2, terms):
        legendre[j] = ((2 * j - 1) * x * legendre[j - 1] - (j - 1) * legendre[j - 2]) / j
    legendre *= np.sqrt((k + 0.5) * 2.0 / FFT_LEN)[:, None]
    return legendre.T @ vectors[:, :count]


def shifts_of(band):
    return 8 if band <= 64 else 4


def turn_lanes(value, shift):
    shift = shift % LANES
    return pltpu.roll(value, shift, axis=1) if shift else value


def packing(band):
    if 3 * (2 * band + 16) <= 2 * LANES:
        return 2 * band + 16, 2 * LANES, True
    count = -(-(2 * band + 32) // (LANES // 2)) * (LANES // 2)
    return count, -(-2 * count // LANES) * LANES, False


@functools.lru_cache(maxsize=4)
def tables(band):
    bf16 = ml_dtypes.bfloat16
    count, packed, triple = packing(band)
    shifts = shifts_of(band)
    basis = frame_basis(band, count)
    high = basis.astype(bf16)
    low = (basis - high.astype(np.float64)).astype(bf16)
    held = high.astype(np.float64) + low.astype(np.float64)
    lanes = -(-count // LANES) * LANES
    analysis = np.zeros((FFT_LEN, 2 * lanes), bf16)
    analysis[:, :count] = high
    analysis[:, lanes : lanes + count] = low

    phase = 2.0 * math.pi / FFT_LEN * (np.outer(np.arange(FFT_LEN), np.arange(band)) % FFT_LEN)
    wave = np.concatenate([np.cos(phase), -np.sin(phase)], axis=1)
    gram = held.T @ held
    taper = prototype()
    mixing = np.zeros((TAPS // shifts, 2, packed, shifts, 2 * band), bf16)
    for t in range(TAPS):
        real = np.linalg.solve(gram, held.T @ (taper[t][:, None] * wave))
        imag = np.concatenate([-real[:, band:], real[:, :band]], axis=1)
        for c, full in enumerate((real, imag)):
            part = mixing[t // shifts, c, :, t % shifts]
            top = full.astype(bf16)
            part[:count] = top
            part[count : 2 * count] = top
            if triple:
                part[2 * count : 3 * count] = (full - top.astype(np.float64)).astype(bf16)
    return analysis, mixing.reshape(-1, shifts * 2 * band)


def channelizer(
    band, dests, first, streams, step, unit, counts, v_ref, u_hbm, w_hbm, out_ref,
    held, u_ref, w_ref, y, p, x, turned, arrived,
):
    i = pl.program_id(0)
    ahead = held.shape[0]
    shifts = shifts_of(band)
    last = pl.num_programs(0) - 1
    count, packed, triple = packing(band)
    lanes = u_ref.shape[1] // 2
    rows = 2 * v_ref.shape[2]
    reach = NSPEC + 8
    wide = max(1, 2 * band // LANES)
    tables_in = [
        pltpu.make_async_copy(u_hbm, u_ref, arrived.at[ahead, 0]),
        pltpu.make_async_copy(w_hbm, w_ref, arrived.at[ahead, 1]),
    ]

    def fetch(block):
        slot = block % ahead
        return [
            pltpu.make_async_copy(
                v_ref.at[first + block * step + r, 0], held.at[slot, r], arrived.at[slot, r]
            )
            for r in range(step)
        ]

    def begin(block):
        for r, copy in enumerate(fetch(block)):
            copy.start(priority=r % 2)

    def analyse():
        signal = held[i % ahead].reshape(step * rows, FFT_LEN)
        coeff = jnp.dot(signal, u_ref[...], preferred_element_type=jnp.float32)
        coeff = coeff[:, :lanes] + coeff[:, lanes:]
        high = coeff.astype(jnp.bfloat16).astype(jnp.float32)
        low = coeff - high
        if triple:
            lane = lax.broadcasted_iota(jnp.int32, coeff.shape, 1)
            low = turn_lanes(low, count)
            spare = 2 * count - LANES
            y[0, : step * rows] = jnp.where(lane < count, high, low)
            y[1, : step * rows] = jnp.where(lane < spare, low, turn_lanes(high, spare))
        else:
            both = jnp.concatenate([high[:, :count], low[:, :count]], axis=1)
            for n in range(packed // LANES):
                y[n, : step * rows] = both[:, n * LANES : (n + 1) * LANES]

    def mix(block):
        taps = []
        for r in range(step):
            taps.append(jnp.concatenate([
                y[n, pl.ds(r * rows + 2 * shifts * m + c, reach, stride=2), :]
                for m in range(TAPS // shifts) for c in range(2) for n in range(packed // LANES)
            ], axis=1))
        taps = jnp.concatenate(taps, axis=0).astype(jnp.bfloat16)
        mixed = jnp.dot(taps, w_ref[...], preferred_element_type=jnp.float32)
        for n in range(mixed.shape[1] // LANES):
            p[n] = mixed[:, n * LANES : (n + 1) * LANES]
        for r in range(step):
            stream = block * step + r
            place = pl.ds(stream // unit * (NSPEC * unit) + stream % unit, NSPEC, stride=unit)
            if 2 * band >= LANES:
                for n in range(wide):
                    x[n, place, :] = sum(
                        p[wide * h + n, pl.ds(r * reach + h, NSPEC), :] for h in range(shifts)
                    )
            else:
                per = LANES // (2 * band)
                lane = lax.broadcasted_iota(jnp.int32, (NSPEC, LANES), 1)
                total = None
                for u in reversed(range(per)):
                    part = sum(
                        p[b, pl.ds(r * reach + b * per + u, NSPEC), :] for b in range(shifts // per)
                    )
                    total = part if total is None else jnp.where(
                        lane < 2 * band * (u + 1), part, total
                    )
                whole = total
                for u in range(1, per):
                    whole = whole + turn_lanes(total, -2 * band * u)
                x[0, place, :] = whole

    @pl.when(i == 0)
    def _():
        begin(0)
        for copy in tables_in:
            copy.start()
        turned[...] = jnp.zeros(turned.shape, jnp.float32)

    @pl.when((i > 0) & (i + ahead - 1 < last))
    def _():
        begin(i + ahead - 1)

    @pl.when(i == 0)
    def _():
        for copy in tables_in:
            copy.wait()
        if streams // step > 1:
            begin(1)

    @pl.when(i < last)
    def _():
        for copy in fetch(i):
            copy.wait()

    @pl.when(i == 0)
    def _():
        for block in range(2, min(ahead, streams // step)):
            begin(block)

    @pl.when(i < last)
    def _():
        mix(jnp.maximum(i - 1, 0))
        analyse()

    @pl.when(i == last)
    def _():
        mix(i - 1)
        lane = lax.broadcasted_iota(jnp.int32, (8, wide * LANES), 1)
        row = lax.broadcasted_iota(jnp.int32, (8, wide * LANES), 0)
        slot = row // 2
        base = (row % 2) * band
        picks = []
        offset = jnp.int32(0)
        for d in range(dests):
            held = counts[d]
            want = offset + jnp.minimum(slot, held - 1) + base
            picks.append(jnp.where((lane == want) & (row < 2 * CAP), 1.0, 0.0))
            offset = offset + held
        pick = jnp.concatenate(picks, axis=0).astype(jnp.bfloat16)
        spectra = jnp.concatenate([x[n] for n in range(wide)], axis=1)
        out = lax.dot_general(
            pick, spectra.astype(jnp.bfloat16), (((1,), (1,)), ((), ())),
            preferred_element_type=jnp.float32,
        )
        tiles = NSPEC * unit // LANES
        for d in range(dests):
            for t in range(streams // unit * tiles):
                row = t // tiles * (2 * CAP * tiles) + t % tiles
                turned[d, pl.ds(row, 2 * CAP, stride=tiles), :] = out[
                    8 * d : 8 * d + 2 * CAP, t * LANES : (t + 1) * LANES
                ]
        out_ref[...] = turned[...].astype(jnp.bfloat16)


def channelize(voltages, chan_counts, dests, start, streams, step, unit, room):
    band = 2 * dests
    frames = voltages.shape[2]
    analysis, mixing = tables(band)
    packed = packing(band)[1]
    shifts = shifts_of(band)
    ahead = 4 if band <= 64 else 2
    payload = payload_rows(streams // unit, unit)
    steps = streams // step
    kernel = functools.partial(channelizer, band, dests, start, streams, step, unit)
    return pl.pallas_call(
        kernel,
        grid_spec=pltpu.PrefetchScalarGridSpec(
            num_scalar_prefetch=1,
            grid=(steps + 1,),
            in_specs=[pl.BlockSpec(memory_space=pl.ANY)] * 3,
            out_specs=pl.BlockSpec((dests, payload, LANES), lambda i, c: (0, 0, 0)),
            scratch_shapes=[
                pltpu.VMEM((ahead, step, frames, 2, FFT_LEN), jnp.bfloat16),
                pltpu.VMEM(analysis.shape, jnp.bfloat16),
                pltpu.VMEM(mixing.shape, jnp.bfloat16),
                pltpu.VMEM((packed // LANES, step * 2 * frames + 16, LANES), jnp.float32),
                pltpu.VMEM((shifts * 2 * band // LANES, step * (NSPEC + 8), LANES), jnp.float32),
                pltpu.VMEM((max(1, 2 * band // LANES), NSPEC * streams, LANES), jnp.float32),
                pltpu.VMEM((dests, payload, LANES), jnp.float32),
                pltpu.SemaphoreType.DMA((ahead + 1, step)),
            ],
        ),
        out_shape=jax.ShapeDtypeStruct((dests, payload, LANES), jnp.bfloat16),
        compiler_params=pltpu.CompilerParams(
            vmem_limit_bytes=room * 1024 * 1024
        ),
        cost_estimate=pl.CostEstimate(
            flops=2 * streams * 2 * frames * analysis.size,
            bytes_accessed=2 * 2 * frames * FFT_LEN * streams, transcendentals=0,
        ),
    )(chan_counts, voltages, jnp.asarray(analysis), jnp.asarray(mixing))


def payload_rows(units, unit):
    return -(-units * 2 * CAP * NSPEC * unit // (16 * LANES)) * 16


def streams_in(part, unit):
    return part.shape[0] * unit * (part.shape[1] * LANES // (2 * CAP * NSPEC * unit))


def regroup(ref, apart, pre, unit, base):
    spread = LANES // unit
    sources, payload = ref.shape[:2]
    units = streams_in(ref, unit) // (sources * unit)
    lane = lax.broadcasted_iota(jnp.int32, (payload, LANES), 1) // unit
    for q in range(sources // spread):
        parts = [ref[spread * q + a].astype(jnp.float32) for a in range(spread)]
        bit = 1
        while bit < spread:
            even = lane // bit % 2 == 0
            mixed = []
            for a in range(spread):
                twin = parts[a ^ bit]
                if a & bit:
                    mixed.append(jnp.where(even, turn_lanes(twin, -unit * bit), parts[a]))
                else:
                    mixed.append(jnp.where(even, parts[a], turn_lanes(twin, unit * bit)))
            parts = mixed
            bit = 2 * bit
        slot = q % 2
        for g in range(spread):
            apart[slot, pl.ds(g, payload, stride=spread), :] = parts[g]
        rows = 2 * CAP * NSPEC
        for u in range(units):
            place = base + (u * (sources // spread) + q) * LANES
            pre[:, place : place + LANES] = apart[slot, u * rows : (u + 1) * rows].astype(jnp.bfloat16)


def one_hot(dest, total):
    spot = lax.broadcasted_iota(jnp.int32, (total, dest.shape[1]), 0)
    return jnp.where(spot == dest, 1.0, 0.0).astype(jnp.bfloat16)


def permute(rows, turn):
    return lax.dot_general(
        rows, turn, (((1,), (1,)), ((), ())), preferred_element_type=jnp.float32
    )


def settler(unit, dest_ref, own_hbm, other_hbm, out_ref, own, other, apart, pre, arrived):
    copies = [
        pltpu.make_async_copy(own_hbm, own, arrived.at[0]),
        pltpu.make_async_copy(other_hbm, other, arrived.at[1]),
    ]
    for copy in copies:
        copy.start()
    turn = one_hot(dest_ref[...], out_ref.shape[2])
    for h, part in enumerate((own, other)):
        copies[h].wait()
        regroup(part, apart, pre, unit, 0)
        out_ref[h] = permute(pre[...], turn).astype(jnp.bfloat16)


def settle(own, other, dest, total, unit):
    rows = 2 * CAP * NSPEC
    return pl.pallas_call(
        functools.partial(settler, unit),
        in_specs=[pl.BlockSpec(memory_space=pltpu.VMEM)] + [pl.BlockSpec(memory_space=pl.ANY)] * 2,
        out_specs=pl.BlockSpec(memory_space=pltpu.VMEM),
        out_shape=jax.ShapeDtypeStruct((2, rows, total), jnp.bfloat16),
        scratch_shapes=[
            pltpu.VMEM(own.shape, jnp.bfloat16),
            pltpu.VMEM(own.shape, jnp.bfloat16),
            pltpu.VMEM((2, own.shape[1] * LANES // unit, LANES), jnp.float32),
            pltpu.VMEM((rows, dest.shape[1]), jnp.bfloat16),
            pltpu.SemaphoreType.DMA((2,)),
        ],
        compiler_params=pltpu.CompilerParams(vmem_limit_bytes=32 * 1024 * 1024),
        cost_estimate=pl.CostEstimate(
            flops=4 * rows * dest.shape[1] * total, bytes_accessed=4 * own.size + 4 * rows * total,
            transcendentals=0,
        ),
    )(dest, own, other)


def correlator(unit, counts, where, dest_ref, *refs):
    given = (len(refs) - 6) // 2
    sources, out_ref, held = refs[:given], refs[given], refs[given + 1 : 2 * given + 1]
    apart, pre, post, near, arrived = refs[2 * given + 1 :]
    k = pl.program_id(0)
    part = pl.program_id(1)
    total = post.shape[2]
    rows = out_ref.shape[3]
    time_len = 2 * NSPEC

    @pl.when((k == 0) & (part == 0))
    def _():
        copies = [
            pltpu.make_async_copy(a, b, arrived.at[n]) for n, (a, b) in enumerate(zip(sources, held))
        ]
        for copy in copies:
            copy.start()
        turn = one_hot(dest_ref[...], total)
        for copy in copies:
            copy.wait()
        for h in range(2):
            regroup(held[h], apart, pre, unit, 0)
            half = permute(pre[...], turn)
            for ref in held[2:]:
                half = half + ref[h].astype(jnp.float32)
            for n in range(2 * CAP):
                first = n % 2 * time_len + h * NSPEC
                post[n // 2, first : first + NSPEC] = half[n * NSPEC : (n + 1) * NSPEC].astype(
                    jnp.bfloat16
                )

    @pl.when(part == 0)
    def _():
        mine = post[k, :, pl.ds(pl.multiple_of(where[1] * rows, LANES), rows)]
        near[...] = mine.T

    valid = jnp.where(k < counts[where[0]], 1.0, 0.0) / jnp.float32(time_len)

    def put(right):
        vis = jnp.dot(near[...], right, preferred_element_type=jnp.float32)
        out_ref[0, 0, 0] = (vis * valid).astype(jnp.bfloat16)

    @pl.when(part == 0)
    def _():
        put(post[k])

    @pl.when(part == 1)
    def _():
        put(jnp.concatenate([-post[k, time_len:], post[k, :time_len]], axis=0))


def correlate(operands, dest, chan_counts, where, total, unit):
    held = dest.shape[1]
    most = operands[0].shape[1]
    rows = total // 2
    return pl.pallas_call(
        functools.partial(correlator, unit),
        grid_spec=pltpu.PrefetchScalarGridSpec(
            num_scalar_prefetch=2,
            grid=(CAP, 2),
            in_specs=[pl.BlockSpec((1, held), lambda k, p, c, w: (0, 0))]
            + [pl.BlockSpec(memory_space=pl.ANY)] * len(operands),
            out_specs=pl.BlockSpec((1, 1, 1, rows, total), lambda k, p, c, w: (0, k, p, 0, 0)),
            scratch_shapes=[pltpu.VMEM(a.shape, jnp.bfloat16) for a in operands]
            + [
                pltpu.VMEM((2, most * LANES // unit, LANES), jnp.float32),
                pltpu.VMEM((2 * CAP * NSPEC, held), jnp.bfloat16),
                pltpu.VMEM((CAP, 4 * NSPEC, total), jnp.bfloat16),
                pltpu.VMEM((rows, 4 * NSPEC), jnp.bfloat16),
                pltpu.SemaphoreType.DMA((len(operands),)),
            ],
        ),
        out_shape=jax.ShapeDtypeStruct((1, CAP, 2, rows, total), jnp.bfloat16),
        compiler_params=pltpu.CompilerParams(vmem_limit_bytes=32 * 1024 * 1024),
    )(chan_counts, where, dest, *operands)


def body(voltages, station_map, chan_counts):
    dests = lax.axis_size("stn")
    streams = voltages.shape[0]
    total = dests * streams
    unit = min(streams, 16)
    dest = (2 * station_map[:, None] + jnp.arange(2, dtype=jnp.int32)[None, :]).reshape(-1)
    dest = dest.reshape(dests, streams // unit, unit).transpose(1, 0, 2)
    where = jnp.stack([lax.axis_index("stn"), lax.axis_index("blk")]).astype(jnp.int32)

    def turn(outgoing):
        return lax.all_to_all(outgoing, "stn", split_axis=0, concat_axis=0, tiled=True)

    def swap(own):
        return lax.ppermute(own, "blk", [(0, 1), (1, 0)])

    def spots(start, size):
        return dest[start // unit : (start + size) // unit].reshape(1, -1)

    if streams == 64:
        early, late = 48, 16
        outgoing = channelize(voltages, chan_counts, dests, 0, early, 4, unit, 60)
        chan_counts, outgoing = lax.optimization_barrier((chan_counts, outgoing))
        first = turn(outgoing)
        outgoing = channelize(voltages, chan_counts, dests, early, late, 2, unit, 32)
        first, outgoing = lax.optimization_barrier((first, outgoing))
        first_other = swap(first)
        own = turn(outgoing)
        own, first_other = lax.optimization_barrier((own, first_other))
        other = swap(own)
        settled = [settle(first, first_other, spots(0, early), total, unit)]
    else:
        late = streams
        own = turn(channelize(voltages, chan_counts, dests, 0, late, 2, unit, 60))
        other = swap(own)
        settled = []
    spot = spots(streams - late, late)
    return correlate([own, other] + settled, spot, chan_counts, where, total, unit)


def solution(mesh):
    return jax.shard_map(
        body,
        mesh=mesh,
        in_specs=(P("stn", "blk", None, None, None), P(), P()),
        out_specs=P("stn", None, None, "blk", None),
        check_vma=False,
    )
```
